32 devices in a mesh: groups: 2 (over y), member: 4 (over x, core), shard: 4 (over z).
Axes of the slice: x: 2, y: 2, z: 4, core: 2. Of those that a mesh axis runs over, the one named last changes fastest.
Arguments:
- context: bfloat16 [8, 2048, 1024], P(('groups', 'member'), 'shard'), parts along dimension 0, may hold values from -6 to 6
- out_grad: bfloat16 [8, 2048, 1024], P(('groups', 'member'), 'shard'), parts along dimension 0, may hold values from -4 to 4
- weight: float32 [8, 1024, 1024], P(('groups', 'member'), 'shard'), parts along dimension 0, may hold values from -5 to 5
- first: float32 [8, 1024, 1024], P(('groups', 'member'), 'shard'), parts along dimension 0, may hold values from -3 to 3
- second: float32 [8, 1024, 1024], P(('groups', 'member'), 'shard'), parts along dimension 0, may hold values from 0.05 to 2
- rates: float32 [8], P('groups'), parts along dimension 0, may hold values from 0.01 to 0.1
- decays: float32 [8], P('groups'), parts along dimension 0, may hold values from 0.1 to 1
- steps: int32 [8], P('groups'), parts along dimension 0, may hold values from 10 to 3000
- donor: int32 [8], P('groups'), parts along dimension 0, may hold values from -1 to 3, as said below
Outputs:
- context_grad: bfloat16 [8, 2048, 1024], P(('groups', 'member'), 'shard'), parts along dimension 0
- new_weight: float32 [8, 1024, 1024], P(('groups', 'member'), 'shard'), parts along dimension 0
- new_first: float32 [8, 1024, 1024], P(('groups', 'member'), 'shard'), parts along dimension 0
- new_second: float32 [8, 1024, 1024], P(('groups', 'member'), 'shard'), parts along dimension 0
The draws below stay inside these ranges and needn't reach their ends.
There are 2 independent parts, one for each index of `groups`. The reference program is written for one: setup_inputs(seed, part) draws one part's arguments, and reference() takes and returns one part's arrays. A program takes and returns all parts, laid end to end along the dimension named above; each array names one. Nothing has to cross between parts.
Inputs may be any that keep to these rules, and one draw needn't show every extreme that they name: Exactly 2 entries are not -1; each of those names a member whose own entry is -1. Member 4 - 1 is always some loser's donor.
All inputs are finite; a program needn't handle non-finite values.
Results may differ from the reference program's by a relative error of at most 0.0049.
Values may be sent and summed in bfloat16 or wider, within the bound.
No kernel may reach another device: no remote copies, remote signals or barrier semaphores. Data moves between devices by JAX's collectives and lax.ppermute only.
A program may use at most 64 MiB of HBM per device.

```python
import math
import jax
import jax.numpy as jnp
from jax import lax

D = 1024
K = 1024
TOK_DEV = 512
TOKENS = 2048
MEMBERS = 4
LOSERS = 2
N_SHARD = 4


def draw_donor(key, part):
    key = jax.random.fold_in(key, 7)
    rest = jax.random.permutation(key, MEMBERS - 1).astype(jnp.int32)
    ranking = jnp.concatenate([jnp.full((1,), MEMBERS - 1, jnp.int32), rest]).astype(jnp.int32)
    positions = jnp.arange(MEMBERS, dtype=jnp.int32)
    picks = jax.random.randint(jax.random.fold_in(key, 1), (MEMBERS,), 0, MEMBERS - LOSERS).astype(jnp.int32)
    picks = jnp.where(positions == MEMBERS - LOSERS, 0, picks).astype(jnp.int32)
    chosen = ranking[picks]
    by_rank = jnp.where(positions >= MEMBERS - LOSERS, chosen, -1).astype(jnp.int32)
    return jnp.zeros((MEMBERS,), jnp.int32).at[ranking].set(by_rank)


def with_ends(drawn, key, low, high):
    longest = drawn.shape.index(max(drawn.shape))
    spots = []
    for shift in (0, 1):
        where = [jax.random.randint(jax.random.fold_in(key, axis), (), 0, length) for axis, length in enumerate(drawn.shape)]
        where[longest] = (where[longest] + shift) % drawn.shape[longest]
        spots.append(tuple(where))
    return drawn.at[spots[0]].set(low).at[spots[1]].set(high)


def raised(drawn, key, source, target, shards_of, factor):
    def block_of(position):
        return (jnp.arange(drawn.shape[position]) // (drawn.shape[position] // shards_of)).reshape((-1,) + (1,) * (drawn.ndim - 1 - position))

    near = jax.random.permutation(key, shards_of)[block_of(target)]
    far = (block_of(target) + shards_of // 2) % shards_of
    return jnp.where((block_of(source) == near) | (block_of(source) == far), factor * drawn, drawn)


def block_levels(stream_key, dims, split, low, largest):
    def one(dim, blocks):
        steps = jax.random.uniform(jax.random.fold_in(jax.random.fold_in(stream_key, 6), dim), (blocks,), jnp.float32, low / len(split), largest / len(split))
        return jnp.repeat(jnp.exp(steps), dims[dim] // blocks).reshape((-1,) + (1,) * (len(dims) - dim - 1))

    factor_of = one(*split[0])
    for cut in split[1:]:
        factor_of = factor_of * one(*cut)
    return factor_of


def centred(key, dims, width, reach, split=(), kind=jnp.bfloat16):
    entries = width * jax.random.normal(key, dims, jnp.float32)
    if split:
        entries = entries * block_levels(key, dims, split, -0.22, 0.18)
    return jnp.clip(entries, -reach, reach).astype(kind)


def bell_draw_with(stream_key, shape, width, bound, shards, heavy, kind=jnp.bfloat16):
    values = width * jax.random.normal(stream_key, shape, jnp.float32)
    if shards:
        values = values * block_levels(stream_key, shape, shards, -0.22, 0.18)
    return jnp.clip(raised(values, jax.random.fold_in(stream_key, 3), *heavy), -bound, bound).astype(kind)


def setup_inputs(seed: int = 0, part: int = 0) -> dict:
    key_of = jax.random.split(jax.random.key(seed), 10)
    part_splits = jax.random.split(jax.random.fold_in(key_of[9], part), 10)
    return {
        "context": bell_draw_with(part_splits[0], (MEMBERS, TOKENS, K), 1.0, 6.0, ((0, 4), (1, 4)), (1, 2, 4, 2.0)),
        "out_grad": centred(part_splits[1], (MEMBERS, TOKENS, D), (max(1, TOK_DEV * N_SHARD // K)) ** -0.5, 4.0, ((0, 4), (1, 4))),
        "weight": centred(part_splits[2], (MEMBERS, K, D), 1.0, 5.0, ((0, 4), (1, 4)), jnp.float32),
        "first": centred(part_splits[3], (MEMBERS, K, D), 0.5, 3.0, ((0, 4), (1, 4)), jnp.float32),
        "second": jnp.clip(jnp.exp(math.log(2.0) - 3.6888794 * jax.random.uniform(part_splits[4], (MEMBERS, K, D), jnp.float32) ** block_levels(part_splits[4], (MEMBERS, K, D), ((0, 4), (1, 4)), -0.2, 0.2)), 0.05, 2.0),
        "rates": jnp.clip(jnp.exp(jax.random.uniform(part_splits[5], (MEMBERS,), jnp.float32, math.log(0.01), math.log(0.1))), 0.01, 0.1),
        "decays": jnp.clip(jnp.exp(jax.random.uniform(part_splits[6], (MEMBERS,), jnp.float32, math.log(0.1), math.log(1.0))), 0.1, 1.0),
        "steps": with_ends(jax.random.randint(part_splits[7], (MEMBERS,), 10, 3001), jax.random.fold_in(part_splits[7], 1), 10, 3000).astype(jnp.int32),
        "donor": draw_donor(jax.random.fold_in(jax.random.fold_in(key_of[9], part), 71), part),
    }


beta_one = 0.9
beta_two = 0.999
epsilon = 1e-08

def reference(context, out_grad, weight, first, second, rates, decays, steps, donor):
    scale = K ** (-0.5)
    half_weight = weight.astype(jnp.bfloat16)

    def backward_input(pair):
        cotangent, weight_rows = pair
        product = lax.dot_general(cotangent, weight_rows, (((1,), (1,)), ((), ())), preferred_element_type=jnp.float32)
        return (product * scale).astype(jnp.bfloat16)
    context_grad = lax.map(backward_input, (out_grad, half_weight))

    def member_grad(pair):
        context_rows, cotangent = pair
        blocks_in = context_rows.reshape(N_SHARD, TOK_DEV, K)
        blocks_out = cotangent.reshape(N_SHARD, TOK_DEV, D)

        def add_block(total, block):
            term = scale * lax.dot_general(block[0], block[1], (((0,), (0,)), ((), ())), preferred_element_type=jnp.float32)
            return (total + term, None)
        total, unused = lax.scan(add_block, jnp.zeros((K, D), jnp.float32), (blocks_in, blocks_out))
        return total
    grad = lax.map(member_grad, (context, out_grad))
    rate = rates[:, None, None]
    decay = decays[:, None, None]
    count = (steps + 1).astype(jnp.float32)[:, None, None]
    first_step = beta_one * first + (1.0 - beta_one) * grad
    second_step = beta_two * second + (1.0 - beta_two) * grad * grad
    first_hat = first_step / (1.0 - jnp.power(beta_one, count))
    second_hat = second_step / (1.0 - jnp.power(beta_two, count))
    weight_step = weight - rate * (first_hat / (jnp.sqrt(second_hat) + epsilon) + decay * weight)
    source = jnp.where(donor >= 0, donor, jnp.arange(MEMBERS, dtype=jnp.int32)).astype(jnp.int32)
    return (context_grad, weight_step[source], first_step[source], second_step[source])
```

```python
import jax
import jax.numpy as jnp
from jax import lax
from jax.sharding import PartitionSpec as P

beta_one = 0.9
beta_two = 0.999
epsilon = 1e-08


def lookup(table, index):
    positions = jnp.arange(table.shape[0], dtype=jnp.int32)
    return jnp.sum(jnp.where(positions == index, table, jnp.zeros_like(table)))


def adam_update(weight_rows, first_rows, second_rows, grad_rows, rates, decays, steps, index):
    rate = lookup(rates, index)
    decay = lookup(decays, index)
    count = (lookup(steps, index) + 1).astype(jnp.float32)
    first_step = beta_one * first_rows + (1.0 - beta_one) * grad_rows
    second_step = beta_two * second_rows + (1.0 - beta_two) * grad_rows * grad_rows
    first_hat = first_step / (1.0 - jnp.power(beta_one, count))
    second_hat = second_step / (1.0 - jnp.power(beta_two, count))
    weight_step = weight_rows - rate * (
        first_hat / (jnp.sqrt(second_hat) + epsilon) + decay * weight_rows
    )
    return (weight_step, first_step, second_step)


def on_device(n, members, context, out_grad, weight, first, second, rates, decays, steps, donor):
    context_rows = context[0]
    cotangent = out_grad[0]
    width = context_rows.shape[1]
    rows = weight.shape[1]
    scale = width ** (-0.5)
    half = jnp.bfloat16
    me = lax.axis_index("shard")
    member = lax.axis_index("member")
    donor_of = lookup(donor, member)
    source = jnp.where(donor_of >= 0, donor_of, member)
    mate = jnp.bitwise_xor(member, 1)
    across = jnp.bitwise_xor(member, 2)
    mate_donor = lookup(donor, mate)
    mate_source = jnp.where(mate_donor >= 0, mate_donor, mate)

    swap_across = [(m, m ^ 2) for m in range(members)]
    swap_mates = [(m, m ^ 1) for m in range(members)]
    to_right = [(s, s + 1) for s in range(n - 1)]
    to_left = [(s + 1, s) for s in range(n - 1)]

    def from_donor(own):
        far = lax.ppermute(own, "member", swap_across)
        near = lax.ppermute(jnp.where(mate_source == across, far, own), "member", swap_mates)
        return jnp.where(source == across, far, near)

    half_weight = weight[0].astype(half)
    state = jnp.concatenate([half_weight, first[0].astype(half), second[0].astype(half)], axis=0)

    partial = scale * lax.dot_general(
        context_rows, cotangent, (((0,), (0,)), ((), ())), preferred_element_type=jnp.float32
    )

    def partial_block(block):
        start = jnp.clip(block, 0, n - 1) * rows
        return lax.dynamic_slice_in_dim(partial, start, rows, 0)

    from_left, from_right = [half_weight], [half_weight]
    for slot in range(1, n + 1):
        right, left = from_left[-1], from_right[-1]
        if slot > 1:
            add_right = jnp.where(me >= slot - 1, 0.0, partial_block(n + 1 + me - slot))
            add_left = jnp.where(n - 1 - me >= slot - 1, 0.0, partial_block(me + slot - n - 1))
            right = (right.astype(jnp.float32) + add_right).astype(half)
            left = (left.astype(jnp.float32) + add_left).astype(half)
        from_left.append(lax.ppermute(right, "shard", to_right))
        from_right.append(lax.ppermute(left, "shard", to_left))

    donor_state = from_donor(state)

    window = jnp.concatenate(from_left[n - 1:0:-1] + [half_weight] + from_right[1:n], axis=0)
    full_weight = lax.dynamic_slice_in_dim(window, (n - 1 - me) * rows, n * rows, 0)
    columns = lax.dot_general(
        cotangent, full_weight, (((1,), (1,)), ((), ())), preferred_element_type=jnp.float32
    )
    context_grad = (columns * scale).astype(half)[None]

    grad = partial_block(me) + from_left[n].astype(jnp.float32) + from_right[n].astype(jnp.float32)
    donor_grad = from_donor(grad.astype(half))

    keeps = source == member
    donor_state = donor_state.astype(jnp.float32)
    updated = adam_update(
        jnp.where(keeps, weight[0], donor_state[:rows]),
        jnp.where(keeps, first[0], donor_state[rows:2 * rows]),
        jnp.where(keeps, second[0], donor_state[2 * rows:]),
        jnp.where(keeps, grad, donor_grad.astype(jnp.float32)),
        rates, decays, steps, source,
    )
    return (context_grad,) + tuple(array[None] for array in updated)


def solution(mesh):
    whole = P(("groups", "member"), "shard", None)
    n, members = mesh.shape["shard"], mesh.shape["member"]

    def run(*args):
        return on_device(n, members, *args)

    return jax.shard_map(
        run, mesh=mesh, in_specs=(whole,) * 5 + (P("groups"),) * 4, out_specs=(whole,) * 4, check_vma=False
    )
```

```python
import functools
import math

import jax
import jax.numpy as jnp
from jax import lax
from jax.experimental import pallas as pl
from jax.experimental.pallas import tpu as pltpu
from jax.sharding import PartitionSpec as P

beta_one = 0.9
beta_two = 0.999
epsilon = 1e-08

MIB = 1 << 20
SMEM = pl.BlockSpec(memory_space=pltpu.SMEM)
VMEM = pl.BlockSpec(memory_space=pltpu.VMEM)
ANY = pl.BlockSpec(memory_space=pl.ANY)


def cost(flops, moved):
    return pl.CostEstimate(flops=flops, bytes_accessed=moved, transcendentals=0)


def partial_kernel(n, chains, scale, where_ref, context_ref, cotangent_ref, *refs):
    blocks, (product, sems) = refs[:-2], refs[-2:]
    width = product.shape[0]
    rows = width // n
    part = rows // chains
    me = where_ref[0]
    tile = min(256, width)
    for start in range(0, width, tile):
        product[start:start + tile, :] = scale * lax.dot_general(
            context_ref[:, start:start + tile], cotangent_ref[...],
            (((0,), (0,)), ((), ())), preferred_element_type=jnp.float32,
        )
    copies = []
    for i in range(n):
        for c in range(chains):
            first_row = pl.multiple_of(lax.rem(me + i, n) * rows + c * part, part)
            copies.append(pltpu.make_async_copy(
                product.at[pl.ds(first_row, part), :], blocks[i * chains + c], sems.at[i * chains + c]
            ))
            copies[-1].start()
    for copy in copies:
        copy.wait()


def partial_blocks(n, chains, scale, where, context_rows, cotangent):
    tokens, width = context_rows.shape
    depth = cotangent.shape[1]
    part = width // n // chains
    return pl.pallas_call(
        functools.partial(partial_kernel, n, chains, scale),
        out_shape=[jax.ShapeDtypeStruct((part, depth), jnp.float32)] * (n * chains),
        in_specs=[SMEM, VMEM, VMEM],
        out_specs=[ANY] * (n * chains),
        scratch_shapes=[pltpu.VMEM((width, depth), jnp.float32), pltpu.SemaphoreType.DMA((n * chains,))],
        compiler_params=pltpu.CompilerParams(vmem_limit_bytes=20 * MIB),
        cost_estimate=cost(2 * tokens * width * depth, 6 * MIB),
        name="partial_blocks",
    )(where, context_rows, cotangent)


def columns_kernel(n, chains, scale, where_ref, cotangent_ref, *refs):
    blocks, (out_ref, full, sems) = refs[:-3], refs[-3:]
    rows = full.shape[0] // n
    part = rows // chains
    me = where_ref[0]
    moves = []
    for k in range(2 * n - 1):
        shard = me + (k - (n - 1))
        there = jnp.logical_and(shard >= 0, shard < n)
        for c in range(chains):
            first_row = pl.multiple_of(jnp.clip(shard, 0, n - 1) * rows + c * part, part)
            moves.append((there, pltpu.make_async_copy(
                blocks[k * chains + c], full.at[pl.ds(first_row, part), :], sems.at[k * chains + c]
            )))
    for there, copy in moves:
        pl.when(there)(copy.start)
    for there, copy in moves:
        pl.when(there)(copy.wait)
    width = full.shape[0]
    tile = min(256, width)
    for start in range(0, width, tile):
        out_ref[:, start:start + tile] = (scale * lax.dot_general(
            cotangent_ref[...], full[start:start + tile, :],
            (((1,), (1,)), ((), ())), preferred_element_type=jnp.float32,
        )).astype(out_ref.dtype)


def columns(n, chains, scale, where, cotangent, blocks):
    tokens, depth = cotangent.shape
    width = blocks[0].shape[0] * n * chains
    return pl.pallas_call(
        functools.partial(columns_kernel, n, chains, scale),
        out_shape=jax.ShapeDtypeStruct((tokens, width), cotangent.dtype),
        in_specs=[SMEM, VMEM] + [ANY] * len(blocks),
        out_specs=VMEM,
        scratch_shapes=[pltpu.VMEM((width, depth), cotangent.dtype), pltpu.SemaphoreType.DMA((len(blocks),))],
        compiler_params=pltpu.CompilerParams(vmem_limit_bytes=20 * MIB),
        cost_estimate=cost(2 * tokens * width * depth, 4 * MIB),
        name="context_grad",
    )(where, cotangent, *blocks)


def adam_kernel(chain, part, filled, where_ref, rates_ref, decays_ref, steps_ref, donor_ref, *refs):
    own, donated, grads = refs[:3], refs[3:6], refs[6:10]
    refs = refs[10 + (3 if filled else 0):]
    outs, (kept, taken, grad, stepped, sems, out_sems) = refs[:3], refs[3:]
    rows = own[0].shape[0]
    member = where_ref[1]
    donor = donor_ref[member]
    source = jnp.where(donor >= 0, donor, member)
    way = jnp.bitwise_xor(source, member)
    rate, decay = rates_ref[source], decays_ref[source]
    count = jnp.full((1, grad.shape[1]), (steps_ref[source] + 1).astype(jnp.float32))
    scale_one = 1.0 / (1.0 - jnp.exp(count * math.log(beta_one)))
    scale_two = 1.0 / (1.0 - jnp.exp(count * math.log(beta_two)))
    mine = pl.ds(chain * part, part)

    def own_copy(k):
        return pltpu.make_async_copy(own[k].at[mine, :], kept.at[k], sems.at[k])

    def donated_copy(w, k):
        return pltpu.make_async_copy(
            donated[w - 1].at[pl.ds(k * rows + chain * part, part), :], taken.at[k], sems.at[k]
        )

    def grad_copy(w):
        return pltpu.make_async_copy(grads[w], grad, sems.at[3])

    def step(i, from_own):
        at = pl.ds(pl.multiple_of(i * 16, 16), 16)
        load = lambda k: kept[k, at, :] if from_own else taken[k, at, :].astype(jnp.float32)
        g = grad[at, :].astype(jnp.float32)
        w = load(0)
        first_step = beta_one * load(1) + (1.0 - beta_one) * g
        second_step = beta_two * load(2) + (1.0 - beta_two) * g * g
        ratio = (first_step * scale_one) / (jnp.sqrt(second_step * scale_two) + epsilon)
        stepped[0, at, :] = w - rate * (ratio + decay * w)
        stepped[1, at, :] = first_step
        stepped[2, at, :] = second_step

    for w in range(4):
        @pl.when(way == w)
        def _():
            grad_copy(w).start()
            for k in range(3):
                (own_copy(k) if w == 0 else donated_copy(w, k)).start()
            grad_copy(w).wait()
            for k in range(3):
                (own_copy(k) if w == 0 else donated_copy(w, k)).wait()

    @pl.when(way == 0)
    def _():
        pl.loop(0, part // 16)(lambda i: step(i, True))

    @pl.when(way != 0)
    def _():
        pl.loop(0, part // 16)(lambda i: step(i, False))

    writes = [
        pltpu.make_async_copy(stepped.at[k], outs[k].at[mine, :], out_sems.at[k]) for k in range(3)
    ]
    for write in writes:
        write.start()
    for write in writes:
        write.wait()


def adam_update(chain, part, where, tables, own, donated, grads, filled):
    rows, depth = own[0].shape
    shape = jax.ShapeDtypeStruct((rows, depth), jnp.float32)
    before = 5 + 3 + 3 + 4
    return pl.pallas_call(
        functools.partial(adam_kernel, chain, part, bool(filled)),
        out_shape=[shape] * 3,
        in_specs=[SMEM] * 5 + [ANY] * (10 + len(filled)),
        out_specs=[ANY] * 3,
        scratch_shapes=[
            pltpu.VMEM((3, part, depth), jnp.float32),
            pltpu.VMEM((3, part, depth), jnp.bfloat16),
            pltpu.VMEM((part, depth), jnp.bfloat16),
            pltpu.VMEM((3, part, depth), jnp.float32),
            pltpu.SemaphoreType.DMA((4,)),
            pltpu.SemaphoreType.DMA((3,)),
        ],
        input_output_aliases={before + k: k for k in range(len(filled))},
        compiler_params=pltpu.CompilerParams(vmem_limit_bytes=16 * MIB),
        cost_estimate=cost(30 * part * depth, 26 * part * depth),
        name="adam",
    )(where, *tables, *own, *donated, *grads, *filled)


def on_device(n, members, context, out_grad, weight, first, second, rates, decays, steps, donor):
    context_rows = context[0]
    cotangent = out_grad[0]
    scale = context_rows.shape[1] ** (-0.5)
    rows = weight.shape[1]
    chains = 2 if rows % 32 == 0 else 1
    part = rows // chains
    half = jnp.bfloat16
    me = lax.axis_index("shard")
    where = jnp.stack([me, lax.axis_index("member")]).astype(jnp.int32)

    swap_across = [(m, m ^ 2) for m in range(members)]
    swap_mates = [(m, m ^ 1) for m in range(members)]
    to_right = [(s, s + 1) for s in range(n - 1)]
    to_left = [(s + 1, s) for s in range(n - 1)]

    def from_members(own):
        across = lax.ppermute(own, "member", swap_across)
        mate = lax.ppermute(own, "member", swap_mates)
        return mate, across, lax.ppermute(across, "member", swap_mates)

    half_weight = weight[0].astype(half)
    pieces = [half_weight[c * part:(c + 1) * part] for c in range(chains)]
    partial = partial_blocks(n, chains, scale, where, context_rows, cotangent)

    from_left, from_right = [pieces], [pieces]
    for slot in range(1, n + 1):
        right, left = from_left[-1], from_right[-1]
        if slot > 1:
            def added(arrived, block, forwards):
                term = jnp.where(forwards, 0.0, block)
                return (arrived.astype(jnp.float32) + term).astype(half)

            right = [
                added(right[c], partial[(n + 1 - slot) * chains + c], me >= slot - 1)
                for c in range(chains)
            ]
            left = [
                added(left[c], partial[(slot - 1) * chains + c], n - 1 - me >= slot - 1)
                for c in range(chains)
            ]
        arrived = [
            (lax.ppermute(right[c], "shard", to_right), lax.ppermute(left[c], "shard", to_left))
            for c in range(chains)
        ]
        from_left.append([pair[0] for pair in arrived])
        from_right.append([pair[1] for pair in arrived])

    state = jnp.concatenate([half_weight, first[0].astype(half), second[0].astype(half)], axis=0)
    donated = from_members(state)

    blocks = from_left[n - 1:0:-1] + [pieces] + from_right[1:n]
    context_grad = columns(n, chains, scale, where, cotangent, [b for pair in blocks for b in pair])

    tables = (rates, decays, steps, donor)
    updated = ()
    for c in range(chains):
        grad = partial[c] + from_left[n][c].astype(jnp.float32) + from_right[n][c].astype(jnp.float32)
        grad = grad.astype(half)
        updated = adam_update(
            c, part, where, tables, (weight[0], first[0], second[0]), donated,
            (grad,) + from_members(grad), updated,
        )
    return (context_grad[None],) + tuple(array[None] for array in updated)


def solution(mesh):
    whole = P(("groups", "member"), "shard", None)
    n, members = mesh.shape["shard"], mesh.shape["member"]
    return jax.shard_map(
        functools.partial(on_device, n, members),
        mesh=mesh,
        in_specs=(whole,) * 5 + (P("groups"),) * 4,
        out_specs=(whole,) * 4,
        check_vma=False,
    )
```

```python
import functools
import math

import jax
import jax.numpy as jnp
from jax import lax
from jax.experimental import pallas as pl
from jax.experimental.pallas import tpu as pltpu
from jax.sharding import PartitionSpec as P

beta_one = 0.9
beta_two = 0.999
epsilon = 1e-08

MIB = 1 << 20
SMEM = pl.BlockSpec(memory_space=pltpu.SMEM)
VMEM = pl.BlockSpec(memory_space=pltpu.VMEM)
ANY = pl.BlockSpec(memory_space=pl.ANY)


SMALL = pl.CostEstimate(flops=0, bytes_accessed=1024, transcendentals=0)


def partial_kernel(n, scale, order, where_ref, context_ref, cotangent_ref, *refs):
    blocks, (product, sems) = refs[:-2], refs[-2:]
    width = product.shape[0]
    rows = width // n
    me = where_ref[0]
    tile = min(256, width)
    for start in range(0, width, tile):
        product[start:start + tile, :] = scale * lax.dot_general(
            context_ref[:, start:start + tile], cotangent_ref[...],
            (((0,), (0,)), ((), ())), preferred_element_type=jnp.float32,
        )
    copies = []
    for k, ahead in enumerate(order):
        first_row = pl.multiple_of(lax.rem(me + ahead, n) * rows, rows)
        copies.append(pltpu.make_async_copy(product.at[pl.ds(first_row, rows), :], blocks[k], sems.at[k]))
        copies[-1].start()
    for copy in copies:
        copy.wait()


def partial_blocks(n, scale, order, where, context_rows, cotangent):
    width, depth = context_rows.shape[1], cotangent.shape[1]
    return pl.pallas_call(
        functools.partial(partial_kernel, n, scale, order),
        out_shape=[jax.ShapeDtypeStruct((width // n, depth), jnp.float32)] * len(order),
        in_specs=[SMEM, VMEM, VMEM],
        out_specs=[ANY] * len(order),
        scratch_shapes=[pltpu.VMEM((width, depth), jnp.float32), pltpu.SemaphoreType.DMA((len(order),))],
        compiler_params=pltpu.CompilerParams(vmem_limit_bytes=20 * MIB),
        cost_estimate=SMALL,
        name="partial_blocks",
    )(where, context_rows, cotangent)


def send_kernel(slot, n, to_right, where_ref, arrived_ref, term_ref, out_ref):
    place = where_ref[0] if to_right else n - 1 - where_ref[0]
    forwards = place >= slot - 1

    @pl.when(forwards)
    def _():
        out_ref[...] = arrived_ref[...]

    @pl.when(jnp.logical_not(forwards))
    def _():
        @pl.loop(0, out_ref.shape[0] // 16)
        def _(i):
            at = pl.ds(pl.multiple_of(i * 16, 16), 16)
            out_ref[at, :] = (arrived_ref[at, :].astype(jnp.float32) + term_ref[at, :]).astype(out_ref.dtype)


def to_send(slot, n, to_right, where, arrived, term, c, part):
    block = pl.BlockSpec((part, arrived.shape[1]), lambda i: (c, 0))
    return pl.pallas_call(
        functools.partial(send_kernel, slot, n, to_right),
        grid=(1,),
        out_shape=jax.ShapeDtypeStruct((part, arrived.shape[1]), arrived.dtype),
        in_specs=[SMEM, block, block],
        out_specs=pl.BlockSpec((part, arrived.shape[1]), lambda i: (0, 0)),
        compiler_params=pltpu.CompilerParams(vmem_limit_bytes=8 * MIB),
        cost_estimate=SMALL,
        name="to_send",
    )(where, arrived, term)


def grad_kernel(term_ref, left_ref, right_ref, _, out_ref):
    @pl.loop(0, out_ref.shape[0] // 16)
    def _(i):
        at = pl.ds(pl.multiple_of(i * 16, 16), 16)
        arrived = left_ref[at, :].astype(jnp.float32) + right_ref[at, :].astype(jnp.float32)
        out_ref[at, :] = (term_ref[at, :] + arrived).astype(out_ref.dtype)


def summed_grad(term, from_left, from_right, after, c):
    part, depth = from_left.shape
    own = pl.BlockSpec((part, depth), lambda i: (c, 0))
    block = pl.BlockSpec((part, depth), lambda i: (0, 0))
    return pl.pallas_call(
        grad_kernel,
        grid=(1,),
        out_shape=jax.ShapeDtypeStruct((part, depth), from_left.dtype),
        in_specs=[own, block, block, ANY],
        out_specs=block,
        compiler_params=pltpu.CompilerParams(vmem_limit_bytes=8 * MIB),
        cost_estimate=SMALL,
        name="summed_grad",
    )(term, from_left, from_right, after)


def columns_kernel(n, scale, where_ref, cotangent_ref, *refs):
    blocks, (out_ref, full, sems) = refs[:-3], refs[-3:]
    rows = full.shape[0] // n
    me = where_ref[0]
    moves = []
    for k in range(2 * n - 1):
        shard = me + (k - (n - 1))
        there = jnp.logical_and(shard >= 0, shard < n)
        first_row = pl.multiple_of(jnp.clip(shard, 0, n - 1) * rows, rows)
        moves.append((there, pltpu.make_async_copy(
            blocks[k], full.at[pl.ds(first_row, rows), :], sems.at[k]
        )))
    for there, copy in moves:
        pl.when(there)(copy.start)
    for there, copy in moves:
        pl.when(there)(copy.wait)
    width = full.shape[0]
    tile = min(256, width)
    for start in range(0, width, tile):
        out_ref[:, start:start + tile] = (scale * lax.dot_general(
            cotangent_ref[...], full[start:start + tile, :],
            (((1,), (1,)), ((), ())), preferred_element_type=jnp.float32,
        )).astype(out_ref.dtype)


def columns(n, scale, where, cotangent, blocks):
    tokens, depth = cotangent.shape
    width = blocks[0].shape[0] * n
    return pl.pallas_call(
        functools.partial(columns_kernel, n, scale),
        out_shape=jax.ShapeDtypeStruct((tokens, width), cotangent.dtype),
        in_specs=[SMEM, VMEM] + [ANY] * len(blocks),
        out_specs=VMEM,
        scratch_shapes=[pltpu.VMEM((width, depth), cotangent.dtype), pltpu.SemaphoreType.DMA((len(blocks),))],
        compiler_params=pltpu.CompilerParams(vmem_limit_bytes=20 * MIB),
        cost_estimate=SMALL,
        name="context_grad",
    )(where, cotangent, *blocks)


def adam_kernel(chain, part, filled, where_ref, rates_ref, decays_ref, steps_ref, donor_ref, *refs):
    own, donated, grads = refs[:3], refs[3:6], refs[6:10]
    refs = refs[10 + (3 if filled else 0):]
    outs, (kept, taken, grad, stepped, sems, out_sems) = refs[:3], refs[3:]
    rows = own[0].shape[0]
    member = where_ref[1]
    donor = donor_ref[member]
    source = jnp.where(donor >= 0, donor, member)
    way = jnp.bitwise_xor(source, member)
    rate, decay = rates_ref[source], decays_ref[source]
    count = jnp.full((1, grad.shape[1]), (steps_ref[source] + 1).astype(jnp.float32))
    scale_one = 1.0 / (1.0 - jnp.exp(count * math.log(beta_one)))
    scale_two = 1.0 / (1.0 - jnp.exp(count * math.log(beta_two)))
    mine = pl.ds(chain * part, part)

    def own_copy(k):
        return pltpu.make_async_copy(own[k].at[mine, :], kept.at[k], sems.at[k])

    def donated_copy(w, k):
        return pltpu.make_async_copy(
            donated[w - 1].at[pl.ds(k * rows + chain * part, part), :], taken.at[k], sems.at[k]
        )

    def grad_copy(w):
        return pltpu.make_async_copy(grads[w], grad, sems.at[3])

    def step(i, from_own):
        at = pl.ds(pl.multiple_of(i * 16, 16), 16)
        load = lambda k: kept[k, at, :] if from_own else taken[k, at, :].astype(jnp.float32)
        g = grad[at, :].astype(jnp.float32)
        w = load(0)
        first_step = beta_one * load(1) + (1.0 - beta_one) * g
        second_step = beta_two * load(2) + (1.0 - beta_two) * g * g
        ratio = (first_step * scale_one) / (jnp.sqrt(second_step * scale_two) + epsilon)
        stepped[0, at, :] = w - rate * (ratio + decay * w)
        stepped[1, at, :] = first_step
        stepped[2, at, :] = second_step

    for w in range(4):
        @pl.when(way == w)
        def _():
            grad_copy(w).start()
            for k in range(3):
                (own_copy(k) if w == 0 else donated_copy(w, k)).start()
            grad_copy(w).wait()
            for k in range(3):
                (own_copy(k) if w == 0 else donated_copy(w, k)).wait()

    @pl.when(way == 0)
    def _():
        pl.loop(0, part // 16)(lambda i: step(i, True))

    @pl.when(way != 0)
    def _():
        pl.loop(0, part // 16)(lambda i: step(i, False))

    writes = [
        pltpu.make_async_copy(stepped.at[k], outs[k].at[mine, :], out_sems.at[k]) for k in range(3)
    ]
    for write in writes:
        write.start()
    for write in writes:
        write.wait()


def adam_update(chain, part, where, tables, own, donated, grads, filled):
    rows, depth = own[0].shape
    shape = jax.ShapeDtypeStruct((rows, depth), jnp.float32)
    before = 5 + 3 + 3 + 4
    return pl.pallas_call(
        functools.partial(adam_kernel, chain, part, bool(filled)),
        out_shape=[shape] * 3,
        in_specs=[SMEM] * 5 + [ANY] * (10 + len(filled)),
        out_specs=[ANY] * 3,
        scratch_shapes=[
            pltpu.VMEM((3, part, depth), jnp.float32),
            pltpu.VMEM((3, part, depth), jnp.bfloat16),
            pltpu.VMEM((part, depth), jnp.bfloat16),
            pltpu.VMEM((3, part, depth), jnp.float32),
            pltpu.SemaphoreType.DMA((4,)),
            pltpu.SemaphoreType.DMA((3,)),
        ],
        input_output_aliases={before + k: k for k in range(len(filled))},
        compiler_params=pltpu.CompilerParams(vmem_limit_bytes=16 * MIB),
        cost_estimate=SMALL,
        name="adam",
    )(where, *tables, *own, *donated, *grads, *filled)


def on_device(n, members, context, out_grad, weight, first, second, rates, decays, steps, donor):
    context_rows = context[0]
    cotangent = out_grad[0]
    scale = context_rows.shape[1] ** (-0.5)
    rows = weight.shape[1]
    chains = 2 if rows % 32 == 0 else 1
    part = rows // chains
    half = jnp.bfloat16
    me = lax.axis_index("shard")
    where = jnp.stack([me, lax.axis_index("member")]).astype(jnp.int32)

    swap_across = [(m, m ^ 2) for m in range(members)]
    swap_mates = [(m, m ^ 1) for m in range(members)]
    to_right = [(s, s + 1) for s in range(n - 1)]
    to_left = [(s + 1, s) for s in range(n - 1)]

    def from_members(own):
        across = lax.ppermute(own, "member", swap_across)
        mate = lax.ppermute(own, "member", swap_mates)
        return mate, across, lax.ppermute(across, "member", swap_mates)

    half_weight = weight[0].astype(half)
    order = list(range(n - 1, 0, -1)) + list(range(1, n)) + [0]
    terms = partial_blocks(n, scale, order, where, context_rows, cotangent)
    right_terms, left_terms, own_term = terms[:n - 1], terms[n - 1:-1], terms[-1]

    from_left, from_right = [half_weight], [half_weight]
    for slot in range(1, n):
        right, left = from_left[-1], from_right[-1]
        if slot > 1:
            right = to_send(slot, n, True, where, right, right_terms[slot - 2], 0, rows)
            left = to_send(slot, n, False, where, left, left_terms[slot - 2], 0, rows)
        from_left.append(lax.ppermute(right, "shard", to_right))
        from_right.append(lax.ppermute(left, "shard", to_left))
    last_left, last_right = [], []
    for c in range(chains):
        right = to_send(n, n, True, where, from_left[-1], right_terms[-1], c, part)
        left = to_send(n, n, False, where, from_right[-1], left_terms[-1], c, part)
        last_left.append(lax.ppermute(right, "shard", to_right))
        last_right.append(lax.ppermute(left, "shard", to_left))

    state = jnp.concatenate([half_weight, first[0].astype(half), second[0].astype(half)], axis=0)
    donated = from_members(state)

    blocks = from_left[n - 1:0:-1] + [half_weight] + from_right[1:n]
    context_grad = columns(n, scale, where, cotangent, blocks)

    tables = (rates, decays, steps, donor)
    updated = ()
    for c in range(chains):
        grad = summed_grad(own_term, last_left[c], last_right[c], context_grad, c)
        updated = adam_update(
            c, part, where, tables, (weight[0], first[0], second[0]), donated,
            (grad,) + from_members(grad), updated,
        )
    return (context_grad[None],) + tuple(array[None] for array in updated)


def solution(mesh):
    whole = P(("groups", "member"), "shard", None)
    n, members = mesh.shape["shard"], mesh.shape["member"]
    return jax.shard_map(
        functools.partial(on_device, n, members),
        mesh=mesh,
        in_specs=(whole,) * 5 + (P("groups"),) * 4,
        out_specs=(whole,) * 4,
        check_vma=False,
    )
```

```python
import functools
import math

import jax
import jax.numpy as jnp
from jax import lax
from jax.experimental import pallas as pl
from jax.experimental.pallas import tpu as pltpu
from jax.sharding import PartitionSpec as P

beta_one = 0.9
beta_two = 0.999
epsilon = 1e-08

MIB = 1 << 20
SMEM = pl.BlockSpec(memory_space=pltpu.SMEM)
VMEM = pl.BlockSpec(memory_space=pltpu.VMEM)
ANY = pl.BlockSpec(memory_space=pl.ANY)


SMALL = pl.CostEstimate(flops=0, bytes_accessed=1024, transcendentals=0)


def halves_kernel(parts, weight_ref, first_ref, second_ref, state_ref, *own_refs):
    rows = weight_ref.shape[0]
    for (start, size), own_ref in zip(parts, own_refs):
        own_ref[...] = weight_ref[start:start + size, :].astype(own_ref.dtype)
    for k, ref in enumerate((weight_ref, first_ref, second_ref)):
        state_ref[k * rows:(k + 1) * rows, :] = ref[...].astype(state_ref.dtype)


def halves(parts, weight, first, second):
    rows, depth = weight.shape
    sizes = [3 * rows] + [size for _, size in parts]
    return pl.pallas_call(
        functools.partial(halves_kernel, parts),
        out_shape=[jax.ShapeDtypeStruct((size, depth), jnp.bfloat16) for size in sizes],
        in_specs=[VMEM] * 3,
        out_specs=[VMEM] * len(sizes),
        compiler_params=pltpu.CompilerParams(vmem_limit_bytes=12 * MIB),
        cost_estimate=SMALL,
        name="halves",
    )(weight, first, second)


def source_of(member, donor_ref):
    donor = donor_ref[member]
    return jnp.where(donor >= 0, donor, member)


def pick_kernel(where_ref, donor_ref, own_ref, mate_ref, after_ref, out_ref, sem):
    member = where_ref[1]
    wants_mate = source_of(jnp.bitwise_xor(member, 2), donor_ref) == jnp.bitwise_xor(member, 1)
    for ref, wanted in ((own_ref, jnp.logical_not(wants_mate)), (mate_ref, wants_mate)):
        @pl.when(wanted)
        def _():
            copy = pltpu.make_async_copy(ref, out_ref, sem.at[0])
            copy.start()
            copy.wait()


def pick(where, donor, own, mate, after):
    return pl.pallas_call(
        pick_kernel,
        out_shape=jax.ShapeDtypeStruct(own.shape, own.dtype),
        in_specs=[SMEM, SMEM, ANY, ANY, ANY],
        out_specs=ANY,
        scratch_shapes=[pltpu.SemaphoreType.DMA((1,))],
        cost_estimate=SMALL,
        name="pick",
    )(where, donor, own, mate, after)


def partial_kernel(n, scale, parts, order, where_ref, context_ref, cotangent_ref, *refs):
    blocks, (product, sems) = refs[:-2], refs[-2:]
    width = product.shape[0]
    rows = width // n
    me = where_ref[0]
    even = lax.rem(me, 2) == 0
    tile = min(256, width)
    for start in range(0, width, tile):
        product[start:start + tile, :] = scale * lax.dot_general(
            context_ref[:, start:start + tile], cotangent_ref[...],
            (((0,), (0,)), ((), ())), preferred_element_type=jnp.float32,
        )
    copies = []
    for k, (if_even, if_odd) in enumerate(order):
        block = lax.rem(me + jnp.where(even, if_even, if_odd), n)
        for c, (first, size) in enumerate(parts):
            at = k * len(parts) + c
            first_row = pl.multiple_of(block * rows + first, 8)
            copies.append(pltpu.make_async_copy(
                product.at[pl.ds(first_row, size), :], blocks[at], sems.at[at]
            ))
            copies[-1].start()
    for copy in copies:
        copy.wait()


def partial_blocks(n, scale, parts, order, where, context_rows, cotangent):
    width, depth = context_rows.shape[1], cotangent.shape[1]
    outs = len(order) * len(parts)
    flat = pl.pallas_call(
        functools.partial(partial_kernel, n, scale, parts, order),
        out_shape=[jax.ShapeDtypeStruct((size, depth), jnp.float32) for _, size in parts] * len(order),
        in_specs=[SMEM, VMEM, VMEM],
        out_specs=[ANY] * outs,
        scratch_shapes=[pltpu.VMEM((width, depth), jnp.float32), pltpu.SemaphoreType.DMA((outs,))],
        compiler_params=pltpu.CompilerParams(vmem_limit_bytes=20 * MIB),
        cost_estimate=SMALL,
        name="partial_blocks",
    )(where, context_rows, cotangent)
    return [flat[k * len(parts):(k + 1) * len(parts)] for k in range(len(order))]


def send_kernel(slot, n, swap, where_ref, arrived_ref, term_ref, after_ref, out_ref):
    me = where_ref[0]
    place = jnp.where(lax.rem(me + swap, 2) == 0, me, n - 1 - me)
    forwards = place >= slot - 1

    @pl.when(forwards)
    def _():
        out_ref[...] = arrived_ref[...]

    @pl.when(jnp.logical_not(forwards))
    def _():
        @pl.loop(0, out_ref.shape[0] // 16)
        def _(i):
            at = pl.ds(pl.multiple_of(i * 16, 16), 16)
            out_ref[at, :] = (arrived_ref[at, :].astype(jnp.float32) + term_ref[at, :]).astype(out_ref.dtype)


def to_send(slot, n, swap, where, arrived, term, after):
    return pl.pallas_call(
        functools.partial(send_kernel, slot, n, swap),
        out_shape=jax.ShapeDtypeStruct(arrived.shape, arrived.dtype),
        in_specs=[SMEM, VMEM, VMEM, ANY],
        out_specs=VMEM,
        compiler_params=pltpu.CompilerParams(vmem_limit_bytes=8 * MIB),
        cost_estimate=SMALL,
        name="to_send",
    )(where, arrived, term, after)


def grad_kernel(term_ref, one_ref, other_ref, after_ref, out_ref):
    @pl.loop(0, out_ref.shape[0] // 16)
    def _(i):
        at = pl.ds(pl.multiple_of(i * 16, 16), 16)
        arrived = one_ref[at, :].astype(jnp.float32) + other_ref[at, :].astype(jnp.float32)
        out_ref[at, :] = (term_ref[at, :] + arrived).astype(out_ref.dtype)


def summed_grad(term, one, other, after):
    return pl.pallas_call(
        grad_kernel,
        out_shape=jax.ShapeDtypeStruct(one.shape, one.dtype),
        in_specs=[VMEM, VMEM, VMEM, ANY],
        out_specs=VMEM,
        compiler_params=pltpu.CompilerParams(vmem_limit_bytes=8 * MIB),
        cost_estimate=SMALL,
        name="summed_grad",
    )(term, one, other, after)


def columns_kernel(n, scale, parts, where_ref, cotangent_ref, after_ref, *refs):
    blocks, (out_ref, token_ref, full, result, sems, out_sems) = refs[:-6], refs[-6:]
    token_ref[...] = jnp.zeros_like(token_ref)
    width = full.shape[0]
    rows = width // n
    me = where_ref[0]
    even = lax.rem(me, 2) == 0
    moves = []
    for k in range(2 * n - 1):
        slot, swap = (k + 1) // 2, (k + 1) % 2
        shard = me + (jnp.where(even, slot, -slot) if swap == 0 else jnp.where(even, -slot, slot))
        there = jnp.logical_and(shard >= 0, shard < n)
        for c, (first, size) in enumerate(parts):
            at = k * len(parts) + c
            first_row = pl.multiple_of(jnp.clip(shard, 0, n - 1) * rows + first, 8)
            moves.append((there, pltpu.make_async_copy(
                blocks[at], full.at[pl.ds(first_row, size), :], sems.at[at]
            )))
    for there, copy in moves:
        pl.when(there)(copy.start)
    for there, copy in moves:
        pl.when(there)(copy.wait)
    tile = min(256, width)
    writes = []
    for i, start in enumerate(range(0, width, tile)):
        result[:, start:start + tile] = (scale * lax.dot_general(
            cotangent_ref[...], full[start:start + tile, :],
            (((1,), (1,)), ((), ())), preferred_element_type=jnp.float32,
        )).astype(out_ref.dtype)
        writes.append(pltpu.make_async_copy(
            result.at[:, start:start + tile], out_ref.at[:, start:start + tile], out_sems.at[i]
        ))
        writes[-1].start()
    for write in writes:
        write.wait()


def columns(n, scale, parts, where, cotangent, after, blocks):
    tokens, depth = cotangent.shape
    width = n * sum(size for _, size in parts)
    return pl.pallas_call(
        functools.partial(columns_kernel, n, scale, parts),
        out_shape=[
            jax.ShapeDtypeStruct((tokens, width), cotangent.dtype), jax.ShapeDtypeStruct((8, 128), jnp.float32)
        ],
        in_specs=[SMEM, VMEM, ANY] + [ANY] * len(blocks),
        out_specs=[pl.BlockSpec(memory_space=pltpu.HBM), VMEM],
        scratch_shapes=[
            pltpu.VMEM((width, depth), cotangent.dtype),
            pltpu.VMEM((tokens, width), cotangent.dtype),
            pltpu.SemaphoreType.DMA((len(blocks),)),
            pltpu.SemaphoreType.DMA((width // min(256, width),)),
        ],
        compiler_params=pltpu.CompilerParams(vmem_limit_bytes=20 * MIB),
        cost_estimate=SMALL,
        name="context_grad",
    )(where, cotangent, after, *blocks)


def adam_kernel(first_row, part, filled, where_ref, rates_ref, decays_ref, steps_ref, donor_ref, *refs):
    own, donated, grads = refs[:3], refs[3:5], refs[5:8]
    refs = refs[9 + (3 if filled else 0):]
    outs, (kept, taken, grad, stepped, sems, out_sems) = refs[:3], refs[3:]
    rows = own[0].shape[0]
    member = where_ref[1]
    source = source_of(member, donor_ref)
    way = jnp.minimum(jnp.bitwise_xor(source, member), 2)
    rate, decay = rates_ref[source], decays_ref[source]
    count = jnp.full((1, grad.shape[1]), (steps_ref[source] + 1).astype(jnp.float32))
    scale_one = 1.0 / (1.0 - jnp.exp(count * math.log(beta_one)))
    scale_two = 1.0 / (1.0 - jnp.exp(count * math.log(beta_two)))
    mine = pl.ds(first_row, part)

    def own_copy(k):
        return pltpu.make_async_copy(own[k].at[mine, :], kept.at[k], sems.at[k])

    def donated_copy(w, k):
        return pltpu.make_async_copy(
            donated[w - 1].at[pl.ds(k * rows + first_row, part), :], taken.at[k], sems.at[k]
        )

    def grad_copy(w):
        return pltpu.make_async_copy(grads[w], grad, sems.at[3])

    def step(i, from_own):
        at = pl.ds(pl.multiple_of(i * 16, 16), 16)
        load = lambda k: kept[k, at, :] if from_own else taken[k, at, :].astype(jnp.float32)
        g = grad[at, :].astype(jnp.float32)
        w = load(0)
        first_step = beta_one * load(1) + (1.0 - beta_one) * g
        second_step = beta_two * load(2) + (1.0 - beta_two) * g * g
        ratio = (first_step * scale_one) / (jnp.sqrt(second_step * scale_two) + epsilon)
        stepped[0, at, :] = w - rate * (ratio + decay * w)
        stepped[1, at, :] = first_step
        stepped[2, at, :] = second_step

    for w in range(3):
        @pl.when(way == w)
        def _():
            grad_copy(w).start()
            for k in range(3):
                (own_copy(k) if w == 0 else donated_copy(w, k)).start()
            grad_copy(w).wait()
            for k in range(3):
                (own_copy(k) if w == 0 else donated_copy(w, k)).wait()

    @pl.when(way == 0)
    def _():
        pl.loop(0, part // 16)(lambda i: step(i, True))

    @pl.when(way != 0)
    def _():
        pl.loop(0, part // 16)(lambda i: step(i, False))

    writes = [
        pltpu.make_async_copy(stepped.at[k], outs[k].at[mine, :], out_sems.at[k]) for k in range(3)
    ]
    for write in writes:
        write.start()
    for write in writes:
        write.wait()


def adam_update(first_row, part, where, tables, own, donated, grads, after, filled):
    rows, depth = own[0].shape
    shape = jax.ShapeDtypeStruct((rows, depth), jnp.float32)
    before = 5 + 3 + 2 + 3 + 1
    return pl.pallas_call(
        functools.partial(adam_kernel, first_row, part, bool(filled)),
        out_shape=[shape] * 3,
        in_specs=[SMEM] * 5 + [ANY] * (9 + len(filled)),
        out_specs=[ANY] * 3,
        scratch_shapes=[
            pltpu.VMEM((3, part, depth), jnp.float32),
            pltpu.VMEM((3, part, depth), jnp.bfloat16),
            pltpu.VMEM((part, depth), jnp.bfloat16),
            pltpu.VMEM((3, part, depth), jnp.float32),
            pltpu.SemaphoreType.DMA((4,)),
            pltpu.SemaphoreType.DMA((3,)),
        ],
        input_output_aliases={before + k: k for k in range(len(filled))},
        compiler_params=pltpu.CompilerParams(vmem_limit_bytes=16 * MIB),
        cost_estimate=SMALL,
        name="adam",
    )(where, *tables, *own, *donated, *grads, after, *filled)


def on_device(n, members, context, out_grad, weight, first, second, rates, decays, steps, donor):
    context_rows = context[0]
    cotangent = out_grad[0]
    scale = context_rows.shape[1] ** (-0.5)
    rows = weight.shape[1]
    chains = 2 if rows % 32 == 0 else 1
    parts = [(c * rows // chains, rows // chains) for c in range(chains)]
    where = jnp.stack([lax.axis_index("shard"), lax.axis_index("member")]).astype(jnp.int32)

    swap_across = [(m, m ^ 2) for m in range(members)]
    swap_mates = [(m, m ^ 1) for m in range(members)]
    swaps = []
    for swap in range(2):
        pairs = [(s, s + 1) for s in range(swap, n - 1, 2)]
        swaps.append(pairs + [(b, a) for a, b in pairs])

    state, *own = halves(parts, weight[0], first[0], second[0])
    order = []
    for slot in range(2, n + 1):
        order += [(n + 1 - slot, slot - 1), (slot - 1, n + 1 - slot)]
    terms = partial_blocks(n, scale, parts, order + [(0, 0)], where, context_rows, cotangent)

    arrived = [[own, own]]
    for slot in range(1, n + 1):
        now = [[], []]
        for c in range(len(parts)):
            for swap in range(2):
                block = arrived[-1][1 - swap][c]
                if slot > 1:
                    block = to_send(slot, n, swap, where, block, terms[2 * (slot - 2) + swap][c], sent)
                now[swap].append(lax.ppermute(block, "shard", swaps[swap]))
                sent = block
                if slot <= 2 and c == 0:
                    early = block
        arrived.append(now)

    def from_members(own, after):
        mate = lax.ppermute(own, "member", swap_mates)
        return mate, lax.ppermute(pick(where, donor, own, mate, after), "member", swap_across)

    donated = from_members(state, early)

    grads = []
    for c in range(len(parts)):
        sent = summed_grad(terms[-1][c], arrived[n][0][c], arrived[n][1][c], sent)
        grads.append(sent)
    blocks = list(own)
    for slot in range(1, n):
        blocks += arrived[slot][0] + arrived[slot][1]
    context_grad, computed = columns(n, scale, parts, where, cotangent, grads[-1], blocks)

    tables = (rates, decays, steps, donor)
    updated = ()
    for (first_row, size), grad in zip(parts, grads):
        updated = adam_update(
            first_row, size, where, tables, (weight[0], first[0], second[0]), donated,
            (grad,) + from_members(grad, grad), computed, updated,
        )
    return (context_grad[None],) + tuple(array[None] for array in updated)


def solution(mesh):
    whole = P(("groups", "member"), "shard", None)
    n, members = mesh.shape["shard"], mesh.shape["member"]
    return jax.shard_map(
        functools.partial(on_device, n, members),
        mesh=mesh,
        in_specs=(whole,) * 5 + (P("groups"),) * 4,
        out_specs=(whole,) * 4,
        check_vma=False,
    )
```

```python
import functools
import math

import jax
import jax.numpy as jnp
from jax import lax
from jax.experimental import pallas as pl
from jax.experimental.pallas import tpu as pltpu
from jax.sharding import PartitionSpec as P

beta_one = 0.9
beta_two = 0.999
epsilon = 1e-08

MIB = 1 << 20
SMEM = pl.BlockSpec(memory_space=pltpu.SMEM)
VMEM = pl.BlockSpec(memory_space=pltpu.VMEM)
HBM = pl.BlockSpec(memory_space=pltpu.HBM)
ANY = pl.BlockSpec(memory_space=pl.ANY)
SMALL = pl.CostEstimate(flops=0, bytes_accessed=1024, transcendentals=0)


def call(kernel, name, out_shape, in_specs, out_specs, limit=8, scratch=(), aliases=None):
    return pl.pallas_call(
        kernel,
        out_shape=out_shape,
        in_specs=in_specs,
        out_specs=out_specs,
        scratch_shapes=scratch,
        input_output_aliases=aliases or {},
        compiler_params=pltpu.CompilerParams(vmem_limit_bytes=limit * MIB),
        cost_estimate=SMALL,
        name=name,
    )


def half_array(rows, depth):
    return jax.ShapeDtypeStruct((rows, depth), jnp.bfloat16)


def by_rows(ref, body, step=16):
    @pl.loop(0, ref.shape[0] // step)
    def _(i):
        body(pl.ds(pl.multiple_of(i * step, step), step))


def source_of(member, donor_ref):
    donor = donor_ref[member]
    return jnp.where(donor >= 0, donor, member)


def choices_kernel(where_ref, rates_ref, decays_ref, steps_ref, donor_ref, out_ref):
    member = where_ref[1]
    source = source_of(member, donor_ref)
    way = jnp.minimum(jnp.bitwise_xor(source, member), 2)
    partner_source = source_of(jnp.bitwise_xor(member, 2), donor_ref)
    flags = [partner_source == jnp.bitwise_xor(member, 1), way == 0, way == 1, way == 2]
    depth = out_ref.shape[1]
    for k, flag in enumerate(flags):
        out_ref[k:k + 1, :] = jnp.full((1, depth), jnp.where(flag, 1.0, 0.0))
    out_ref[4:5, :] = jnp.full((1, depth), rates_ref[source])
    out_ref[5:6, :] = jnp.full((1, depth), decays_ref[source])
    count = jnp.full((1, depth), (steps_ref[source] + 1).astype(jnp.float32))
    out_ref[6:7, :] = 1.0 / (1.0 - jnp.exp(count * math.log(beta_one)))
    out_ref[7:8, :] = 1.0 / (1.0 - jnp.exp(count * math.log(beta_two)))


def halves_kernel(parts, weight_ref, first_ref, second_ref, state_ref, *refs):
    own_refs, (full, sems) = refs[:-2], refs[-2:]
    rows = weight_ref.shape[0]
    copies = []
    for k, ref in enumerate((weight_ref, first_ref, second_ref)):
        for c, (start, size) in enumerate(parts):
            copies.append(pltpu.make_async_copy(
                ref.at[pl.ds(start, size), :], full.at[k, pl.ds(start, size), :], sems.at[k * len(parts) + c]
            ))
            copies[-1].start()
    for k in range(3):
        for c, (start, size) in enumerate(parts):
            copies[k * len(parts) + c].wait()
            rounded = full[k, start:start + size, :].astype(jnp.bfloat16)
            if k == 0:
                own_refs[c][...] = rounded
            state_ref[k * rows + start:k * rows + start + size, :] = rounded


def halves(parts, weight, first, second):
    rows, depth = weight.shape
    sizes = [3 * rows] + [size for _, size in parts]
    return call(
        functools.partial(halves_kernel, parts), "halves",
        [half_array(size, depth) for size in sizes], [HBM] * 3, [VMEM] * len(sizes), limit=56,
        scratch=[pltpu.VMEM((3, rows, depth), jnp.float32), pltpu.SemaphoreType.DMA((3 * len(parts),))],
    )(weight, first, second)


def pick_kernel(choices_ref, own_ref, mate_ref, after_ref, out_ref):
    def body(at):
        wants_mate = jnp.broadcast_to(choices_ref[0:1, :], (16, out_ref.shape[1])) > 0
        own, mate = own_ref[at, :].astype(jnp.float32), mate_ref[at, :].astype(jnp.float32)
        out_ref[at, :] = jnp.where(wants_mate, mate, own).astype(out_ref.dtype)

    by_rows(out_ref, body)


def pick(choices, own, mate, after):
    return call(pick_kernel, "pick", half_array(*own.shape), [VMEM, VMEM, VMEM, ANY], VMEM)(
        choices, own, mate, after
    )


def partial_kernel(n, scale, parts, order, where_ref, context_ref, cotangent_ref, *refs):
    outs, (context, cotangent, product, rounded, sems, out_sems) = refs[:-6], refs[-6:]
    width = product.shape[0]
    rows = width // n
    me = where_ref[0]
    even = lax.rem(me, 2) == 0
    tile = min(256, width)
    tokens = context.shape[0]
    loads = []
    for i, start in enumerate(range(0, tokens, tokens // 4)):
        at = pl.ds(start, tokens // 4)
        loads.append(pltpu.make_async_copy(cotangent_ref.at[at, :], cotangent.at[at, :], sems.at[i]))
    for i, start in enumerate(range(0, width, tile)):
        at = pl.ds(start, tile)
        loads.append(pltpu.make_async_copy(context_ref.at[:, at], context.at[:, at], sems.at[4 + i]))
    for load in loads:
        load.start()
    rounded[width:, :] = jnp.zeros((rows, rounded.shape[1]), rounded.dtype)
    for load in loads[:4]:
        load.wait()
    for i, start in enumerate(range(0, width, tile)):
        loads[4 + i].wait()
        block = scale * lax.dot_general(
            context[:, start:start + tile], cotangent[...],
            (((0,), (0,)), ((), ())), preferred_element_type=jnp.float32,
        )
        product[start:start + tile, :] = block
        rounded[start:start + tile, :] = block.astype(rounded.dtype)
    writes = []

    def write(source, first_row, size):
        at = len(writes)
        writes.append(pltpu.make_async_copy(
            source.at[pl.ds(pl.multiple_of(first_row, 16), size), :], outs[at], out_sems.at[at]
        ))
        writes[-1].start()

    for slot, swap in order:
        rightward = even if swap == 0 else jnp.logical_not(even)
        block = lax.rem(me + jnp.where(rightward, n + 1 - slot, slot - 1), n)
        place = jnp.where(rightward, me, n - 1 - me)
        first_row = jnp.where(place >= slot - 1, width, block * rows)
        for start, size in parts:
            write(rounded, first_row + start, size)
    for start, size in parts:
        write(product, me * rows + start, size)
    for copy in writes:
        copy.wait()


def partial_blocks(n, scale, parts, order, where, context_rows, cotangent):
    tokens, width = context_rows.shape
    depth = cotangent.shape[1]
    outs = (len(order) + 1) * len(parts)
    flat = call(
        functools.partial(partial_kernel, n, scale, parts, order), "partial_blocks",
        [half_array(size, depth) for _, size in parts] * len(order)
        + [jax.ShapeDtypeStruct((size, depth), jnp.float32) for _, size in parts],
        [SMEM, HBM, HBM], [HBM] * outs, limit=14,
        scratch=[
            pltpu.VMEM(context_rows.shape, context_rows.dtype),
            pltpu.VMEM(cotangent.shape, cotangent.dtype),
            pltpu.VMEM((width, depth), jnp.float32),
            pltpu.VMEM((width + width // n, depth), jnp.bfloat16),
            pltpu.SemaphoreType.DMA((4 + width // min(256, width),)),
            pltpu.SemaphoreType.DMA((outs,)),
        ],
    )(where, context_rows, cotangent)
    return [flat[k * len(parts):(k + 1) * len(parts)] for k in range(len(order) + 1)]


def sum_kernel(arrived_ref, term_ref, after_ref, out_ref):
    def body(at):
        total = arrived_ref[at, :].astype(jnp.float32) + term_ref[at, :].astype(jnp.float32)
        out_ref[at, :] = total.astype(out_ref.dtype)

    by_rows(out_ref, body)


def grad_kernel(own_ref, one_ref, other_ref, after_ref, out_ref):
    def body(at):
        arrived = one_ref[at, :].astype(jnp.float32) + other_ref[at, :].astype(jnp.float32)
        out_ref[at, :] = (own_ref[at, :] + arrived).astype(out_ref.dtype)

    by_rows(out_ref, body)


def summed(kernel, name, addends, after):
    return call(kernel, name, half_array(*addends[0].shape), [VMEM] * len(addends) + [ANY], VMEM)(
        *addends, after
    )


def columns_kernel(n, scale, parts, where_ref, cotangent_ref, after_ref, *refs):
    blocks, (out_ref, token_ref, full, result, out_sems) = refs[:-5], refs[-5:]
    token_ref[...] = jnp.zeros_like(token_ref)
    width = full.shape[0]
    rows = width // n
    me = where_ref[0]
    even = lax.rem(me, 2) == 0
    for k in range(2 * n - 1):
        slot, swap = (k + 1) // 2, (k + 1) % 2
        shard = me + (jnp.where(even, slot, -slot) if swap == 0 else jnp.where(even, -slot, slot))

        @pl.when(jnp.logical_and(shard >= 0, shard < n))
        def _():
            for c, (start, size) in enumerate(parts):
                first_row = pl.multiple_of(shard * rows + start, 16)
                full[pl.ds(first_row, size), :] = blocks[k * len(parts) + c][...]
    tile = min(256, width)
    writes = []
    for i, start in enumerate(range(0, width, tile)):
        result[:, start:start + tile] = (scale * lax.dot_general(
            cotangent_ref[...], full[start:start + tile, :],
            (((1,), (1,)), ((), ())), preferred_element_type=jnp.float32,
        )).astype(out_ref.dtype)
        at = pl.ds(start, tile)
        writes.append(pltpu.make_async_copy(result.at[:, at], out_ref.at[:, at], out_sems.at[i]))
        writes[-1].start()
    for write in writes:
        write.wait()


def columns(n, scale, parts, where, cotangent, after, blocks):
    tokens, depth = cotangent.shape
    width = n * sum(size for _, size in parts)
    return call(
        functools.partial(columns_kernel, n, scale, parts), "context_grad",
        [half_array(tokens, width), jax.ShapeDtypeStruct((8, 128), jnp.float32)],
        [SMEM, VMEM, ANY] + [VMEM] * len(blocks), [HBM, VMEM], limit=14,
        scratch=[
            pltpu.VMEM((width, depth), cotangent.dtype),
            pltpu.VMEM((tokens, width), cotangent.dtype),
            pltpu.SemaphoreType.DMA((width // min(256, width),)),
        ],
    )(where, cotangent, after, *blocks)


def state_kernel(parts, where_ref, donor_ref, *refs):
    own, (mate_ref, across_ref), refs = refs[:3], refs[3:5], refs[5:]
    outs, (taken, sems) = refs[:-2], refs[-2:]
    rows = own[0].shape[0]
    member = where_ref[1]
    way = jnp.bitwise_xor(source_of(member, donor_ref), member)

    @pl.when(way == 0)
    def _():
        copies = []
        for c, (start, size) in enumerate(parts):
            for k in range(3):
                copies.append(pltpu.make_async_copy(
                    own[k].at[pl.ds(start, size), :], outs[c].at[pl.ds(k * size, size), :], sems.at[c * 3 + k]
                ))
                copies[-1].start()
        for copy in copies:
            copy.wait()

    def widen(ref):
        copies = []
        for k in range(3):
            at = pl.ds(k * rows, rows)
            copies.append(pltpu.make_async_copy(ref.at[at, :], taken.at[at, :], sems.at[k]))
            copies[-1].start()
        for k in range(3):
            copies[k].wait()
            for c, (start, size) in enumerate(parts):
                first_row = k * rows + start
                outs[c][k * size:(k + 1) * size, :] = taken[first_row:first_row + size, :].astype(jnp.float32)

    pl.when(way == 1)(lambda: widen(mate_ref))
    pl.when(way > 1)(lambda: widen(across_ref))


def taken_state(parts, where, donor, own, donated):
    rows, depth = own[0].shape
    return call(
        functools.partial(state_kernel, parts), "taken_state",
        [jax.ShapeDtypeStruct((3 * size, depth), jnp.float32) for _, size in parts],
        [SMEM, SMEM] + [HBM] * 3 + [ANY] * 2, [VMEM] * len(parts),
        scratch=[pltpu.VMEM((3 * rows, depth), jnp.bfloat16), pltpu.SemaphoreType.DMA((3 * len(parts),))],
    )(where, donor, *own, *donated)


def adam_kernel(start, size, filled, choices_ref, state_ref, grad_ref, mate_ref, across_ref, *refs):
    refs = refs[3 if filled else 0:]
    outs, (stepped, sems) = refs[:3], refs[3:]
    depth = grad_ref.shape[1]
    pieces = 4 if size % 64 == 0 else 1
    piece = size // pieces
    writes = []
    for p in range(pieces):
        def body(i):
            at = pl.ds(pl.multiple_of(p * piece + i * 16, 16), 16)
            row = lambda k: jnp.broadcast_to(choices_ref[k:k + 1, :], (16, depth))
            load = lambda k: state_ref[pl.ds(pl.multiple_of(k * size + p * piece + i * 16, 16), 16), :]
            g = jnp.where(
                row(1) > 0, grad_ref[at, :].astype(jnp.float32),
                jnp.where(row(2) > 0, mate_ref[at, :].astype(jnp.float32), across_ref[at, :].astype(jnp.float32)),
            )
            w = load(0)
            first_step = beta_one * load(1) + (1.0 - beta_one) * g
            second_step = beta_two * load(2) + (1.0 - beta_two) * g * g
            ratio = (first_step * row(6)) / (jnp.sqrt(second_step * row(7)) + epsilon)
            stepped[0, at, :] = w - row(4) * (ratio + row(5) * w)
            stepped[1, at, :] = first_step
            stepped[2, at, :] = second_step

        pl.loop(0, piece // 16)(body)
        for k in range(3):
            writes.append(pltpu.make_async_copy(
                stepped.at[k, pl.ds(p * piece, piece), :],
                outs[k].at[pl.ds(start + p * piece, piece), :], sems.at[p * 3 + k],
            ))
            writes[-1].start()
    for write in writes:
        write.wait()


def adam_update(start, size, rows, choices, state, grads, filled):
    depth = state.shape[1]
    return call(
        functools.partial(adam_kernel, start, size, bool(filled)), "adam",
        [jax.ShapeDtypeStruct((rows, depth), jnp.float32)] * 3,
        [VMEM] * 5 + [HBM] * len(filled), [HBM] * 3,
        scratch=[pltpu.VMEM((3, size, depth), jnp.float32), pltpu.SemaphoreType.DMA((12,))],
        aliases={5 + k: k for k in range(len(filled))},
    )(choices, state, *grads, *filled)


def on_device(n, members, context, out_grad, weight, first, second, rates, decays, steps, donor):
    context_rows = context[0]
    cotangent = out_grad[0]
    scale = context_rows.shape[1] ** (-0.5)
    rows, depth = weight.shape[1:]
    chains = 2 if rows % 32 == 0 else 1
    parts = [(c * rows // chains, rows // chains) for c in range(chains)]
    where = jnp.stack([lax.axis_index("shard"), lax.axis_index("member")]).astype(jnp.int32)

    swap_across = [(m, m ^ 2) for m in range(members)]
    swap_mates = [(m, m ^ 1) for m in range(members)]
    swaps = []
    for swap in range(2):
        pairs = [(s, s + 1) for s in range(swap, n - 1, 2)]
        swaps.append(pairs + [(b, a) for a, b in pairs])

    state, *own = halves(parts, weight[0], first[0], second[0])
    choices = call(
        choices_kernel, "choices", jax.ShapeDtypeStruct((8, depth), jnp.float32), [SMEM] * 5, VMEM
    )(where, rates, decays, steps, donor)
    order = [(slot, swap) for slot in range(2, n + 1) for swap in range(2)]
    terms = partial_blocks(n, scale, parts, order, where, context_rows, cotangent)

    arrived = [[own, own]]
    sent = early = own[0]
    for slot in range(1, n + 1):
        now = [[], []]
        for c in range(len(parts)):
            for swap in range(2):
                block = arrived[-1][1 - swap][c]
                if slot > 1:
                    addends = (block, terms[2 * (slot - 2) + swap][c])
                    block = sent = summed(sum_kernel, "to_send", addends, sent)
                if slot == 2 and c == 0:
                    early = block
                now[swap].append(lax.ppermute(block, "shard", swaps[swap]))
        arrived.append(now)

    def from_members(held, after):
        mate = lax.ppermute(held, "member", swap_mates)
        return mate, lax.ppermute(pick(choices, held, mate, after), "member", swap_across)

    states = taken_state(
        parts, where, donor, (weight[0], first[0], second[0]), from_members(state, early)
    )
    blocks = list(own)
    for slot in range(1, n):
        blocks += arrived[slot][0] + arrived[slot][1]
    context_grad, sent = columns(n, scale, parts, where, cotangent, sent, blocks)

    grads = []
    for c in range(len(parts)):
        addends = (terms[-1][c], arrived[n][0][c], arrived[n][1][c])
        sent = summed(grad_kernel, "summed_grad", addends, sent)
        grads.append(sent)

    updated = ()
    for (start, size), held, grad in zip(parts, states, grads):
        updated = adam_update(
            start, size, rows, choices, held, (grad,) + from_members(grad, grad), updated
        )
    return (context_grad[None],) + tuple(array[None] for array in updated)


def solution(mesh):
    whole = P(("groups", "member"), "shard", None)
    n, members = mesh.shape["shard"], mesh.shape["member"]
    return jax.shard_map(
        functools.partial(on_device, n, members),
        mesh=mesh,
        in_specs=(whole,) * 5 + (P("groups"),) * 4,
        out_specs=(whole,) * 4,
        check_vma=False,
    )
```

```python
import functools
import math

import jax
import jax.numpy as jnp
from jax import lax
from jax.experimental import pallas as pl
from jax.experimental.pallas import tpu as pltpu
from jax.sharding import PartitionSpec as P

beta_one = 0.9
beta_two = 0.999
epsilon = 1e-08

MIB = 1 << 20
SMEM = pl.BlockSpec(memory_space=pltpu.SMEM)
VMEM = pl.BlockSpec(memory_space=pltpu.VMEM)
HBM = pl.BlockSpec(memory_space=pltpu.HBM)
ANY = pl.BlockSpec(memory_space=pl.ANY)


def call(kernel, name, out_shape, in_specs, out_specs, limit=8, scratch=(), aliases=None):
    return pl.pallas_call(
        kernel,
        out_shape=out_shape,
        in_specs=in_specs,
        out_specs=out_specs,
        scratch_shapes=scratch,
        input_output_aliases=aliases or {},
        compiler_params=pltpu.CompilerParams(vmem_limit_bytes=limit * MIB),
        cost_estimate=pl.CostEstimate(flops=0, bytes_accessed=1024, transcendentals=0),
        name=name,
    )


def half_array(rows, depth):
    return jax.ShapeDtypeStruct((rows, depth), jnp.bfloat16)


def gate_kernel(value_ref, after_ref, out_ref):
    pass


def gate(value, after):
    return call(gate_kernel, "gate", half_array(*value.shape), [ANY, ANY], ANY, aliases={0: 0})(value, after)


def by_rows(ref, body, step=16):
    @pl.loop(0, ref.shape[0] // step)
    def _(i):
        body(pl.ds(pl.multiple_of(i * step, step), step))


def source_of(member, donor_ref):
    donor = donor_ref[member]
    return jnp.where(donor >= 0, donor, member)


def choices_kernel(where_ref, rates_ref, decays_ref, steps_ref, donor_ref, out_ref):
    member = where_ref[1]
    source = source_of(member, donor_ref)
    way = jnp.bitwise_xor(source, member)
    partner_source = source_of(jnp.bitwise_xor(member, 2), donor_ref)
    flags = [partner_source == jnp.bitwise_xor(member, 1), way == 0, way == 1, way == 2]
    depth = out_ref.shape[1]
    for k, flag in enumerate(flags):
        out_ref[k:k + 1, :] = jnp.full((1, depth), jnp.where(flag, 1.0, 0.0))
    out_ref[4:5, :] = jnp.full((1, depth), rates_ref[source])
    out_ref[5:6, :] = jnp.full((1, depth), decays_ref[source])
    count = jnp.full((1, depth), (steps_ref[source] + 1).astype(jnp.float32))
    out_ref[6:7, :] = 1.0 / (1.0 - jnp.exp(count * math.log(beta_one)))
    out_ref[7:8, :] = 1.0 / (1.0 - jnp.exp(count * math.log(beta_two)))


def halves_kernel(parts, weight_ref, first_ref, second_ref, state_ref, *refs):
    own_refs, (full, sems) = refs[:-2], refs[-2:]
    rows = weight_ref.shape[0]
    copies = []
    for k, ref in enumerate((weight_ref, first_ref, second_ref)):
        for c, (start, size) in enumerate(parts):
            copies.append(pltpu.make_async_copy(
                ref.at[pl.ds(start, size), :], full.at[k, pl.ds(start, size), :], sems.at[k * len(parts) + c]
            ))
            copies[-1].start()
    for k in range(3):
        for c, (start, size) in enumerate(parts):
            copies[k * len(parts) + c].wait()
            rounded = full[k, start:start + size, :].astype(jnp.bfloat16)
            if k == 0:
                own_refs[c][...] = rounded
            state_ref[k * rows + start:k * rows + start + size, :] = rounded


def halves(parts, weight, first, second):
    rows, depth = weight.shape
    sizes = [3 * rows] + [size for _, size in parts]
    return call(
        functools.partial(halves_kernel, parts), "halves",
        [half_array(size, depth) for size in sizes], [HBM] * 3, [VMEM] * len(sizes), limit=56,
        scratch=[pltpu.VMEM((3, rows, depth), jnp.float32), pltpu.SemaphoreType.DMA((3 * len(parts),))],
    )(weight, first, second)


def pick_kernel(choices_ref, own_ref, mate_ref, after_ref, out_ref):
    def body(at):
        wants_mate = jnp.broadcast_to(choices_ref[0:1, :], (16, out_ref.shape[1])) > 0
        own, mate = own_ref[at, :].astype(jnp.float32), mate_ref[at, :].astype(jnp.float32)
        out_ref[at, :] = jnp.where(wants_mate, mate, own).astype(out_ref.dtype)

    by_rows(out_ref, body)


def pick(choices, own, mate, after):
    return call(pick_kernel, "pick", half_array(*own.shape), [VMEM, VMEM, VMEM, ANY], VMEM)(
        choices, own, mate, after
    )


def partial_kernel(n, scale, parts, order, where_ref, context_ref, cotangent_ref, *refs):
    outs, (context, cotangent, product, rounded, sems, out_sems) = refs[:-6], refs[-6:]
    width = product.shape[0]
    rows = width // n
    me = where_ref[0]
    even = lax.rem(me, 2) == 0
    tile = min(256, width)
    tokens = context.shape[0]
    loads = []
    for i, start in enumerate(range(0, tokens, tokens // 4)):
        at = pl.ds(start, tokens // 4)
        loads.append(pltpu.make_async_copy(cotangent_ref.at[at, :], cotangent.at[at, :], sems.at[i]))
    for i, start in enumerate(range(0, width, tile)):
        at = pl.ds(start, tile)
        loads.append(pltpu.make_async_copy(context_ref.at[:, at], context.at[:, at], sems.at[4 + i]))
    for load in loads:
        load.start()
    rounded[width:, :] = jnp.zeros((rows, rounded.shape[1]), rounded.dtype)
    for load in loads[:4]:
        load.wait()
    for i, start in enumerate(range(0, width, tile)):
        loads[4 + i].wait()
        block = scale * lax.dot_general(
            context[:, start:start + tile], cotangent[...],
            (((0,), (0,)), ((), ())), preferred_element_type=jnp.float32,
        )
        product[start:start + tile, :] = block
        rounded[start:start + tile, :] = block.astype(rounded.dtype)
    writes = []

    def write(source, first_row, size):
        at = len(writes)
        writes.append(pltpu.make_async_copy(
            source.at[pl.ds(pl.multiple_of(first_row, 16), size), :], outs[at], out_sems.at[at]
        ))
        writes[-1].start()

    for slot, swap in order:
        rightward = even if swap == 0 else jnp.logical_not(even)
        block = lax.rem(me + jnp.where(rightward, n + 1 - slot, slot - 1), n)
        place = jnp.where(rightward, me, n - 1 - me)
        first_row = jnp.where(place >= slot - 1, width, block * rows)
        for start, size in parts:
            write(rounded, first_row + start, size)
    for start, size in parts:
        write(product, me * rows + start, size)
    for copy in writes:
        copy.wait()


def partial_blocks(n, scale, parts, order, where, context_rows, cotangent):
    tokens, width = context_rows.shape
    depth = cotangent.shape[1]
    outs = (len(order) + 1) * len(parts)
    flat = call(
        functools.partial(partial_kernel, n, scale, parts, order), "partial_blocks",
        [half_array(size, depth) for _, size in parts] * len(order)
        + [jax.ShapeDtypeStruct((size, depth), jnp.float32) for _, size in parts],
        [SMEM, HBM, HBM], [HBM] * outs, limit=14,
        scratch=[
            pltpu.VMEM(context_rows.shape, context_rows.dtype),
            pltpu.VMEM(cotangent.shape, cotangent.dtype),
            pltpu.VMEM((width, depth), jnp.float32),
            pltpu.VMEM((width + width // n, depth), jnp.bfloat16),
            pltpu.SemaphoreType.DMA((4 + width // min(256, width),)),
            pltpu.SemaphoreType.DMA((outs,)),
        ],
    )(where, context_rows, cotangent)
    return [flat[k * len(parts):(k + 1) * len(parts)] for k in range(len(order) + 1)]


def sum_kernel(arrived_ref, term_ref, after_ref, out_ref):
    def body(at):
        total = arrived_ref[at, :].astype(jnp.float32) + term_ref[at, :].astype(jnp.float32)
        out_ref[at, :] = total.astype(out_ref.dtype)

    by_rows(out_ref, body)


def grad_kernel(own_ref, one_ref, other_ref, after_ref, out_ref):
    def body(at):
        arrived = one_ref[at, :].astype(jnp.float32) + other_ref[at, :].astype(jnp.float32)
        out_ref[at, :] = (own_ref[at, :] + arrived).astype(out_ref.dtype)

    by_rows(out_ref, body)


def summed(kernel, name, addends, after):
    return call(
        kernel, name, half_array(*addends[0].shape), [VMEM] * len(addends) + [ANY], VMEM
    )(*addends, after)


def columns_kernel(n, scale, parts, where_ref, cotangent_ref, after_ref, *refs):
    blocks, (out_ref, token_ref, full, result, out_sems) = refs[:-5], refs[-5:]
    token_ref[...] = jnp.zeros_like(token_ref)
    width = full.shape[0]
    rows = width // n
    me = where_ref[0]
    even = lax.rem(me, 2) == 0
    for k in range(2 * n - 1):
        slot, swap = (k + 1) // 2, (k + 1) % 2
        shard = me + (jnp.where(even, slot, -slot) if swap == 0 else jnp.where(even, -slot, slot))

        @pl.when(jnp.logical_and(shard >= 0, shard < n))
        def _():
            for c, (start, size) in enumerate(parts):
                first_row = pl.multiple_of(shard * rows + start, 16)
                full[pl.ds(first_row, size), :] = blocks[k * len(parts) + c][...]
    tile = min(256, width)
    writes = []
    for i, start in enumerate(range(0, width, tile)):
        result[:, start:start + tile] = (scale * lax.dot_general(
            cotangent_ref[...], full[start:start + tile, :],
            (((1,), (1,)), ((), ())), preferred_element_type=jnp.float32,
        )).astype(out_ref.dtype)
        at = pl.ds(start, tile)
        writes.append(pltpu.make_async_copy(result.at[:, at], out_ref.at[:, at], out_sems.at[i]))
        writes[-1].start()
    for write in writes:
        write.wait()


def columns(n, scale, parts, where, cotangent, after, blocks):
    tokens, depth = cotangent.shape
    width = n * sum(size for _, size in parts)
    return call(
        functools.partial(columns_kernel, n, scale, parts), "context_grad",
        [half_array(tokens, width), jax.ShapeDtypeStruct((8, 128), jnp.float32)],
        [SMEM, VMEM, ANY] + [VMEM] * len(blocks), [HBM, VMEM], limit=14,
        scratch=[
            pltpu.VMEM((width, depth), cotangent.dtype),
            pltpu.VMEM((tokens, width), cotangent.dtype),
            pltpu.SemaphoreType.DMA((width // min(256, width),)),
        ],
    )(where, cotangent, after, *blocks)


def state_kernel(parts, where_ref, donor_ref, after_ref, *refs):
    own, (mate_ref, across_ref), refs = refs[:3], refs[3:5], refs[5:]
    outs, (taken, sems) = refs[:-2], refs[-2:]
    rows = own[0].shape[0]
    member = where_ref[1]
    way = jnp.bitwise_xor(source_of(member, donor_ref), member)

    @pl.when(way == 0)
    def _():
        copies = []
        for c, (start, size) in enumerate(parts):
            for k in range(3):
                copies.append(pltpu.make_async_copy(
                    own[k].at[pl.ds(start, size), :], outs[c].at[pl.ds(k * size, size), :], sems.at[c * 3 + k]
                ))
                copies[-1].start()
        for copy in copies:
            copy.wait()

    def widen(ref):
        copies = []
        for k in range(3):
            at = pl.ds(k * rows, rows)
            copies.append(pltpu.make_async_copy(ref.at[at, :], taken.at[at, :], sems.at[k]))
            copies[-1].start()
        for k in range(3):
            copies[k].wait()
            for c, (start, size) in enumerate(parts):
                first_row = k * rows + start
                outs[c][k * size:(k + 1) * size, :] = taken[first_row:first_row + size, :].astype(jnp.float32)

    pl.when(way == 1)(lambda: widen(mate_ref))
    pl.when(way > 1)(lambda: widen(across_ref))


def taken_state(parts, where, donor, own, donated, after):
    rows, depth = own[0].shape
    return call(
        functools.partial(state_kernel, parts), "taken_state",
        [jax.ShapeDtypeStruct((3 * size, depth), jnp.float32) for _, size in parts],
        [SMEM, SMEM, ANY] + [HBM] * 3 + [ANY] * 2, [VMEM] * len(parts),
        scratch=[pltpu.VMEM((3 * rows, depth), jnp.bfloat16), pltpu.SemaphoreType.DMA((3 * len(parts),))],
    )(where, donor, after, *own, *donated)


def adam_kernel(start, size, filled, choices_ref, state_ref, own_ref, mate_ref, across_ref, far_ref, after_ref, *refs):
    refs = refs[3 if filled else 0:]
    outs, (stepped, sems) = refs[:3], refs[3:]
    depth = own_ref.shape[1]
    pieces = 4 if size % 64 == 0 else 1
    piece = size // pieces
    writes = []
    for p in range(pieces):
        def body(i):
            at = pl.ds(pl.multiple_of(p * piece + i * 16, 16), 16)
            row = lambda k: jnp.broadcast_to(choices_ref[k:k + 1, :], (16, depth))
            load = lambda k: state_ref[pl.ds(pl.multiple_of(k * size + p * piece + i * 16, 16), 16), :]
            g = far_ref[at, :].astype(jnp.float32)
            for k, ref in ((1, own_ref), (2, mate_ref), (3, across_ref)):
                g = jnp.where(row(k) > 0, ref[at, :].astype(jnp.float32), g)
            w = load(0)
            first_step = beta_one * load(1) + (1.0 - beta_one) * g
            second_step = beta_two * load(2) + (1.0 - beta_two) * g * g
            ratio = (first_step * row(6)) / (jnp.sqrt(second_step * row(7)) + epsilon)
            stepped[0, at, :] = w - row(4) * (ratio + row(5) * w)
            stepped[1, at, :] = first_step
            stepped[2, at, :] = second_step

        pl.loop(0, piece // 16)(body)
        for k in range(3):
            writes.append(pltpu.make_async_copy(
                stepped.at[k, pl.ds(p * piece, piece), :],
                outs[k].at[pl.ds(start + p * piece, piece), :], sems.at[p * 3 + k],
            ))
            writes[-1].start()
    for write in writes:
        write.wait()


def adam_update(start, size, rows, choices, state, grads, after, filled):
    depth = state.shape[1]
    return call(
        functools.partial(adam_kernel, start, size, bool(filled)), "adam",
        [jax.ShapeDtypeStruct((rows, depth), jnp.float32)] * 3,
        [VMEM] * 6 + [ANY] + [HBM] * len(filled), [HBM] * 3,
        scratch=[pltpu.VMEM((3, size, depth), jnp.float32), pltpu.SemaphoreType.DMA((12,))],
        aliases={7 + k: k for k in range(len(filled))},
    )(choices, state, *grads, after, *filled)


def on_device(n, members, context, out_grad, weight, first, second, rates, decays, steps, donor):
    context_rows = context[0]
    cotangent = out_grad[0]
    scale = context_rows.shape[1] ** (-0.5)
    rows, depth = weight.shape[1:]
    chains = 2 if rows % 32 == 0 else 1
    parts = [(c * rows // chains, rows // chains) for c in range(chains)]
    where = jnp.stack([lax.axis_index("shard"), lax.axis_index("member")]).astype(jnp.int32)

    swap_across = [(m, m ^ 2) for m in range(members)]
    swap_mates = [(m, m ^ 1) for m in range(members)]
    swaps = []
    for swap in range(2):
        pairs = [(s, s + 1) for s in range(swap, n - 1, 2)]
        swaps.append(pairs + [(b, a) for a, b in pairs])

    state, *own = halves(parts, weight[0], first[0], second[0])
    choices = call(
        choices_kernel, "choices", jax.ShapeDtypeStruct((8, depth), jnp.float32), [SMEM] * 5, VMEM
    )(where, rates, decays, steps, donor)
    order = [(slot, swap) for slot in range(2, n + 1) for swap in range(2)]
    terms = partial_blocks(n, scale, parts, order, where, context_rows, cotangent)

    arrived = [[own, own]]
    sent = early = own[0]
    for slot in range(1, n + 1):
        now = [[], []]
        for c in range(len(parts)):
            for swap in range(2):
                block = arrived[-1][1 - swap][c]
                if slot > 1:
                    addends = (block, terms[2 * (slot - 2) + swap][c])
                    block = sent = summed(sum_kernel, "to_send", addends, sent)
                if slot == 2 and c == 0:
                    early = block
                now[swap].append(lax.ppermute(block, "shard", swaps[swap]))
        arrived.append(now)

    mate = lax.ppermute(state, "member", swap_mates)
    across = lax.ppermute(pick(choices, state, mate, early), "member", swap_across)
    states = taken_state(parts, where, donor, (weight[0], first[0], second[0]), (mate, across), sent)

    grads = []
    for c in range(len(parts)):
        addends = (terms[-1][c], arrived[n][0][c], arrived[n][1][c])
        sent = summed(grad_kernel, "summed_grad", addends, sent)
        grads.append(sent)
    blocks = list(own)
    for slot in range(1, n):
        blocks += arrived[slot][0] + arrived[slot][1]
    context_grad, computed = columns(n, scale, parts, where, cotangent, sent, blocks)

    updated = ()
    for c, (start, size) in enumerate(parts):
        mate = lax.ppermute(grads[c], "member", swap_mates)
        across = lax.ppermute(grads[c], "member", swap_across)
        if c == 0:
            across = gate(across, computed)
        far = lax.ppermute(across, "member", swap_mates)
        updated = adam_update(
            start, size, rows, choices, states[c], (grads[c], mate, across, far), computed, updated
        )
    return (context_grad[None],) + tuple(array[None] for array in updated)


def solution(mesh):
    whole = P(("groups", "member"), "shard", None)
    n, members = mesh.shape["shard"], mesh.shape["member"]
    return jax.shard_map(
        functools.partial(on_device, n, members),
        mesh=mesh,
        in_specs=(whole,) * 5 + (P("groups"),) * 4,
        out_specs=(whole,) * 4,
        check_vma=False,
    )
```

```python
import functools
import math

import jax
import jax.numpy as jnp
from jax import lax
from jax.experimental import pallas as pl
from jax.experimental.pallas import tpu as pltpu
from jax.sharding import PartitionSpec as P

beta_one = 0.9
beta_two = 0.999
epsilon = 1e-08

MIB = 1 << 20
SUM_FLOPS = 2 ** 30
SMEM = pl.BlockSpec(memory_space=pltpu.SMEM)
VMEM = pl.BlockSpec(memory_space=pltpu.VMEM)
HBM = pl.BlockSpec(memory_space=pltpu.HBM)
ANY = pl.BlockSpec(memory_space=pl.ANY)


def call(kernel, name, out_shape, in_specs, out_specs, limit=8, scratch=(), aliases=None, flops=0):
    return pl.pallas_call(
        kernel,
        out_shape=out_shape,
        in_specs=in_specs,
        out_specs=out_specs,
        scratch_shapes=scratch,
        input_output_aliases=aliases or {},
        compiler_params=pltpu.CompilerParams(vmem_limit_bytes=limit * MIB),
        cost_estimate=pl.CostEstimate(flops=flops, bytes_accessed=1024, transcendentals=0),
        name=name,
    )


def half_array(rows, depth):
    return jax.ShapeDtypeStruct((rows, depth), jnp.bfloat16)


def by_rows(ref, body, step=16):
    @pl.loop(0, ref.shape[0] // step)
    def _(i):
        body(pl.ds(pl.multiple_of(i * step, step), step))


def source_of(member, donor_ref):
    donor = donor_ref[member]
    return jnp.where(donor >= 0, donor, member)


def choices_kernel(where_ref, rates_ref, decays_ref, steps_ref, donor_ref, out_ref):
    member = where_ref[1]
    source = source_of(member, donor_ref)
    way = jnp.bitwise_xor(source, member)
    partner_source = source_of(jnp.bitwise_xor(member, 2), donor_ref)
    flags = [partner_source == jnp.bitwise_xor(member, 1), way == 0, way == 1, way == 2]
    depth = out_ref.shape[1]
    for k, flag in enumerate(flags):
        out_ref[k:k + 1, :] = jnp.full((1, depth), jnp.where(flag, 1.0, 0.0))
    out_ref[4:5, :] = jnp.full((1, depth), rates_ref[source])
    out_ref[5:6, :] = jnp.full((1, depth), decays_ref[source])
    count = jnp.full((1, depth), (steps_ref[source] + 1).astype(jnp.float32))
    out_ref[6:7, :] = 1.0 / (1.0 - jnp.exp(count * math.log(beta_one)))
    out_ref[7:8, :] = 1.0 / (1.0 - jnp.exp(count * math.log(beta_two)))


def halves_kernel(parts, weight_ref, first_ref, second_ref, state_ref, *refs):
    own_refs, (full, sems) = refs[:-2], refs[-2:]
    rows = weight_ref.shape[0]
    copies = []
    for k, ref in enumerate((weight_ref, first_ref, second_ref)):
        for c, (start, size) in enumerate(parts):
            copies.append(pltpu.make_async_copy(
                ref.at[pl.ds(start, size), :], full.at[k, pl.ds(start, size), :], sems.at[k * len(parts) + c]
            ))
            copies[-1].start()
    for k in range(3):
        for c, (start, size) in enumerate(parts):
            copies[k * len(parts) + c].wait()
            rounded = full[k, start:start + size, :].astype(jnp.bfloat16)
            if k == 0:
                own_refs[c][...] = rounded
            state_ref[k * rows + start:k * rows + start + size, :] = rounded


def halves(parts, weight, first, second):
    rows, depth = weight.shape
    sizes = [3 * rows] + [size for _, size in parts]
    return call(
        functools.partial(halves_kernel, parts), "halves",
        [half_array(size, depth) for size in sizes], [HBM] * 3, [VMEM] * len(sizes), limit=56,
        scratch=[pltpu.VMEM((3, rows, depth), jnp.float32), pltpu.SemaphoreType.DMA((3 * len(parts),))],
    )(weight, first, second)


def pick_kernel(choices_ref, own_ref, mate_ref, after_ref, out_ref):
    def body(at):
        wants_mate = jnp.broadcast_to(choices_ref[0:1, :], (16, out_ref.shape[1])) > 0
        own, mate = own_ref[at, :].astype(jnp.float32), mate_ref[at, :].astype(jnp.float32)
        out_ref[at, :] = jnp.where(wants_mate, mate, own).astype(out_ref.dtype)

    by_rows(out_ref, body)


def pick(choices, own, mate, after):
    return call(pick_kernel, "pick", half_array(*own.shape), [VMEM, VMEM, VMEM, ANY], VMEM)(
        choices, own, mate, after
    )


def partial_kernel(n, scale, parts, order, where_ref, context_ref, cotangent_ref, *refs):
    outs, (context, cotangent, product, rounded, sems, out_sems) = refs[:-6], refs[-6:]
    width = product.shape[0]
    rows = width // n
    me = where_ref[0]
    even = lax.rem(me, 2) == 0
    tile = min(256, width)
    tokens = context.shape[0]
    loads = []
    for i, start in enumerate(range(0, tokens, tokens // 4)):
        at = pl.ds(start, tokens // 4)
        loads.append(pltpu.make_async_copy(cotangent_ref.at[at, :], cotangent.at[at, :], sems.at[i]))
    for i, start in enumerate(range(0, width, tile)):
        at = pl.ds(start, tile)
        loads.append(pltpu.make_async_copy(context_ref.at[:, at], context.at[:, at], sems.at[4 + i]))
    for load in loads:
        load.start()
    rounded[width:, :] = jnp.zeros((rows, rounded.shape[1]), rounded.dtype)
    for load in loads[:4]:
        load.wait()
    for i, start in enumerate(range(0, width, tile)):
        loads[4 + i].wait()
        block = scale * lax.dot_general(
            context[:, start:start + tile], cotangent[...],
            (((0,), (0,)), ((), ())), preferred_element_type=jnp.float32,
        )
        product[start:start + tile, :] = block
        rounded[start:start + tile, :] = block.astype(rounded.dtype)
    writes = []

    def write(source, first_row, size):
        at = len(writes)
        writes.append(pltpu.make_async_copy(
            source.at[pl.ds(pl.multiple_of(first_row, 16), size), :], outs[at], out_sems.at[at]
        ))
        writes[-1].start()

    for slot, swap in order:
        rightward = even if swap == 0 else jnp.logical_not(even)
        block = lax.rem(me + jnp.where(rightward, n + 1 - slot, slot - 1), n)
        place = jnp.where(rightward, me, n - 1 - me)
        first_row = jnp.where(place >= slot - 1, width, block * rows)
        for start, size in parts:
            write(rounded, first_row + start, size)
    for start, size in parts:
        write(product, me * rows + start, size)
    for copy in writes:
        copy.wait()


def partial_blocks(n, scale, parts, order, where, context_rows, cotangent):
    tokens, width = context_rows.shape
    depth = cotangent.shape[1]
    outs = (len(order) + 1) * len(parts)
    flat = call(
        functools.partial(partial_kernel, n, scale, parts, order), "partial_blocks",
        [half_array(size, depth) for _, size in parts] * len(order)
        + [jax.ShapeDtypeStruct((size, depth), jnp.float32) for _, size in parts],
        [SMEM, HBM, HBM], [HBM] * outs, limit=14,
        scratch=[
            pltpu.VMEM(context_rows.shape, context_rows.dtype),
            pltpu.VMEM(cotangent.shape, cotangent.dtype),
            pltpu.VMEM((width, depth), jnp.float32),
            pltpu.VMEM((width + width // n, depth), jnp.bfloat16),
            pltpu.SemaphoreType.DMA((4 + width // min(256, width),)),
            pltpu.SemaphoreType.DMA((outs,)),
        ],
    )(where, context_rows, cotangent)
    return [flat[k * len(parts):(k + 1) * len(parts)] for k in range(len(order) + 1)]


def send_kernel(arrived_ref, term_ref, arrived_too_ref, term_too_ref, after_ref, out_ref, out_too_ref):
    def body(at):
        total = arrived_ref[at, :].astype(jnp.float32) + term_ref[at, :].astype(jnp.float32)
        out_ref[at, :] = total.astype(out_ref.dtype)
        total = arrived_too_ref[at, :].astype(jnp.float32) + term_too_ref[at, :].astype(jnp.float32)
        out_too_ref[at, :] = total.astype(out_too_ref.dtype)

    by_rows(out_ref, body)


def to_send(pairs, after):
    like = half_array(*pairs[0][0].shape)
    return call(send_kernel, "to_send", [like] * 2, [VMEM] * 4 + [ANY], [VMEM] * 2, flops=SUM_FLOPS)(
        *pairs[0], *pairs[1], after
    )


def grad_kernel(own_ref, one_ref, other_ref, after_ref, out_ref):
    def body(at):
        arrived = one_ref[at, :].astype(jnp.float32) + other_ref[at, :].astype(jnp.float32)
        out_ref[at, :] = (own_ref[at, :] + arrived).astype(out_ref.dtype)

    by_rows(out_ref, body)


def summed_grad(own, one, other, after):
    return call(grad_kernel, "summed_grad", half_array(*one.shape), [VMEM] * 3 + [ANY], VMEM)(
        own, one, other, after
    )


def columns_kernel(n, scale, parts, where_ref, cotangent_ref, *refs):
    blocks, (out_ref, full, result, out_sems) = refs[:-4], refs[-4:]
    width = full.shape[0]
    rows = width // n
    me = where_ref[0]
    even = lax.rem(me, 2) == 0
    for k in range(2 * n - 1):
        slot, swap = (k + 1) // 2, (k + 1) % 2
        shard = me + (jnp.where(even, slot, -slot) if swap == 0 else jnp.where(even, -slot, slot))

        @pl.when(jnp.logical_and(shard >= 0, shard < n))
        def _():
            for c, (start, size) in enumerate(parts):
                first_row = pl.multiple_of(shard * rows + start, 16)
                full[pl.ds(first_row, size), :] = blocks[k * len(parts) + c][...]
    tile = min(256, width)
    writes = []
    for i, start in enumerate(range(0, width, tile)):
        result[:, start:start + tile] = (scale * lax.dot_general(
            cotangent_ref[...], full[start:start + tile, :],
            (((1,), (1,)), ((), ())), preferred_element_type=jnp.float32,
        )).astype(out_ref.dtype)
        at = pl.ds(start, tile)
        writes.append(pltpu.make_async_copy(result.at[:, at], out_ref.at[:, at], out_sems.at[i]))
        writes[-1].start()
    for write in writes:
        write.wait()


def columns(n, scale, parts, where, cotangent, blocks):
    tokens, depth = cotangent.shape
    width = n * sum(size for _, size in parts)
    return call(
        functools.partial(columns_kernel, n, scale, parts), "context_grad",
        half_array(tokens, width), [SMEM, VMEM] + [VMEM] * len(blocks), HBM, limit=14,
        scratch=[
            pltpu.VMEM((width, depth), cotangent.dtype),
            pltpu.VMEM((tokens, width), cotangent.dtype),
            pltpu.SemaphoreType.DMA((width // min(256, width),)),
        ],
    )(where, cotangent, *blocks)


def slot_columns_kernel(scale, parts, slot, filled, cotangent_ref, *refs):
    groups = 3 if slot == 1 else 2
    count = groups * len(parts)
    blocks, (out_ref, token_ref, result, sems) = refs[:count], refs[count + filled:]
    token_ref[...] = jnp.zeros_like(token_ref)
    me, n = lax.axis_index("shard"), lax.axis_size("shard")
    rows = sum(size for _, size in parts)
    even = lax.rem(me, 2) == 0
    for group in range(groups):
        ahead = (jnp.where(even, slot, -slot), jnp.where(even, -slot, slot), 0)[group]
        shard = me + ahead

        @pl.when(jnp.logical_and(shard >= 0, shard < n))
        def _():
            writes = []
            for c, (start, size) in enumerate(parts):
                at = pl.ds(group * rows + start, size)
                result[:, at] = (scale * lax.dot_general(
                    cotangent_ref[...], blocks[group * len(parts) + c][...],
                    (((1,), (1,)), ((), ())), preferred_element_type=jnp.float32,
                )).astype(out_ref.dtype)
                column = pl.multiple_of(shard * rows + start, 128)
                writes.append(pltpu.make_async_copy(
                    result.at[:, at], out_ref.at[:, pl.ds(column, size)], sems.at[group, c]
                ))
                writes[-1].start()
            for write in writes:
                write.wait()


def slot_columns(scale, width, parts, slot, cotangent, blocks, filled):
    tokens, depth = cotangent.shape
    rows = sum(size for _, size in parts)
    return call(
        functools.partial(slot_columns_kernel, scale, parts, slot, len(filled)), "context_grad",
        [half_array(tokens, width), jax.ShapeDtypeStruct((8, 128), jnp.float32)],
        [VMEM] * (1 + len(blocks)) + [HBM] * len(filled), [HBM, VMEM],
        scratch=[pltpu.VMEM((tokens, 3 * rows), cotangent.dtype), pltpu.SemaphoreType.DMA((3, len(parts)))],
        aliases={1 + len(blocks): 0} if filled else None,
    )(cotangent, *blocks, *filled)


def state_kernel(parts, where_ref, donor_ref, after_ref, *refs):
    own, (mate_ref, across_ref), refs = refs[:3], refs[3:5], refs[5:]
    outs, (taken, sems) = refs[:-2], refs[-2:]
    rows = own[0].shape[0]
    member = where_ref[1]
    way = jnp.bitwise_xor(source_of(member, donor_ref), member)

    @pl.when(way == 0)
    def _():
        copies = []
        for c, (start, size) in enumerate(parts):
            for k in range(3):
                copies.append(pltpu.make_async_copy(
                    own[k].at[pl.ds(start, size), :], outs[c].at[pl.ds(k * size, size), :], sems.at[c * 3 + k]
                ))
                copies[-1].start()
        for copy in copies:
            copy.wait()

    def widen(ref):
        copies = []
        for k in range(3):
            at = pl.ds(k * rows, rows)
            copies.append(pltpu.make_async_copy(ref.at[at, :], taken.at[at, :], sems.at[k]))
            copies[-1].start()
        for k in range(3):
            copies[k].wait()
            for c, (start, size) in enumerate(parts):
                first_row = k * rows + start
                outs[c][k * size:(k + 1) * size, :] = taken[first_row:first_row + size, :].astype(jnp.float32)

    pl.when(way == 1)(lambda: widen(mate_ref))
    pl.when(way > 1)(lambda: widen(across_ref))


def taken_state(parts, where, donor, own, donated, after):
    rows, depth = own[0].shape
    return call(
        functools.partial(state_kernel, parts), "taken_state",
        [jax.ShapeDtypeStruct((3 * size, depth), jnp.float32) for _, size in parts],
        [SMEM, SMEM, ANY] + [HBM] * 3 + [ANY] * 2, [VMEM] * len(parts),
        scratch=[pltpu.VMEM((3 * rows, depth), jnp.bfloat16), pltpu.SemaphoreType.DMA((3 * len(parts),))],
    )(where, donor, after, *own, *donated)


def adam_kernel(start, size, filled, choices_ref, state_ref, own_ref, mate_ref, across_ref, far_ref, *refs):
    refs = refs[3 if filled else 0:]
    outs, (stepped, sems) = refs[:3], refs[3:]
    depth = own_ref.shape[1]
    pieces = 4 if size % 64 == 0 else 1
    piece = size // pieces
    writes = []
    for p in range(pieces):
        def body(i):
            at = pl.ds(pl.multiple_of(p * piece + i * 16, 16), 16)
            row = lambda k: jnp.broadcast_to(choices_ref[k:k + 1, :], (16, depth))
            load = lambda k: state_ref[pl.ds(pl.multiple_of(k * size + p * piece + i * 16, 16), 16), :]
            g = far_ref[at, :].astype(jnp.float32)
            for k, ref in ((1, own_ref), (2, mate_ref), (3, across_ref)):
                g = jnp.where(row(k) > 0, ref[at, :].astype(jnp.float32), g)
            w = load(0)
            first_step = beta_one * load(1) + (1.0 - beta_one) * g
            second_step = beta_two * load(2) + (1.0 - beta_two) * g * g
            ratio = (first_step * row(6)) / (jnp.sqrt(second_step * row(7)) + epsilon)
            stepped[0, at, :] = w - row(4) * (ratio + row(5) * w)
            stepped[1, at, :] = first_step
            stepped[2, at, :] = second_step

        pl.loop(0, piece // 16)(body)
        for k in range(3):
            writes.append(pltpu.make_async_copy(
                stepped.at[k, pl.ds(p * piece, piece), :],
                outs[k].at[pl.ds(start + p * piece, piece), :], sems.at[p * 3 + k],
            ))
            writes[-1].start()
    for write in writes:
        write.wait()


def adam_update(start, size, rows, choices, state, grads, filled):
    depth = state.shape[1]
    return call(
        functools.partial(adam_kernel, start, size, bool(filled)), "adam",
        [jax.ShapeDtypeStruct((rows, depth), jnp.float32)] * 3,
        [VMEM] * 6 + [HBM] * len(filled), [HBM] * 3,
        scratch=[pltpu.VMEM((3, size, depth), jnp.float32), pltpu.SemaphoreType.DMA((12,))],
        aliases={6 + k: k for k in range(len(filled))},
    )(choices, state, *grads, *filled)


def on_device(n, members, context, out_grad, weight, first, second, rates, decays, steps, donor):
    context_rows = context[0]
    cotangent = out_grad[0]
    scale = context_rows.shape[1] ** (-0.5)
    rows, depth = weight.shape[1:]
    chains = 2 if rows % 32 == 0 else 1
    parts = [(c * rows // chains, rows // chains) for c in range(chains)]
    where = jnp.stack([lax.axis_index("shard"), lax.axis_index("member")]).astype(jnp.int32)

    swap_across = [(m, m ^ 2) for m in range(members)]
    swap_mates = [(m, m ^ 1) for m in range(members)]
    swaps = []
    for swap in range(2):
        pairs = [(s, s + 1) for s in range(swap, n - 1, 2)]
        swaps.append(pairs + [(b, a) for a, b in pairs])

    state, *own = halves(parts, weight[0], first[0], second[0])
    choices = call(
        choices_kernel, "choices", jax.ShapeDtypeStruct((8, depth), jnp.float32), [SMEM] * 5, VMEM
    )(where, rates, decays, steps, donor)
    order = [(slot, swap) for slot in range(2, n + 1) for swap in range(2)]
    terms = partial_blocks(n, scale, parts, order, where, context_rows, cotangent)

    width = context_rows.shape[1]
    by_slots = all(size % 128 == 0 for _, size in parts)
    context_grad = ()

    arrived = [[own, own]]
    sent = own[0]
    for slot in range(1, n + 1):
        now = [[], []]
        for c in range(len(parts)):
            blocks = [arrived[-1][1][c], arrived[-1][0][c]]
            if slot > 1:
                blocks = to_send([(blocks[swap], terms[2 * (slot - 2) + swap][c]) for swap in range(2)], sent)
                sent = blocks[0]
            if slot == 2 and c == 0:
                early = sent
            for swap in range(2):
                now[swap].append(lax.ppermute(blocks[swap], "shard", swaps[swap]))
        arrived.append(now)
        if by_slots and slot > 1:
            blocks = arrived[slot - 1][0] + arrived[slot - 1][1] + (list(own) if slot == 2 else [])
            *context_grad, sent = slot_columns(scale, width, parts, slot - 1, cotangent, blocks, context_grad)
    if not by_slots:
        blocks = [block for now in arrived[1:n] for swap in now for block in swap]
        context_grad = [columns(n, scale, parts, where, cotangent, list(own) + blocks)]

    mate = lax.ppermute(state, "member", swap_mates)
    across = lax.ppermute(pick(choices, state, mate, early), "member", swap_across)
    states = taken_state(parts, where, donor, (weight[0], first[0], second[0]), (mate, across), own[0])

    updated = ()
    for c, (start, size) in enumerate(parts):
        grad = sent = summed_grad(terms[-1][c], arrived[n][0][c], arrived[n][1][c], sent)
        mate = lax.ppermute(grad, "member", swap_mates)
        if c == len(parts) - 1:
            far = across = lax.ppermute(pick(choices, grad, mate, grad), "member", swap_across)
        else:
            across = lax.ppermute(grad, "member", swap_across)
            far = lax.ppermute(across, "member", swap_mates)
        updated = adam_update(start, size, rows, choices, states[c], (grad, mate, across, far), updated)
    return (context_grad[0][None],) + tuple(array[None] for array in updated)


def solution(mesh):
    whole = P(("groups", "member"), "shard", None)
    n, members = mesh.shape["shard"], mesh.shape["member"]
    return jax.shard_map(
        functools.partial(on_device, n, members),
        mesh=mesh,
        in_specs=(whole,) * 5 + (P("groups"),) * 4,
        out_specs=(whole,) * 4,
        check_vma=False,
    )
```

```python
import functools
import math

import jax
import jax.numpy as jnp
from jax import lax
from jax.experimental import pallas as pl
from jax.experimental.pallas import tpu as pltpu
from jax.sharding import PartitionSpec as P

beta_one = 0.9
beta_two = 0.999
epsilon = 1e-08

MIB = 1 << 20
SUM_FLOPS = 3 * 2 ** 29
SMEM = pl.BlockSpec(memory_space=pltpu.SMEM)
VMEM = pl.BlockSpec(memory_space=pltpu.VMEM)
HBM = pl.BlockSpec(memory_space=pltpu.HBM)
ANY = pl.BlockSpec(memory_space=pl.ANY)


def call(kernel, name, out_shape, in_specs, out_specs, limit=8, scratch=(), aliases=None, flops=0):
    return pl.pallas_call(
        kernel,
        out_shape=out_shape,
        in_specs=in_specs,
        out_specs=out_specs,
        scratch_shapes=scratch,
        input_output_aliases=aliases or {},
        compiler_params=pltpu.CompilerParams(vmem_limit_bytes=limit * MIB),
        cost_estimate=pl.CostEstimate(flops=flops, bytes_accessed=1024, transcendentals=0),
        name=name,
    )


def half_array(rows, depth):
    return jax.ShapeDtypeStruct((rows, depth), jnp.bfloat16)


def gate_kernel(value_ref, after_ref, out_ref):
    pass


def gate(value, after):
    return call(gate_kernel, "gate", half_array(*value.shape), [ANY, ANY], ANY, aliases={0: 0})(value, after)


def by_rows(ref, body, step=16):
    @pl.loop(0, ref.shape[0] // step)
    def _(i):
        body(pl.ds(pl.multiple_of(i * step, step), step))


def source_of(member, donor_ref):
    donor = donor_ref[member]
    return jnp.where(donor >= 0, donor, member)


def choices_kernel(where_ref, rates_ref, decays_ref, steps_ref, donor_ref, out_ref):
    member = where_ref[1]
    source = source_of(member, donor_ref)
    way = jnp.bitwise_xor(source, member)
    partner_source = source_of(jnp.bitwise_xor(member, 2), donor_ref)
    flags = [partner_source == jnp.bitwise_xor(member, 1), way == 0, way == 1, way == 2]
    depth = out_ref.shape[1]
    for k, flag in enumerate(flags):
        out_ref[k:k + 1, :] = jnp.full((1, depth), jnp.where(flag, 1.0, 0.0))
    out_ref[4:5, :] = jnp.full((1, depth), rates_ref[source])
    out_ref[5:6, :] = jnp.full((1, depth), decays_ref[source])
    count = jnp.full((1, depth), (steps_ref[source] + 1).astype(jnp.float32))
    out_ref[6:7, :] = 1.0 / (1.0 - jnp.exp(count * math.log(beta_one)))
    out_ref[7:8, :] = 1.0 / (1.0 - jnp.exp(count * math.log(beta_two)))


def halves_kernel(parts, weight_ref, first_ref, second_ref, state_ref, *refs):
    own_refs, (full, sems) = refs[:-2], refs[-2:]
    rows = weight_ref.shape[0]
    copies = []
    for k, ref in enumerate((weight_ref, first_ref, second_ref)):
        for c, (start, size) in enumerate(parts):
            copies.append(pltpu.make_async_copy(
                ref.at[pl.ds(start, size), :], full.at[k, pl.ds(start, size), :], sems.at[k * len(parts) + c]
            ))
            copies[-1].start()
    for k in range(3):
        for c, (start, size) in enumerate(parts):
            copies[k * len(parts) + c].wait()
            rounded = full[k, start:start + size, :].astype(jnp.bfloat16)
            if k == 0:
                own_refs[c][...] = rounded
            state_ref[k * rows + start:k * rows + start + size, :] = rounded


def halves(parts, weight, first, second):
    rows, depth = weight.shape
    sizes = [3 * rows] + [size for _, size in parts]
    return call(
        functools.partial(halves_kernel, parts), "halves",
        [half_array(size, depth) for size in sizes], [HBM] * 3, [VMEM] * len(sizes), limit=56,
        scratch=[pltpu.VMEM((3, rows, depth), jnp.float32), pltpu.SemaphoreType.DMA((3 * len(parts),))],
    )(weight, first, second)


def pick_kernel(choices_ref, own_ref, mate_ref, after_ref, out_ref):
    def body(at):
        wants_mate = jnp.broadcast_to(choices_ref[0:1, :], (16, out_ref.shape[1])) > 0
        own, mate = own_ref[at, :].astype(jnp.float32), mate_ref[at, :].astype(jnp.float32)
        out_ref[at, :] = jnp.where(wants_mate, mate, own).astype(out_ref.dtype)

    by_rows(out_ref, body)


def pick(choices, own, mate, after):
    return call(pick_kernel, "pick", half_array(*own.shape), [VMEM, VMEM, VMEM, ANY], VMEM)(
        choices, own, mate, after
    )


def partial_kernel(n, scale, parts, order, where_ref, context_ref, cotangent_ref, *refs):
    outs, (context, cotangent, product, rounded, sems, out_sems) = refs[:-6], refs[-6:]
    width = product.shape[0]
    rows = width // n
    me = where_ref[0]
    even = lax.rem(me, 2) == 0
    tile = min(256, width)
    tokens = context.shape[0]
    loads = []
    for i, start in enumerate(range(0, tokens, tokens // 4)):
        at = pl.ds(start, tokens // 4)
        loads.append(pltpu.make_async_copy(cotangent_ref.at[at, :], cotangent.at[at, :], sems.at[i]))
    for i, start in enumerate(range(0, width, tile)):
        at = pl.ds(start, tile)
        loads.append(pltpu.make_async_copy(context_ref.at[:, at], context.at[:, at], sems.at[4 + i]))
    for load in loads:
        load.start()
    rounded[width:, :] = jnp.zeros((rows, rounded.shape[1]), rounded.dtype)
    for load in loads[:4]:
        load.wait()
    for i, start in enumerate(range(0, width, tile)):
        loads[4 + i].wait()
        block = scale * lax.dot_general(
            context[:, start:start + tile], cotangent[...],
            (((0,), (0,)), ((), ())), preferred_element_type=jnp.float32,
        )
        product[start:start + tile, :] = block
        rounded[start:start + tile, :] = block.astype(rounded.dtype)
    writes = []

    def write(source, first_row, size):
        at = len(writes)
        writes.append(pltpu.make_async_copy(
            source.at[pl.ds(pl.multiple_of(first_row, 16), size), :], outs[at], out_sems.at[at]
        ))
        writes[-1].start()

    for slot, swap in order:
        rightward = even if swap == 0 else jnp.logical_not(even)
        block = lax.rem(me + jnp.where(rightward, n + 1 - slot, slot - 1), n)
        place = jnp.where(rightward, me, n - 1 - me)
        first_row = jnp.where(place >= slot - 1, width, block * rows)
        for start, size in parts:
            write(rounded, first_row + start, size)
    for start, size in parts:
        write(product, me * rows + start, size)
    for copy in writes:
        copy.wait()


def partial_blocks(n, scale, parts, order, where, context_rows, cotangent):
    tokens, width = context_rows.shape
    depth = cotangent.shape[1]
    outs = (len(order) + 1) * len(parts)
    flat = call(
        functools.partial(partial_kernel, n, scale, parts, order), "partial_blocks",
        [half_array(size, depth) for _, size in parts] * len(order)
        + [jax.ShapeDtypeStruct((size, depth), jnp.float32) for _, size in parts],
        [SMEM, HBM, HBM], [HBM] * outs, limit=14,
        scratch=[
            pltpu.VMEM(context_rows.shape, context_rows.dtype),
            pltpu.VMEM(cotangent.shape, cotangent.dtype),
            pltpu.VMEM((width, depth), jnp.float32),
            pltpu.VMEM((width + width // n, depth), jnp.bfloat16),
            pltpu.SemaphoreType.DMA((4 + width // min(256, width),)),
            pltpu.SemaphoreType.DMA((outs,)),
        ],
    )(where, context_rows, cotangent)
    return [flat[k * len(parts):(k + 1) * len(parts)] for k in range(len(order) + 1)]


def send_kernel(arrived_ref, term_ref, arrived_too_ref, term_too_ref, after_ref, out_ref, out_too_ref):
    def body(at):
        total = arrived_ref[at, :].astype(jnp.float32) + term_ref[at, :].astype(jnp.float32)
        out_ref[at, :] = total.astype(out_ref.dtype)
        total = arrived_too_ref[at, :].astype(jnp.float32) + term_too_ref[at, :].astype(jnp.float32)
        out_too_ref[at, :] = total.astype(out_too_ref.dtype)

    by_rows(out_ref, body)


def to_send(pairs, after):
    like = half_array(*pairs[0][0].shape)
    return call(send_kernel, "to_send", [like] * 2, [VMEM] * 4 + [ANY], [VMEM] * 2, flops=SUM_FLOPS)(
        *pairs[0], *pairs[1], after
    )


def grad_kernel(own_ref, one_ref, other_ref, after_ref, out_ref):
    def body(at):
        arrived = one_ref[at, :].astype(jnp.float32) + other_ref[at, :].astype(jnp.float32)
        out_ref[at, :] = (own_ref[at, :] + arrived).astype(out_ref.dtype)

    by_rows(out_ref, body)


def summed_grad(own, one, other, after):
    return call(grad_kernel, "summed_grad", half_array(*one.shape), [VMEM] * 3 + [ANY], VMEM)(
        own, one, other, after
    )


def columns_kernel(n, scale, parts, where_ref, cotangent_ref, after_ref, *refs):
    blocks, (out_ref, token_ref, full, result, out_sems) = refs[:-5], refs[-5:]
    token_ref[...] = jnp.zeros_like(token_ref)
    width = full.shape[0]
    rows = width // n
    me = where_ref[0]
    even = lax.rem(me, 2) == 0
    for k in range(2 * n - 1):
        slot, swap = (k + 1) // 2, (k + 1) % 2
        shard = me + (jnp.where(even, slot, -slot) if swap == 0 else jnp.where(even, -slot, slot))

        @pl.when(jnp.logical_and(shard >= 0, shard < n))
        def _():
            for c, (start, size) in enumerate(parts):
                first_row = pl.multiple_of(shard * rows + start, 16)
                full[pl.ds(first_row, size), :] = blocks[k * len(parts) + c][...]
    tile = min(256, width)
    writes = []
    for i, start in enumerate(range(0, width, tile)):
        result[:, start:start + tile] = (scale * lax.dot_general(
            cotangent_ref[...], full[start:start + tile, :],
            (((1,), (1,)), ((), ())), preferred_element_type=jnp.float32,
        )).astype(out_ref.dtype)
        at = pl.ds(start, tile)
        writes.append(pltpu.make_async_copy(result.at[:, at], out_ref.at[:, at], out_sems.at[i]))
        writes[-1].start()
    for write in writes:
        write.wait()


def columns(n, scale, parts, where, cotangent, after, blocks):
    tokens, depth = cotangent.shape
    width = n * sum(size for _, size in parts)
    return call(
        functools.partial(columns_kernel, n, scale, parts), "context_grad",
        [half_array(tokens, width), jax.ShapeDtypeStruct((8, 128), jnp.float32)],
        [SMEM, VMEM, ANY] + [VMEM] * len(blocks), [HBM, VMEM], limit=14,
        scratch=[
            pltpu.VMEM((width, depth), cotangent.dtype),
            pltpu.VMEM((tokens, width), cotangent.dtype),
            pltpu.SemaphoreType.DMA((width // min(256, width),)),
        ],
    )(where, cotangent, after, *blocks)


def state_kernel(parts, where_ref, donor_ref, after_ref, *refs):
    own, (mate_ref, across_ref), refs = refs[:3], refs[3:5], refs[5:]
    outs, (taken, sems) = refs[:-2], refs[-2:]
    rows = own[0].shape[0]
    member = where_ref[1]
    way = jnp.bitwise_xor(source_of(member, donor_ref), member)

    @pl.when(way == 0)
    def _():
        copies = []
        for c, (start, size) in enumerate(parts):
            for k in range(3):
                copies.append(pltpu.make_async_copy(
                    own[k].at[pl.ds(start, size), :], outs[c].at[pl.ds(k * size, size), :], sems.at[c * 3 + k]
                ))
                copies[-1].start()
        for copy in copies:
            copy.wait()

    def widen(ref):
        copies = []
        for k in range(3):
            at = pl.ds(k * rows, rows)
            copies.append(pltpu.make_async_copy(ref.at[at, :], taken.at[at, :], sems.at[k]))
            copies[-1].start()
        for k in range(3):
            copies[k].wait()
            for c, (start, size) in enumerate(parts):
                first_row = k * rows + start
                outs[c][k * size:(k + 1) * size, :] = taken[first_row:first_row + size, :].astype(jnp.float32)

    pl.when(way == 1)(lambda: widen(mate_ref))
    pl.when(way > 1)(lambda: widen(across_ref))


def taken_state(parts, where, donor, own, donated, after):
    rows, depth = own[0].shape
    return call(
        functools.partial(state_kernel, parts), "taken_state",
        [jax.ShapeDtypeStruct((3 * size, depth), jnp.float32) for _, size in parts],
        [SMEM, SMEM, ANY] + [HBM] * 3 + [ANY] * 2, [VMEM] * len(parts),
        scratch=[pltpu.VMEM((3 * rows, depth), jnp.bfloat16), pltpu.SemaphoreType.DMA((3 * len(parts),))],
    )(where, donor, after, *own, *donated)


def adam_kernel(start, size, filled, choices_ref, state_ref, own_ref, mate_ref, across_ref, far_ref, after_ref, *refs):
    refs = refs[3 if filled else 0:]
    outs, (token_ref, stepped, sems) = refs[:3], refs[3:]
    token_ref[...] = jnp.zeros_like(token_ref)
    depth = own_ref.shape[1]
    pieces = 4 if size % 64 == 0 else 3 if size % 48 == 0 else 1
    piece = size // pieces
    writes = []
    for p in range(pieces):
        def body(i):
            at = pl.ds(pl.multiple_of(p * piece + i * 16, 16), 16)
            row = lambda k: jnp.broadcast_to(choices_ref[k:k + 1, :], (16, depth))
            load = lambda k: state_ref[pl.ds(pl.multiple_of(k * size + p * piece + i * 16, 16), 16), :]
            g = far_ref[at, :].astype(jnp.float32)
            for k, ref in ((1, own_ref), (2, mate_ref), (3, across_ref)):
                g = jnp.where(row(k) > 0, ref[at, :].astype(jnp.float32), g)
            w = load(0)
            first_step = beta_one * load(1) + (1.0 - beta_one) * g
            second_step = beta_two * load(2) + (1.0 - beta_two) * g * g
            ratio = (first_step * row(6)) / (jnp.sqrt(second_step * row(7)) + epsilon)
            stepped[0, at, :] = w - row(4) * (ratio + row(5) * w)
            stepped[1, at, :] = first_step
            stepped[2, at, :] = second_step

        pl.loop(0, piece // 16)(body)
        for k in range(3):
            writes.append(pltpu.make_async_copy(
                stepped.at[k, pl.ds(p * piece, piece), :],
                outs[k].at[pl.ds(start + p * piece, piece), :], sems.at[p * 3 + k],
            ))
            writes[-1].start()
    for write in writes:
        write.wait()


def adam_update(start, size, rows, choices, state, grads, after, filled):
    depth = state.shape[1]
    return call(
        functools.partial(adam_kernel, start, size, bool(filled)), "adam",
        [jax.ShapeDtypeStruct((rows, depth), jnp.float32)] * 3 + [jax.ShapeDtypeStruct((8, 128), jnp.float32)],
        [VMEM] * 6 + [ANY] + [HBM] * len(filled), [HBM] * 3 + [VMEM],
        scratch=[pltpu.VMEM((3, size, depth), jnp.float32), pltpu.SemaphoreType.DMA((12,))],
        aliases={7 + k: k for k in range(len(filled))},
    )(choices, state, *grads, after, *filled)


def on_device(n, members, context, out_grad, weight, first, second, rates, decays, steps, donor):
    context_rows = context[0]
    cotangent = out_grad[0]
    scale = context_rows.shape[1] ** (-0.5)
    rows, depth = weight.shape[1:]
    smaller = rows * 112 // 256 // 16 * 16
    parts = [(0, smaller), (smaller, rows - smaller)] if smaller else [(0, rows)]
    where = jnp.stack([lax.axis_index("shard"), lax.axis_index("member")]).astype(jnp.int32)

    swap_across = [(m, m ^ 2) for m in range(members)]
    swap_mates = [(m, m ^ 1) for m in range(members)]
    swaps = []
    for swap in range(2):
        pairs = [(s, s + 1) for s in range(swap, n - 1, 2)]
        swaps.append(pairs + [(b, a) for a, b in pairs])

    state, *own = halves(parts, weight[0], first[0], second[0])
    choices = call(
        choices_kernel, "choices", jax.ShapeDtypeStruct((8, depth), jnp.float32), [SMEM] * 5, VMEM
    )(where, rates, decays, steps, donor)
    order = [(slot, swap) for slot in range(2, n + 1) for swap in range(2)]
    terms = partial_blocks(n, scale, parts, order, where, context_rows, cotangent)

    arrived = [[own, own]]
    sent = own[0]
    for slot in range(1, n + 1):
        now = [[], []]
        for c in range(len(parts)):
            blocks = [arrived[-1][1][c], arrived[-1][0][c]]
            if slot > 1:
                blocks = to_send([(blocks[swap], terms[2 * (slot - 2) + swap][c]) for swap in range(2)], sent)
                sent = blocks[0]
            if slot == 2 and c == 0:
                early = sent
            for swap in range(2):
                now[swap].append(lax.ppermute(blocks[swap], "shard", swaps[swap]))
        arrived.append(now)

    mate = lax.ppermute(state, "member", swap_mates)
    across = lax.ppermute(pick(choices, state, mate, early), "member", swap_across)
    states = taken_state(parts, where, donor, (weight[0], first[0], second[0]), (mate, across), sent)

    grads = []
    for c in range(len(parts)):
        sent = summed_grad(terms[-1][c], arrived[n][0][c], arrived[n][1][c], sent)
        grads.append(sent)
    blocks = list(own)
    for slot in range(1, n):
        blocks += arrived[slot][0] + arrived[slot][1]
    context_grad, computed = columns(n, scale, parts, where, cotangent, sent, blocks)

    updated = ()
    for c, (start, size) in enumerate(parts):
        mate = lax.ppermute(grads[c], "member", swap_mates)
        across = gate(lax.ppermute(grads[c], "member", swap_across), computed)
        far = lax.ppermute(across, "member", swap_mates)
        *updated, computed = adam_update(
            start, size, rows, choices, states[c], (grads[c], mate, across, far), computed, updated
        )
    return (context_grad[None],) + tuple(array[None] for array in updated)


def solution(mesh):
    whole = P(("groups", "member"), "shard", None)
    n, members = mesh.shape["shard"], mesh.shape["member"]
    return jax.shard_map(
        functools.partial(on_device, n, members),
        mesh=mesh,
        in_specs=(whole,) * 5 + (P("groups"),) * 4,
        out_specs=(whole,) * 4,
        check_vma=False,
    )
```

```python
import functools
import math

import jax
import jax.numpy as jnp
from jax import lax
from jax.experimental import pallas as pl
from jax.experimental.pallas import tpu as pltpu
from jax.sharding import PartitionSpec as P

beta_one = 0.9
beta_two = 0.999
epsilon = 1e-08

MIB = 1 << 20
SUM_FLOPS = 2 ** 30
SMEM = pl.BlockSpec(memory_space=pltpu.SMEM)
VMEM = pl.BlockSpec(memory_space=pltpu.VMEM)
HBM = pl.BlockSpec(memory_space=pltpu.HBM)
ANY = pl.BlockSpec(memory_space=pl.ANY)


def call(kernel, name, out_shape, in_specs, out_specs, limit=8, scratch=(), aliases=None, flops=0):
    return pl.pallas_call(
        kernel,
        out_shape=out_shape,
        in_specs=in_specs,
        out_specs=out_specs,
        scratch_shapes=scratch,
        input_output_aliases=aliases or {},
        compiler_params=pltpu.CompilerParams(vmem_limit_bytes=limit * MIB),
        cost_estimate=pl.CostEstimate(flops=flops, bytes_accessed=1024, transcendentals=0),
        name=name,
    )


def half_array(rows, depth):
    return jax.ShapeDtypeStruct((rows, depth), jnp.bfloat16)


def gate_kernel(value_ref, after_ref, out_ref):
    pass


def gate(value, after):
    return call(gate_kernel, "gate", half_array(*value.shape), [ANY, ANY], ANY, aliases={0: 0})(value, after)


def by_rows(ref, body, step=16):
    @pl.loop(0, ref.shape[0] // step)
    def _(i):
        body(pl.ds(pl.multiple_of(i * step, step), step))


def source_of(member, donor_ref):
    donor = donor_ref[member]
    return jnp.where(donor >= 0, donor, member)


def choices_kernel(where_ref, rates_ref, decays_ref, steps_ref, donor_ref, out_ref):
    member = where_ref[1]
    source = source_of(member, donor_ref)
    way = jnp.bitwise_xor(source, member)
    partner_source = source_of(jnp.bitwise_xor(member, 2), donor_ref)
    flags = [partner_source == jnp.bitwise_xor(member, 1), way == 0, way == 1, way == 2]
    depth = out_ref.shape[1]
    for k, flag in enumerate(flags):
        out_ref[k:k + 1, :] = jnp.full((1, depth), jnp.where(flag, 1.0, 0.0))
    out_ref[4:5, :] = jnp.full((1, depth), rates_ref[source])
    out_ref[5:6, :] = jnp.full((1, depth), decays_ref[source])
    count = jnp.full((1, depth), (steps_ref[source] + 1).astype(jnp.float32))
    out_ref[6:7, :] = 1.0 / (1.0 - jnp.exp(count * math.log(beta_one)))
    out_ref[7:8, :] = 1.0 / (1.0 - jnp.exp(count * math.log(beta_two)))


def halves_kernel(parts, weight_ref, first_ref, second_ref, state_ref, *refs):
    own_refs, (full, sems) = refs[:-2], refs[-2:]
    rows = weight_ref.shape[0]
    copies = []
    for k, ref in enumerate((weight_ref, first_ref, second_ref)):
        for c, (start, size) in enumerate(parts):
            copies.append(pltpu.make_async_copy(
                ref.at[pl.ds(start, size), :], full.at[k, pl.ds(start, size), :], sems.at[k * len(parts) + c]
            ))
            copies[-1].start()
    for k in range(3):
        for c, (start, size) in enumerate(parts):
            copies[k * len(parts) + c].wait()
            rounded = full[k, start:start + size, :].astype(jnp.bfloat16)
            if k == 0:
                own_refs[c][...] = rounded
            state_ref[k * rows + start:k * rows + start + size, :] = rounded


def halves(parts, weight, first, second):
    rows, depth = weight.shape
    sizes = [3 * rows] + [size for _, size in parts]
    return call(
        functools.partial(halves_kernel, parts), "halves",
        [half_array(size, depth) for size in sizes], [HBM] * 3, [VMEM] * len(sizes), limit=56,
        scratch=[pltpu.VMEM((3, rows, depth), jnp.float32), pltpu.SemaphoreType.DMA((3 * len(parts),))],
    )(weight, first, second)


def pick_kernel(choices_ref, own_ref, mate_ref, after_ref, out_ref):
    def body(at):
        wants_mate = jnp.broadcast_to(choices_ref[0:1, :], (16, out_ref.shape[1])) > 0
        own, mate = own_ref[at, :].astype(jnp.float32), mate_ref[at, :].astype(jnp.float32)
        out_ref[at, :] = jnp.where(wants_mate, mate, own).astype(out_ref.dtype)

    by_rows(out_ref, body)


def pick(choices, own, mate, after):
    return call(pick_kernel, "pick", half_array(*own.shape), [VMEM, VMEM, VMEM, ANY], VMEM)(
        choices, own, mate, after
    )


def partial_kernel(n, scale, parts, order, where_ref, context_ref, cotangent_ref, *refs):
    outs, (context, cotangent, product, rounded, sems, out_sems) = refs[:-6], refs[-6:]
    width = product.shape[0]
    rows = width // n
    me = where_ref[0]
    even = lax.rem(me, 2) == 0
    tile = min(256, width)
    tokens = context.shape[0]
    loads = []
    for i, start in enumerate(range(0, tokens, tokens // 4)):
        at = pl.ds(start, tokens // 4)
        loads.append(pltpu.make_async_copy(cotangent_ref.at[at, :], cotangent.at[at, :], sems.at[i]))
    for i, start in enumerate(range(0, width, tile)):
        at = pl.ds(start, tile)
        loads.append(pltpu.make_async_copy(context_ref.at[:, at], context.at[:, at], sems.at[4 + i]))
    for load in loads:
        load.start()
    rounded[width:, :] = jnp.zeros((rows, rounded.shape[1]), rounded.dtype)
    for load in loads[:4]:
        load.wait()
    for i, start in enumerate(range(0, width, tile)):
        loads[4 + i].wait()
        block = scale * lax.dot_general(
            context[:, start:start + tile], cotangent[...],
            (((0,), (0,)), ((), ())), preferred_element_type=jnp.float32,
        )
        product[start:start + tile, :] = block
        rounded[start:start + tile, :] = block.astype(rounded.dtype)
    writes = []

    def write(source, first_row, size):
        at = len(writes)
        writes.append(pltpu.make_async_copy(
            source.at[pl.ds(pl.multiple_of(first_row, 16), size), :], outs[at], out_sems.at[at]
        ))
        writes[-1].start()

    for slot, swap in order:
        rightward = even if swap == 0 else jnp.logical_not(even)
        block = lax.rem(me + jnp.where(rightward, n + 1 - slot, slot - 1), n)
        place = jnp.where(rightward, me, n - 1 - me)
        first_row = jnp.where(place >= slot - 1, width, block * rows)
        for start, size in parts:
            write(rounded, first_row + start, size)
    for start, size in parts:
        write(product, me * rows + start, size)
    for copy in writes:
        copy.wait()


def partial_blocks(n, scale, parts, order, where, context_rows, cotangent):
    tokens, width = context_rows.shape
    depth = cotangent.shape[1]
    outs = (len(order) + 1) * len(parts)
    flat = call(
        functools.partial(partial_kernel, n, scale, parts, order), "partial_blocks",
        [half_array(size, depth) for _, size in parts] * len(order)
        + [jax.ShapeDtypeStruct((size, depth), jnp.float32) for _, size in parts],
        [SMEM, HBM, HBM], [HBM] * outs, limit=14,
        scratch=[
            pltpu.VMEM(context_rows.shape, context_rows.dtype),
            pltpu.VMEM(cotangent.shape, cotangent.dtype),
            pltpu.VMEM((width, depth), jnp.float32),
            pltpu.VMEM((width + width // n, depth), jnp.bfloat16),
            pltpu.SemaphoreType.DMA((4 + width // min(256, width),)),
            pltpu.SemaphoreType.DMA((outs,)),
        ],
    )(where, context_rows, cotangent)
    return [flat[k * len(parts):(k + 1) * len(parts)] for k in range(len(order) + 1)]


def send_kernel(arrived_ref, term_ref, arrived_too_ref, term_too_ref, after_ref, out_ref, out_too_ref):
    def body(at):
        total = arrived_ref[at, :].astype(jnp.float32) + term_ref[at, :].astype(jnp.float32)
        out_ref[at, :] = total.astype(out_ref.dtype)
        total = arrived_too_ref[at, :].astype(jnp.float32) + term_too_ref[at, :].astype(jnp.float32)
        out_too_ref[at, :] = total.astype(out_too_ref.dtype)

    by_rows(out_ref, body)


def to_send(pairs, after):
    like = half_array(*pairs[0][0].shape)
    return call(send_kernel, "to_send", [like] * 2, [VMEM] * 4 + [ANY], [VMEM] * 2, flops=SUM_FLOPS)(
        *pairs[0], *pairs[1], after
    )


def grad_kernel(cuts, own_ref, one_ref, other_ref, after_ref, *refs):
    def body(at):
        arrived = one_ref[at, :].astype(jnp.float32) + other_ref[at, :].astype(jnp.float32)
        return (own_ref[at, :] + arrived).astype(jnp.bfloat16)

    first = 0
    carried = refs[0] if len(refs) > len(cuts) else None
    for out_ref, size in zip(refs[len(refs) - len(cuts):], cuts):
        top = 0
        if carried is not None:
            top = carried.shape[0]
            out_ref[0:top, :] = carried[...]

        @pl.loop(0, (size - top) // 16)
        def _(i):
            out_ref[pl.ds(pl.multiple_of(top + i * 16, 16), 16), :] = body(
                pl.ds(pl.multiple_of(first + i * 16, 16), 16)
            )

        first, carried = first + size - top, None


def summed_grad(own, one, other, after, cuts, carried=()):
    depth = one.shape[1]
    return call(
        functools.partial(grad_kernel, cuts), "summed_grad", [half_array(size, depth) for size in cuts],
        [VMEM] * 3 + [ANY] + [VMEM] * len(carried), [VMEM] * len(cuts),
    )(own, one, other, after, *carried)


def columns_kernel(n, scale, parts, where_ref, cotangent_ref, after_ref, *refs):
    blocks, (out_ref, token_ref, full, result, out_sems) = refs[:-5], refs[-5:]
    token_ref[...] = jnp.zeros_like(token_ref)
    width = full.shape[0]
    rows = width // n
    me = where_ref[0]
    even = lax.rem(me, 2) == 0
    for k in range(2 * n - 1):
        slot, swap = (k + 1) // 2, (k + 1) % 2
        shard = me + (jnp.where(even, slot, -slot) if swap == 0 else jnp.where(even, -slot, slot))

        @pl.when(jnp.logical_and(shard >= 0, shard < n))
        def _():
            for c, (start, size) in enumerate(parts):
                first_row = pl.multiple_of(shard * rows + start, 16)
                full[pl.ds(first_row, size), :] = blocks[k * len(parts) + c][...]
    tile = min(256, width)
    writes = []
    for i, start in enumerate(range(0, width, tile)):
        result[:, start:start + tile] = (scale * lax.dot_general(
            cotangent_ref[...], full[start:start + tile, :],
            (((1,), (1,)), ((), ())), preferred_element_type=jnp.float32,
        )).astype(out_ref.dtype)
        at = pl.ds(start, tile)
        writes.append(pltpu.make_async_copy(result.at[:, at], out_ref.at[:, at], out_sems.at[i]))
        writes[-1].start()
    for write in writes:
        write.wait()


def columns(n, scale, parts, where, cotangent, after, blocks):
    tokens, depth = cotangent.shape
    width = n * sum(size for _, size in parts)
    return call(
        functools.partial(columns_kernel, n, scale, parts), "context_grad",
        [half_array(tokens, width), jax.ShapeDtypeStruct((8, 128), jnp.float32)],
        [SMEM, VMEM, ANY] + [VMEM] * len(blocks), [HBM, VMEM], limit=14,
        scratch=[
            pltpu.VMEM((width, depth), cotangent.dtype),
            pltpu.VMEM((tokens, width), cotangent.dtype),
            pltpu.SemaphoreType.DMA((width // min(256, width),)),
        ],
    )(where, cotangent, after, *blocks)


def state_kernel(parts, where_ref, donor_ref, after_ref, *refs):
    own, (mate_ref, across_ref), refs = refs[:3], refs[3:5], refs[5:]
    outs, (taken, sems) = refs[:-2], refs[-2:]
    rows = own[0].shape[0]
    member = where_ref[1]
    way = jnp.bitwise_xor(source_of(member, donor_ref), member)

    @pl.when(way == 0)
    def _():
        copies = []
        for c, (start, size) in enumerate(parts):
            for k in range(3):
                copies.append(pltpu.make_async_copy(
                    own[k].at[pl.ds(start, size), :], outs[c].at[pl.ds(k * size, size), :], sems.at[c * 3 + k]
                ))
                copies[-1].start()
        for copy in copies:
            copy.wait()

    def widen(ref):
        copies = []
        for k in range(3):
            at = pl.ds(k * rows, rows)
            copies.append(pltpu.make_async_copy(ref.at[at, :], taken.at[at, :], sems.at[k]))
            copies[-1].start()
        for k in range(3):
            copies[k].wait()
            for c, (start, size) in enumerate(parts):
                first_row = k * rows + start
                outs[c][k * size:(k + 1) * size, :] = taken[first_row:first_row + size, :].astype(jnp.float32)

    pl.when(way == 1)(lambda: widen(mate_ref))
    pl.when(way > 1)(lambda: widen(across_ref))


def taken_state(parts, where, donor, own, donated, after):
    rows, depth = own[0].shape
    return call(
        functools.partial(state_kernel, parts), "taken_state",
        [jax.ShapeDtypeStruct((3 * size, depth), jnp.float32) for _, size in parts],
        [SMEM, SMEM, ANY] + [HBM] * 3 + [ANY] * 2, [VMEM] * len(parts),
        scratch=[pltpu.VMEM((3 * rows, depth), jnp.bfloat16), pltpu.SemaphoreType.DMA((3 * len(parts),))],
    )(where, donor, after, *own, *donated)


def adam_kernel(start, size, filled, choices_ref, state_ref, own_ref, mate_ref, across_ref, far_ref, after_ref, *refs):
    refs = refs[3 if filled else 0:]
    outs, (token_ref, stepped, sems) = refs[:3], refs[3:]
    token_ref[...] = jnp.zeros_like(token_ref)
    depth = own_ref.shape[1]
    pieces = 4 if size % 64 == 0 else 3 if size % 48 == 0 else 1
    piece = size // pieces
    writes = []
    for p in range(pieces):
        def body(i):
            at = pl.ds(pl.multiple_of(p * piece + i * 16, 16), 16)
            row = lambda k: jnp.broadcast_to(choices_ref[k:k + 1, :], (16, depth))
            load = lambda k: state_ref[pl.ds(pl.multiple_of(k * size + p * piece + i * 16, 16), 16), :]
            g = far_ref[at, :].astype(jnp.float32)
            for k, ref in ((1, own_ref), (2, mate_ref), (3, across_ref)):
                g = jnp.where(row(k) > 0, ref[at, :].astype(jnp.float32), g)
            w = load(0)
            first_step = beta_one * load(1) + (1.0 - beta_one) * g
            second_step = beta_two * load(2) + (1.0 - beta_two) * g * g
            ratio = (first_step * row(6)) / (jnp.sqrt(second_step * row(7)) + epsilon)
            stepped[0, at, :] = w - row(4) * (ratio + row(5) * w)
            stepped[1, at, :] = first_step
            stepped[2, at, :] = second_step

        pl.loop(0, piece // 16)(body)
        for k in range(3):
            writes.append(pltpu.make_async_copy(
                stepped.at[k, pl.ds(p * piece, piece), :],
                outs[k].at[pl.ds(start + p * piece, piece), :], sems.at[p * 3 + k],
            ))
            writes[-1].start()
    for write in writes:
        write.wait()


def adam_update(start, size, rows, choices, state, grads, after, filled):
    depth = state.shape[1]
    return call(
        functools.partial(adam_kernel, start, size, bool(filled)), "adam",
        [jax.ShapeDtypeStruct((rows, depth), jnp.float32)] * 3 + [jax.ShapeDtypeStruct((8, 128), jnp.float32)],
        [VMEM] * 6 + [ANY] + [HBM] * len(filled), [HBM] * 3 + [VMEM],
        scratch=[pltpu.VMEM((3, size, depth), jnp.float32), pltpu.SemaphoreType.DMA((12,))],
        aliases={7 + k: k for k in range(len(filled))},
    )(choices, state, *grads, after, *filled)


def on_device(n, members, context, out_grad, weight, first, second, rates, decays, steps, donor):
    context_rows = context[0]
    cotangent = out_grad[0]
    scale = context_rows.shape[1] ** (-0.5)
    rows, depth = weight.shape[1:]
    chains = 2 if rows % 32 == 0 else 1
    parts = [(c * rows // chains, rows // chains) for c in range(chains)]
    lower = rows * 112 // 256 // 16 * 16
    steps_of = [(0, lower), (lower, rows - lower)] if chains == 2 and lower else [(0, rows)]
    where = jnp.stack([lax.axis_index("shard"), lax.axis_index("member")]).astype(jnp.int32)

    swap_across = [(m, m ^ 2) for m in range(members)]
    swap_mates = [(m, m ^ 1) for m in range(members)]
    swaps = []
    for swap in range(2):
        pairs = [(s, s + 1) for s in range(swap, n - 1, 2)]
        swaps.append(pairs + [(b, a) for a, b in pairs])

    state, *own = halves(parts, weight[0], first[0], second[0])
    choices = call(
        choices_kernel, "choices", jax.ShapeDtypeStruct((8, depth), jnp.float32), [SMEM] * 5, VMEM
    )(where, rates, decays, steps, donor)
    order = [(slot, swap) for slot in range(2, n + 1) for swap in range(2)]
    terms = partial_blocks(n, scale, parts, order, where, context_rows, cotangent)

    arrived = [[own, own]]
    sent = own[0]
    for slot in range(1, n + 1):
        now = [[], []]
        for c in range(len(parts)):
            blocks = [arrived[-1][1][c], arrived[-1][0][c]]
            if slot > 1:
                blocks = to_send([(blocks[swap], terms[2 * (slot - 2) + swap][c]) for swap in range(2)], sent)
                sent = blocks[0]
            for swap in range(2):
                now[swap].append(lax.ppermute(blocks[swap], "shard", swaps[swap]))
        arrived.append(now)

    mate = lax.ppermute(state, "member", swap_mates)
    across = lax.ppermute(pick(choices, state, mate, own[0]), "member", swap_across)
    states = taken_state(steps_of, where, donor, (weight[0], first[0], second[0]), (mate, across), sent)

    grads, carried = [], ()
    for c, (_, size) in enumerate(parts):
        last = c == len(parts) - 1
        cuts = [steps_of[c][1]] if last else [steps_of[c][1], size - steps_of[c][1]]
        cuts = [cut for cut in cuts if cut]
        sums = summed_grad(terms[-1][c], arrived[n][0][c], arrived[n][1][c], sent, cuts, carried)
        grads.append(sums[0])
        sent, carried = sums[0], tuple(sums[1:])
    blocks = list(own)
    for slot in range(1, n):
        blocks += arrived[slot][0] + arrived[slot][1]
    context_grad, computed = columns(n, scale, parts, where, cotangent, sent, blocks)

    updated = ()
    for c, (start, size) in enumerate(steps_of):
        mate = lax.ppermute(grads[c], "member", swap_mates)
        across = gate(lax.ppermute(grads[c], "member", swap_across), computed)
        far = lax.ppermute(across, "member", swap_mates)
        *updated, computed = adam_update(
            start, size, rows, choices, states[c], (grads[c], mate, across, far), computed, updated
        )
    return (context_grad[None],) + tuple(array[None] for array in updated)


def solution(mesh):
    whole = P(("groups", "member"), "shard", None)
    n, members = mesh.shape["shard"], mesh.shape["member"]
    return jax.shard_map(
        functools.partial(on_device, n, members),
        mesh=mesh,
        in_specs=(whole,) * 5 + (P("groups"),) * 4,
        out_specs=(whole,) * 4,
        check_vma=False,
    )
```

```python
import functools
import math

import jax
import jax.numpy as jnp
from jax import lax
from jax.experimental import pallas as pl
from jax.experimental.pallas import tpu as pltpu
from jax.sharding import PartitionSpec as P

beta_one = 0.9
beta_two = 0.999
epsilon = 1e-08

MIB = 1 << 20
SUM_FLOPS = 5 * 2 ** 28
SMEM = pl.BlockSpec(memory_space=pltpu.SMEM)
VMEM = pl.BlockSpec(memory_space=pltpu.VMEM)
HBM = pl.BlockSpec(memory_space=pltpu.HBM)
ANY = pl.BlockSpec(memory_space=pl.ANY)


def call(kernel, name, out_shape, in_specs, out_specs, limit=8, scratch=(), aliases=None, flops=0):
    return pl.pallas_call(
        kernel,
        out_shape=out_shape,
        in_specs=in_specs,
        out_specs=out_specs,
        scratch_shapes=scratch,
        input_output_aliases=aliases or {},
        compiler_params=pltpu.CompilerParams(vmem_limit_bytes=limit * MIB),
        cost_estimate=pl.CostEstimate(flops=flops, bytes_accessed=1024, transcendentals=0),
        name=name,
    )


def half_array(rows, depth):
    return jax.ShapeDtypeStruct((rows, depth), jnp.bfloat16)


def gate_kernel(value_ref, after_ref, out_ref):
    pass


def gate(value, after):
    return call(gate_kernel, "gate", half_array(*value.shape), [ANY, ANY], ANY, aliases={0: 0})(value, after)


def by_rows(ref, body, step=16):
    @pl.loop(0, ref.shape[0] // step)
    def _(i):
        body(pl.ds(pl.multiple_of(i * step, step), step))


def source_of(member, donor_ref):
    donor = donor_ref[member]
    return jnp.where(donor >= 0, donor, member)


def choices_kernel(where_ref, rates_ref, decays_ref, steps_ref, donor_ref, out_ref):
    member = where_ref[1]
    source = source_of(member, donor_ref)
    way = jnp.bitwise_xor(source, member)
    partner_source = source_of(jnp.bitwise_xor(member, 2), donor_ref)
    flags = [partner_source == jnp.bitwise_xor(member, 1), way == 0, way == 1, way == 2]
    depth = out_ref.shape[1]
    for k, flag in enumerate(flags):
        out_ref[k:k + 1, :] = jnp.full((1, depth), jnp.where(flag, 1.0, 0.0))
    out_ref[4:5, :] = jnp.full((1, depth), rates_ref[source])
    out_ref[5:6, :] = jnp.full((1, depth), decays_ref[source])
    count = jnp.full((1, depth), (steps_ref[source] + 1).astype(jnp.float32))
    out_ref[6:7, :] = 1.0 / (1.0 - jnp.exp(count * math.log(beta_one)))
    out_ref[7:8, :] = 1.0 / (1.0 - jnp.exp(count * math.log(beta_two)))


def halves_kernel(parts, weight_ref, first_ref, second_ref, state_ref, *refs):
    own_refs, (full, sems) = refs[:-2], refs[-2:]
    rows = weight_ref.shape[0]
    copies = []
    for k, ref in enumerate((weight_ref, first_ref, second_ref)):
        for c, (start, size) in enumerate(parts):
            copies.append(pltpu.make_async_copy(
                ref.at[pl.ds(start, size), :], full.at[k, pl.ds(start, size), :], sems.at[k * len(parts) + c]
            ))
            copies[-1].start()
    for k in range(3):
        for c, (start, size) in enumerate(parts):
            copies[k * len(parts) + c].wait()
            rounded = full[k, start:start + size, :].astype(jnp.bfloat16)
            if k == 0:
                own_refs[c][...] = rounded
            state_ref[k * rows + start:k * rows + start + size, :] = rounded


def halves(parts, weight, first, second):
    rows, depth = weight.shape
    sizes = [3 * rows] + [size for _, size in parts]
    return call(
        functools.partial(halves_kernel, parts), "halves",
        [half_array(size, depth) for size in sizes], [HBM] * 3, [VMEM] * len(sizes), limit=56,
        scratch=[pltpu.VMEM((3, rows, depth), jnp.float32), pltpu.SemaphoreType.DMA((3 * len(parts),))],
    )(weight, first, second)


def pick_kernel(choices_ref, own_ref, mate_ref, after_ref, out_ref):
    def body(at):
        wants_mate = jnp.broadcast_to(choices_ref[0:1, :], (16, out_ref.shape[1])) > 0
        own, mate = own_ref[at, :].astype(jnp.float32), mate_ref[at, :].astype(jnp.float32)
        out_ref[at, :] = jnp.where(wants_mate, mate, own).astype(out_ref.dtype)

    by_rows(out_ref, body)


def pick(choices, own, mate, after):
    return call(pick_kernel, "pick", half_array(*own.shape), [VMEM, VMEM, VMEM, ANY], VMEM)(
        choices, own, mate, after
    )


def partial_kernel(n, scale, parts, order, where_ref, context_ref, cotangent_ref, *refs):
    outs, (context, cotangent, product, rounded, sems, out_sems) = refs[:-6], refs[-6:]
    width = product.shape[0]
    rows = width // n
    me = where_ref[0]
    even = lax.rem(me, 2) == 0
    tile = min(256, width)
    tokens = context.shape[0]
    loads = []
    for i, start in enumerate(range(0, tokens, tokens // 4)):
        at = pl.ds(start, tokens // 4)
        loads.append(pltpu.make_async_copy(cotangent_ref.at[at, :], cotangent.at[at, :], sems.at[i]))
    for i, start in enumerate(range(0, width, tile)):
        at = pl.ds(start, tile)
        loads.append(pltpu.make_async_copy(context_ref.at[:, at], context.at[:, at], sems.at[4 + i]))
    for load in loads:
        load.start()
    rounded[width:, :] = jnp.zeros((rows, rounded.shape[1]), rounded.dtype)
    for load in loads[:4]:
        load.wait()
    for i, start in enumerate(range(0, width, tile)):
        loads[4 + i].wait()
        block = scale * lax.dot_general(
            context[:, start:start + tile], cotangent[...],
            (((0,), (0,)), ((), ())), preferred_element_type=jnp.float32,
        )
        product[start:start + tile, :] = block
        rounded[start:start + tile, :] = block.astype(rounded.dtype)
    writes = []

    def write(source, first_row, size):
        at = len(writes)
        writes.append(pltpu.make_async_copy(
            source.at[pl.ds(pl.multiple_of(first_row, 16), size), :], outs[at], out_sems.at[at]
        ))
        writes[-1].start()

    for slot, swap in order:
        rightward = even if swap == 0 else jnp.logical_not(even)
        block = lax.rem(me + jnp.where(rightward, n + 1 - slot, slot - 1), n)
        place = jnp.where(rightward, me, n - 1 - me)
        first_row = jnp.where(place >= slot - 1, width, block * rows)
        for start, size in parts:
            write(rounded, first_row + start, size)
    for start, size in parts:
        write(product, me * rows + start, size)
    for copy in writes:
        copy.wait()


def partial_blocks(n, scale, parts, order, where, context_rows, cotangent):
    tokens, width = context_rows.shape
    depth = cotangent.shape[1]
    outs = (len(order) + 1) * len(parts)
    flat = call(
        functools.partial(partial_kernel, n, scale, parts, order), "partial_blocks",
        [half_array(size, depth) for _, size in parts] * len(order)
        + [jax.ShapeDtypeStruct((size, depth), jnp.float32) for _, size in parts],
        [SMEM, HBM, HBM], [HBM] * outs, limit=14,
        scratch=[
            pltpu.VMEM(context_rows.shape, context_rows.dtype),
            pltpu.VMEM(cotangent.shape, cotangent.dtype),
            pltpu.VMEM((width, depth), jnp.float32),
            pltpu.VMEM((width + width // n, depth), jnp.bfloat16),
            pltpu.SemaphoreType.DMA((4 + width // min(256, width),)),
            pltpu.SemaphoreType.DMA((outs,)),
        ],
    )(where, context_rows, cotangent)
    return [flat[k * len(parts):(k + 1) * len(parts)] for k in range(len(order) + 1)]


def send_kernel(arrived_ref, term_ref, arrived_too_ref, term_too_ref, after_ref, out_ref, out_too_ref):
    def body(at):
        total = arrived_ref[at, :].astype(jnp.float32) + term_ref[at, :].astype(jnp.float32)
        out_ref[at, :] = total.astype(out_ref.dtype)
        total = arrived_too_ref[at, :].astype(jnp.float32) + term_too_ref[at, :].astype(jnp.float32)
        out_too_ref[at, :] = total.astype(out_too_ref.dtype)

    by_rows(out_ref, body)


def to_send(pairs, after):
    like = half_array(*pairs[0][0].shape)
    return call(send_kernel, "to_send", [like] * 2, [VMEM] * 4 + [ANY], [VMEM] * 2, flops=SUM_FLOPS)(
        *pairs[0], *pairs[1], after
    )


def grad_kernel(cuts, own_ref, one_ref, other_ref, after_ref, *refs):
    def body(at):
        arrived = one_ref[at, :].astype(jnp.float32) + other_ref[at, :].astype(jnp.float32)
        return (own_ref[at, :] + arrived).astype(jnp.bfloat16)

    first = 0
    carried = refs[0] if len(refs) > len(cuts) else None
    for out_ref, size in zip(refs[len(refs) - len(cuts):], cuts):
        top = 0
        if carried is not None:
            top = carried.shape[0]
            out_ref[0:top, :] = carried[...]

        @pl.loop(0, (size - top) // 16)
        def _(i):
            out_ref[pl.ds(pl.multiple_of(top + i * 16, 16), 16), :] = body(
                pl.ds(pl.multiple_of(first + i * 16, 16), 16)
            )

        first, carried = first + size - top, None


def summed_grad(own, one, other, after, cuts, carried=()):
    depth = one.shape[1]
    return call(
        functools.partial(grad_kernel, cuts), "summed_grad", [half_array(size, depth) for size in cuts],
        [VMEM] * 3 + [ANY] + [VMEM] * len(carried), [VMEM] * len(cuts),
    )(own, one, other, after, *carried)


def columns_kernel(n, scale, parts, where_ref, cotangent_ref, after_ref, *refs):
    blocks, (out_ref, token_ref, full, result, out_sems) = refs[:-5], refs[-5:]
    token_ref[...] = jnp.zeros_like(token_ref)
    width = full.shape[0]
    rows = width // n
    me = where_ref[0]
    even = lax.rem(me, 2) == 0
    for k in range(2 * n - 1):
        slot, swap = (k + 1) // 2, (k + 1) % 2
        shard = me + (jnp.where(even, slot, -slot) if swap == 0 else jnp.where(even, -slot, slot))

        @pl.when(jnp.logical_and(shard >= 0, shard < n))
        def _():
            for c, (start, size) in enumerate(parts):
                first_row = pl.multiple_of(shard * rows + start, 16)
                full[pl.ds(first_row, size), :] = blocks[k * len(parts) + c][...]
    tile = min(256, width)
    writes = []
    for i, start in enumerate(range(0, width, tile)):
        result[:, start:start + tile] = (scale * lax.dot_general(
            cotangent_ref[...], full[start:start + tile, :],
            (((1,), (1,)), ((), ())), preferred_element_type=jnp.float32,
        )).astype(out_ref.dtype)
        at = pl.ds(start, tile)
        writes.append(pltpu.make_async_copy(result.at[:, at], out_ref.at[:, at], out_sems.at[i]))
        writes[-1].start()
    for write in writes:
        write.wait()


def columns(n, scale, parts, where, cotangent, after, blocks):
    tokens, depth = cotangent.shape
    width = n * sum(size for _, size in parts)
    return call(
        functools.partial(columns_kernel, n, scale, parts), "context_grad",
        [half_array(tokens, width), jax.ShapeDtypeStruct((8, 128), jnp.float32)],
        [SMEM, VMEM, ANY] + [VMEM] * len(blocks), [HBM, VMEM], limit=14,
        scratch=[
            pltpu.VMEM((width, depth), cotangent.dtype),
            pltpu.VMEM((tokens, width), cotangent.dtype),
            pltpu.SemaphoreType.DMA((width // min(256, width),)),
        ],
    )(where, cotangent, after, *blocks)


def state_kernel(parts, where_ref, donor_ref, after_ref, *refs):
    own, (mate_ref, across_ref), refs = refs[:3], refs[3:5], refs[5:]
    outs, (taken, sems) = refs[:-2], refs[-2:]
    rows = own[0].shape[0]
    member = where_ref[1]
    way = jnp.bitwise_xor(source_of(member, donor_ref), member)

    @pl.when(way == 0)
    def _():
        copies = []
        for c, (start, size) in enumerate(parts):
            for k in range(3):
                copies.append(pltpu.make_async_copy(
                    own[k].at[pl.ds(start, size), :], outs[c].at[pl.ds(k * size, size), :], sems.at[c * 3 + k]
                ))
                copies[-1].start()
        for copy in copies:
            copy.wait()

    def widen(ref):
        copies = []
        for k in range(3):
            at = pl.ds(k * rows, rows)
            copies.append(pltpu.make_async_copy(ref.at[at, :], taken.at[at, :], sems.at[k]))
            copies[-1].start()
        for k in range(3):
            copies[k].wait()
            for c, (start, size) in enumerate(parts):
                first_row = k * rows + start
                outs[c][k * size:(k + 1) * size, :] = taken[first_row:first_row + size, :].astype(jnp.float32)

    pl.when(way == 1)(lambda: widen(mate_ref))
    pl.when(way > 1)(lambda: widen(across_ref))


def taken_state(parts, where, donor, own, donated, after):
    rows, depth = own[0].shape
    return call(
        functools.partial(state_kernel, parts), "taken_state",
        [jax.ShapeDtypeStruct((3 * size, depth), jnp.float32) for _, size in parts],
        [SMEM, SMEM, ANY] + [HBM] * 3 + [ANY] * 2, [VMEM] * len(parts),
        scratch=[pltpu.VMEM((3 * rows, depth), jnp.bfloat16), pltpu.SemaphoreType.DMA((3 * len(parts),))],
    )(where, donor, after, *own, *donated)


def adam_kernel(start, size, filled, choices_ref, state_ref, own_ref, mate_ref, across_ref, far_ref, after_ref, *refs):
    refs = refs[3 if filled else 0:]
    outs, (token_ref, stepped, sems) = refs[:3], refs[3:]
    token_ref[...] = jnp.zeros_like(token_ref)
    depth = own_ref.shape[1]
    writes = []
    piece = 32
    for top in range(0, size, piece):
        height = min(piece, size - top)

        def body(i):
            at = pl.ds(pl.multiple_of(top + i * 16, 16), 16)
            row = lambda k: jnp.broadcast_to(choices_ref[k:k + 1, :], (16, depth))
            load = lambda k: state_ref[pl.ds(pl.multiple_of(k * size + top + i * 16, 16), 16), :]
            g = far_ref[at, :].astype(jnp.float32)
            for k, ref in ((1, own_ref), (2, mate_ref), (3, across_ref)):
                g = jnp.where(row(k) > 0, ref[at, :].astype(jnp.float32), g)
            w = load(0)
            first_step = beta_one * load(1) + (1.0 - beta_one) * g
            second_step = beta_two * load(2) + (1.0 - beta_two) * g * g
            ratio = (first_step * row(6)) / (jnp.sqrt(second_step * row(7)) + epsilon)
            stepped[0, at, :] = w - row(4) * (ratio + row(5) * w)
            stepped[1, at, :] = first_step
            stepped[2, at, :] = second_step

        pl.loop(0, height // 16)(body)
        for k in range(3):
            writes.append(pltpu.make_async_copy(
                stepped.at[k, pl.ds(top, height), :],
                outs[k].at[pl.ds(start + top, height), :], sems.at[len(writes)],
            ))
            writes[-1].start()
    for write in writes:
        write.wait()


def adam_update(start, size, rows, choices, state, grads, after, filled):
    depth = state.shape[1]
    return call(
        functools.partial(adam_kernel, start, size, bool(filled)), "adam",
        [jax.ShapeDtypeStruct((rows, depth), jnp.float32)] * 3 + [jax.ShapeDtypeStruct((8, 128), jnp.float32)],
        [VMEM] * 6 + [ANY] + [HBM] * len(filled), [HBM] * 3 + [VMEM],
        scratch=[pltpu.VMEM((3, size, depth), jnp.float32), pltpu.SemaphoreType.DMA((3 * (-(-size // 32)),))],
        aliases={7 + k: k for k in range(len(filled))},
    )(choices, state, *grads, after, *filled)


def on_device(n, members, context, out_grad, weight, first, second, rates, decays, steps, donor):
    context_rows = context[0]
    cotangent = out_grad[0]
    scale = context_rows.shape[1] ** (-0.5)
    rows, depth = weight.shape[1:]
    chains = 2 if rows % 32 == 0 else 1
    parts = [(c * rows // chains, rows // chains) for c in range(chains)]
    lower = rows * 112 // 256 // 16 * 16
    steps_of = [(0, lower), (lower, rows - lower)] if chains == 2 and lower else [(0, rows)]
    where = jnp.stack([lax.axis_index("shard"), lax.axis_index("member")]).astype(jnp.int32)

    swap_across = [(m, m ^ 2) for m in range(members)]
    swap_mates = [(m, m ^ 1) for m in range(members)]
    swaps = []
    for swap in range(2):
        pairs = [(s, s + 1) for s in range(swap, n - 1, 2)]
        swaps.append(pairs + [(b, a) for a, b in pairs])

    state, *own = halves(parts, weight[0], first[0], second[0])
    choices = call(
        choices_kernel, "choices", jax.ShapeDtypeStruct((8, depth), jnp.float32), [SMEM] * 5, VMEM
    )(where, rates, decays, steps, donor)
    order = [(slot, swap) for slot in range(2, n + 1) for swap in range(2)]
    terms = partial_blocks(n, scale, parts, order, where, context_rows, cotangent)

    arrived = [[own, own]]
    sent = own[0]
    for slot in range(1, n + 1):
        now = [[], []]
        for c in range(len(parts)):
            blocks = [arrived[-1][1][c], arrived[-1][0][c]]
            if slot > 1:
                blocks = to_send([(blocks[swap], terms[2 * (slot - 2) + swap][c]) for swap in range(2)], sent)
                sent = blocks[0]
            for swap in range(2):
                now[swap].append(lax.ppermute(blocks[swap], "shard", swaps[swap]))
        arrived.append(now)

    mate = lax.ppermute(state, "member", swap_mates)
    across = lax.ppermute(pick(choices, state, mate, terms[0][0]), "member", swap_across)
    states = taken_state(steps_of, where, donor, (weight[0], first[0], second[0]), (mate, across), sent)

    grads, carried = [], ()
    for c, (_, size) in enumerate(parts):
        last = c == len(parts) - 1
        cuts = [steps_of[c][1]] if last else [steps_of[c][1], size - steps_of[c][1]]
        cuts = [cut for cut in cuts if cut]
        sums = summed_grad(terms[-1][c], arrived[n][0][c], arrived[n][1][c], sent, cuts, carried)
        grads.append(sums[0])
        sent, carried = sums[0], tuple(sums[1:])
    blocks = list(own)
    for slot in range(1, n):
        blocks += arrived[slot][0] + arrived[slot][1]
    context_grad, computed = columns(n, scale, parts, where, cotangent, sent, blocks)

    updated = ()
    for c, (start, size) in enumerate(steps_of):
        mate = lax.ppermute(grads[c], "member", swap_mates)
        across = gate(lax.ppermute(grads[c], "member", swap_across), computed)
        far = lax.ppermute(across, "member", swap_mates)
        *updated, computed = adam_update(
            start, size, rows, choices, states[c], (grads[c], mate, across, far), computed, updated
        )
    return (context_grad[None],) + tuple(array[None] for array in updated)


def solution(mesh):
    whole = P(("groups", "member"), "shard", None)
    n, members = mesh.shape["shard"], mesh.shape["member"]
    return jax.shard_map(
        functools.partial(on_device, n, members),
        mesh=mesh,
        in_specs=(whole,) * 5 + (P("groups"),) * 4,
        out_specs=(whole,) * 4,
        check_vma=False,
    )
```

```python
import functools
import math

import jax
import jax.numpy as jnp
from jax import lax
from jax.experimental import pallas as pl
from jax.experimental.pallas import tpu as pltpu
from jax.sharding import PartitionSpec as P

beta_one = 0.9
beta_two = 0.999
epsilon = 1e-08

MIB = 1 << 20
SUM_FLOPS = 5 * 2 ** 28
SMEM = pl.BlockSpec(memory_space=pltpu.SMEM)
VMEM = pl.BlockSpec(memory_space=pltpu.VMEM)
HBM = pl.BlockSpec(memory_space=pltpu.HBM)
ANY = pl.BlockSpec(memory_space=pl.ANY)


def call(kernel, name, out_shape, in_specs, out_specs, limit=8, scratch=(), aliases=None, flops=0):
    return pl.pallas_call(
        kernel,
        out_shape=out_shape,
        in_specs=in_specs,
        out_specs=out_specs,
        scratch_shapes=scratch,
        input_output_aliases=aliases or {},
        compiler_params=pltpu.CompilerParams(vmem_limit_bytes=limit * MIB),
        cost_estimate=pl.CostEstimate(flops=flops, bytes_accessed=1024, transcendentals=0),
        name=name,
    )


def half_array(rows, depth):
    return jax.ShapeDtypeStruct((rows, depth), jnp.bfloat16)


def gate_kernel(value_ref, after_ref, out_ref):
    pass


def gate(value, after):
    return call(gate_kernel, "gate", half_array(*value.shape), [ANY, ANY], ANY, aliases={0: 0})(value, after)


def by_rows(ref, body, step=16):
    @pl.loop(0, ref.shape[0] // step)
    def _(i):
        body(pl.ds(pl.multiple_of(i * step, step), step))


def source_of(member, donor_ref):
    donor = donor_ref[member]
    return jnp.where(donor >= 0, donor, member)


def make_choices(where_ref, rates_ref, decays_ref, steps_ref, donor_ref, out_ref):
    member = where_ref[1]
    source = source_of(member, donor_ref)
    way = jnp.bitwise_xor(source, member)
    partner_source = source_of(jnp.bitwise_xor(member, 2), donor_ref)
    flags = [partner_source == jnp.bitwise_xor(member, 1), way == 0, way == 1, way == 2]
    depth = out_ref.shape[1]
    for k, flag in enumerate(flags):
        out_ref[k:k + 1, :] = jnp.full((1, depth), jnp.where(flag, 1.0, 0.0))
    out_ref[4:5, :] = jnp.full((1, depth), rates_ref[source])
    out_ref[5:6, :] = jnp.full((1, depth), decays_ref[source])
    count = jnp.full((1, depth), (steps_ref[source] + 1).astype(jnp.float32))
    out_ref[6:7, :] = 1.0 / (1.0 - jnp.exp(count * math.log(beta_one)))
    out_ref[7:8, :] = 1.0 / (1.0 - jnp.exp(count * math.log(beta_two)))


def halves_kernel(parts, weight_ref, first_ref, second_ref, *refs):
    tables, (state_ref, choices_ref), own_refs, (full, sems) = refs[:5], refs[5:7], refs[7:-2], refs[-2:]
    rows = weight_ref.shape[0]
    copies = []
    for k, ref in enumerate((weight_ref, first_ref, second_ref)):
        for c, (start, size) in enumerate(parts):
            copies.append(pltpu.make_async_copy(
                ref.at[pl.ds(start, size), :], full.at[k, pl.ds(start, size), :], sems.at[k * len(parts) + c]
            ))
            copies[-1].start()
    make_choices(*tables, choices_ref)
    for k in range(3):
        for c, (start, size) in enumerate(parts):
            copies[k * len(parts) + c].wait()
            rounded = full[k, start:start + size, :].astype(jnp.bfloat16)
            if k == 0:
                own_refs[c][...] = rounded
            state_ref[k * rows + start:k * rows + start + size, :] = rounded


def halves(parts, arrays, tables):
    rows, depth = arrays[0].shape
    shapes = [half_array(3 * rows, depth), jax.ShapeDtypeStruct((8, depth), jnp.float32)]
    shapes += [half_array(size, depth) for _, size in parts]
    return call(
        functools.partial(halves_kernel, parts), "halves",
        shapes, [HBM] * 3 + [SMEM] * 5, [VMEM] * len(shapes), limit=56,
        scratch=[pltpu.VMEM((3, rows, depth), jnp.float32), pltpu.SemaphoreType.DMA((3 * len(parts),))],
    )(*arrays, *tables)


def pick_kernel(choices_ref, own_ref, mate_ref, after_ref, out_ref):
    def body(at):
        wants_mate = jnp.broadcast_to(choices_ref[0:1, :], (16, out_ref.shape[1])) > 0
        own, mate = own_ref[at, :].astype(jnp.float32), mate_ref[at, :].astype(jnp.float32)
        out_ref[at, :] = jnp.where(wants_mate, mate, own).astype(out_ref.dtype)

    by_rows(out_ref, body)


def pick(choices, own, mate, after):
    return call(pick_kernel, "pick", half_array(*own.shape), [VMEM, VMEM, VMEM, ANY], VMEM)(
        choices, own, mate, after
    )


def partial_kernel(n, scale, parts, order, where_ref, context_ref, cotangent_ref, *refs):
    outs, (product, rounded, out_sems) = refs[:-3], refs[-3:]
    width = product.shape[0]
    rows = width // n
    me = where_ref[0]
    even = lax.rem(me, 2) == 0
    tile = min(256, width)
    rounded[width:, :] = jnp.zeros((rows, rounded.shape[1]), rounded.dtype)
    for start in range(0, width, tile):
        block = scale * lax.dot_general(
            context_ref[:, start:start + tile], cotangent_ref[...],
            (((0,), (0,)), ((), ())), preferred_element_type=jnp.float32,
        )
        product[start:start + tile, :] = block
        rounded[start:start + tile, :] = block.astype(rounded.dtype)
    writes = []

    def write(source, first_row, size):
        at = len(writes)
        writes.append(pltpu.make_async_copy(
            source.at[pl.ds(pl.multiple_of(first_row, 16), size), :], outs[at], out_sems.at[at]
        ))
        writes[-1].start()

    for slot, swap in order:
        rightward = even if swap == 0 else jnp.logical_not(even)
        block = lax.rem(me + jnp.where(rightward, n + 1 - slot, slot - 1), n)
        place = jnp.where(rightward, me, n - 1 - me)
        first_row = jnp.where(place >= slot - 1, width, block * rows)
        for start, size in parts:
            write(rounded, first_row + start, size)
    for start, size in parts:
        write(product, me * rows + start, size)
    for copy in writes:
        copy.wait()


def partial_blocks(n, scale, parts, order, where, context_rows, cotangent):
    tokens, width = context_rows.shape
    depth = cotangent.shape[1]
    outs = (len(order) + 1) * len(parts)
    flat = call(
        functools.partial(partial_kernel, n, scale, parts, order), "partial_blocks",
        [half_array(size, depth) for _, size in parts] * len(order)
        + [jax.ShapeDtypeStruct((size, depth), jnp.float32) for _, size in parts],
        [SMEM, VMEM, VMEM], [HBM] * outs, limit=14,
        scratch=[
            pltpu.VMEM((width, depth), jnp.float32),
            pltpu.VMEM((width + width // n, depth), jnp.bfloat16),
            pltpu.SemaphoreType.DMA((outs,)),
        ],
    )(where, context_rows, cotangent)
    return [flat[k * len(parts):(k + 1) * len(parts)] for k in range(len(order) + 1)]


def send_kernel(arrived_ref, term_ref, arrived_too_ref, term_too_ref, after_ref, out_ref, out_too_ref):
    def body(at):
        total = arrived_ref[at, :].astype(jnp.float32) + term_ref[at, :].astype(jnp.float32)
        out_ref[at, :] = total.astype(out_ref.dtype)
        total = arrived_too_ref[at, :].astype(jnp.float32) + term_too_ref[at, :].astype(jnp.float32)
        out_too_ref[at, :] = total.astype(out_too_ref.dtype)

    by_rows(out_ref, body)


def to_send(pairs, after):
    like = half_array(*pairs[0][0].shape)
    return call(send_kernel, "to_send", [like] * 2, [VMEM] * 4 + [ANY], [VMEM] * 2, flops=SUM_FLOPS)(
        *pairs[0], *pairs[1], after
    )


def grad_kernel(cuts, own_ref, one_ref, other_ref, after_ref, *refs):
    def body(at):
        arrived = one_ref[at, :].astype(jnp.float32) + other_ref[at, :].astype(jnp.float32)
        return (own_ref[at, :] + arrived).astype(jnp.bfloat16)

    first = 0
    carried = refs[0] if len(refs) > len(cuts) else None
    for out_ref, size in zip(refs[len(refs) - len(cuts):], cuts):
        top = 0
        if carried is not None:
            top = carried.shape[0]
            out_ref[0:top, :] = carried[...]

        @pl.loop(0, (size - top) // 16)
        def _(i):
            out_ref[pl.ds(pl.multiple_of(top + i * 16, 16), 16), :] = body(
                pl.ds(pl.multiple_of(first + i * 16, 16), 16)
            )

        first, carried = first + size - top, None


def summed_grad(own, one, other, after, cuts, carried=()):
    depth = one.shape[1]
    return call(
        functools.partial(grad_kernel, cuts), "summed_grad", [half_array(size, depth) for size in cuts],
        [VMEM] * 3 + [ANY] + [VMEM] * len(carried), [VMEM] * len(cuts),
    )(own, one, other, after, *carried)


def columns_kernel(n, scale, parts, where_ref, cotangent_ref, after_ref, *refs):
    blocks, (out_ref, token_ref, full, result, out_sems) = refs[:-5], refs[-5:]
    token_ref[...] = jnp.zeros_like(token_ref)
    width = full.shape[0]
    rows = width // n
    me = where_ref[0]
    even = lax.rem(me, 2) == 0
    for k in range(2 * n - 1):
        slot, swap = (k + 1) // 2, (k + 1) % 2
        shard = me + (jnp.where(even, slot, -slot) if swap == 0 else jnp.where(even, -slot, slot))

        @pl.when(jnp.logical_and(shard >= 0, shard < n))
        def _():
            for c, (start, size) in enumerate(parts):
                first_row = pl.multiple_of(shard * rows + start, 16)
                full[pl.ds(first_row, size), :] = blocks[k * len(parts) + c][...]
    tile = min(256, width)
    writes = []
    for i, start in enumerate(range(0, width, tile)):
        result[:, start:start + tile] = (scale * lax.dot_general(
            cotangent_ref[...], full[start:start + tile, :],
            (((1,), (1,)), ((), ())), preferred_element_type=jnp.float32,
        )).astype(out_ref.dtype)
        at = pl.ds(start, tile)
        writes.append(pltpu.make_async_copy(result.at[:, at], out_ref.at[:, at], out_sems.at[i]))
        writes[-1].start()
    for write in writes:
        write.wait()


def columns(n, scale, parts, where, cotangent, after, blocks):
    tokens, depth = cotangent.shape
    width = n * sum(size for _, size in parts)
    return call(
        functools.partial(columns_kernel, n, scale, parts), "context_grad",
        [half_array(tokens, width), jax.ShapeDtypeStruct((8, 128), jnp.float32)],
        [SMEM, VMEM, ANY] + [VMEM] * len(blocks), [HBM, VMEM], limit=14,
        scratch=[
            pltpu.VMEM((width, depth), cotangent.dtype),
            pltpu.VMEM((tokens, width), cotangent.dtype),
            pltpu.SemaphoreType.DMA((width // min(256, width),)),
        ],
    )(where, cotangent, after, *blocks)


def state_kernel(parts, where_ref, donor_ref, after_ref, *refs):
    own, (mate_ref, across_ref), refs = refs[:3], refs[3:5], refs[5:]
    outs, (taken, sems) = refs[:-2], refs[-2:]
    rows = own[0].shape[0]
    member = where_ref[1]
    way = jnp.bitwise_xor(source_of(member, donor_ref), member)

    @pl.when(way == 0)
    def _():
        copies = []
        for c, (start, size) in enumerate(parts):
            for k in range(3):
                copies.append(pltpu.make_async_copy(
                    own[k].at[pl.ds(start, size), :], outs[c].at[pl.ds(k * size, size), :], sems.at[c * 3 + k]
                ))
                copies[-1].start()
        for copy in copies:
            copy.wait()

    def widen(ref):
        copies = []
        for k in range(3):
            at = pl.ds(k * rows, rows)
            copies.append(pltpu.make_async_copy(ref.at[at, :], taken.at[at, :], sems.at[k]))
            copies[-1].start()
        for k in range(3):
            copies[k].wait()
            for c, (start, size) in enumerate(parts):
                first_row = k * rows + start
                outs[c][k * size:(k + 1) * size, :] = taken[first_row:first_row + size, :].astype(jnp.float32)

    pl.when(way == 1)(lambda: widen(mate_ref))
    pl.when(way > 1)(lambda: widen(across_ref))


def taken_state(parts, where, donor, own, donated, after):
    rows, depth = own[0].shape
    return call(
        functools.partial(state_kernel, parts), "taken_state",
        [jax.ShapeDtypeStruct((3 * size, depth), jnp.float32) for _, size in parts],
        [SMEM, SMEM, ANY] + [HBM] * 3 + [ANY] * 2, [VMEM] * len(parts),
        scratch=[pltpu.VMEM((3 * rows, depth), jnp.bfloat16), pltpu.SemaphoreType.DMA((3 * len(parts),))],
    )(where, donor, after, *own, *donated)


def adam_kernel(start, size, filled, choices_ref, state_ref, own_ref, mate_ref, across_ref, far_ref, after_ref, *refs):
    refs = refs[3 if filled else 0:]
    outs, (token_ref, stepped, sems) = refs[:3], refs[3:]
    token_ref[...] = jnp.zeros_like(token_ref)
    depth = own_ref.shape[1]
    writes = []
    piece = 32
    for top in range(0, size, piece):
        height = min(piece, size - top)

        def body(i):
            at = pl.ds(pl.multiple_of(top + i * 16, 16), 16)
            row = lambda k: jnp.broadcast_to(choices_ref[k:k + 1, :], (16, depth))
            load = lambda k: state_ref[pl.ds(pl.multiple_of(k * size + top + i * 16, 16), 16), :]
            g = far_ref[at, :].astype(jnp.float32)
            for k, ref in ((1, own_ref), (2, mate_ref), (3, across_ref)):
                g = jnp.where(row(k) > 0, ref[at, :].astype(jnp.float32), g)
            w = load(0)
            first_step = beta_one * load(1) + (1.0 - beta_one) * g
            second_step = beta_two * load(2) + (1.0 - beta_two) * g * g
            ratio = (first_step * row(6)) / (jnp.sqrt(second_step * row(7)) + epsilon)
            stepped[0, at, :] = w - row(4) * (ratio + row(5) * w)
            stepped[1, at, :] = first_step
            stepped[2, at, :] = second_step

        pl.loop(0, height // 16)(body)
        for k in range(3):
            writes.append(pltpu.make_async_copy(
                stepped.at[k, pl.ds(top, height), :],
                outs[k].at[pl.ds(start + top, height), :], sems.at[len(writes)],
            ))
            writes[-1].start()
    for write in writes:
        write.wait()


def adam_update(start, size, rows, choices, state, grads, after, filled):
    depth = state.shape[1]
    return call(
        functools.partial(adam_kernel, start, size, bool(filled)), "adam",
        [jax.ShapeDtypeStruct((rows, depth), jnp.float32)] * 3 + [jax.ShapeDtypeStruct((8, 128), jnp.float32)],
        [VMEM] * 6 + [ANY] + [HBM] * len(filled), [HBM] * 3 + [VMEM],
        scratch=[pltpu.VMEM((3, size, depth), jnp.float32), pltpu.SemaphoreType.DMA((3 * (-(-size // 32)),))],
        aliases={7 + k: k for k in range(len(filled))},
    )(choices, state, *grads, after, *filled)


def on_device(n, members, context, out_grad, weight, first, second, rates, decays, steps, donor):
    context_rows = context[0]
    cotangent = out_grad[0]
    scale = context_rows.shape[1] ** (-0.5)
    rows, depth = weight.shape[1:]
    chains = 2 if rows % 32 == 0 else 1
    parts = [(c * rows // chains, rows // chains) for c in range(chains)]
    lower = rows * 112 // 256 // 16 * 16
    steps_of = [(0, lower), (lower, rows - lower)] if chains == 2 and lower else [(0, rows)]
    where = jnp.stack([lax.axis_index("shard"), lax.axis_index("member")]).astype(jnp.int32)

    swap_across = [(m, m ^ 2) for m in range(members)]
    swap_mates = [(m, m ^ 1) for m in range(members)]
    swaps = []
    for swap in range(2):
        pairs = [(s, s + 1) for s in range(swap, n - 1, 2)]
        swaps.append(pairs + [(b, a) for a, b in pairs])

    arrays = (weight[0], first[0], second[0])
    state, choices, *own = halves(parts, arrays, (where, rates, decays, steps, donor))
    order = [(slot, swap) for slot in range(2, n + 1) for swap in range(2)]
    terms = partial_blocks(n, scale, parts, order, where, context_rows, cotangent)

    arrived = [[own, own]]
    sent = own[0]
    for slot in range(1, n + 1):
        now = [[], []]
        for c in range(len(parts)):
            blocks = [arrived[-1][1][c], arrived[-1][0][c]]
            if slot > 1:
                blocks = to_send([(blocks[swap], terms[2 * (slot - 2) + swap][c]) for swap in range(2)], sent)
                sent = blocks[0]
            for swap in range(2):
                now[swap].append(lax.ppermute(blocks[swap], "shard", swaps[swap]))
        arrived.append(now)

    mate = lax.ppermute(state, "member", swap_mates)
    across = lax.ppermute(pick(choices, state, mate, terms[0][0]), "member", swap_across)
    states = taken_state(steps_of, where, donor, arrays, (mate, across), sent)

    grads, carried = [], ()
    for c, (_, size) in enumerate(parts):
        last = c == len(parts) - 1
        cuts = [steps_of[c][1]] if last else [steps_of[c][1], size - steps_of[c][1]]
        cuts = [cut for cut in cuts if cut]
        sums = summed_grad(terms[-1][c], arrived[n][0][c], arrived[n][1][c], sent, cuts, carried)
        grads.append(sums[0])
        sent, carried = sums[0], tuple(sums[1:])
    blocks = list(own)
    for slot in range(1, n):
        blocks += arrived[slot][0] + arrived[slot][1]
    context_grad, computed = columns(n, scale, parts, where, cotangent, sent, blocks)

    updated = ()
    for c, (start, size) in enumerate(steps_of):
        mate = lax.ppermute(grads[c], "member", swap_mates)
        across = gate(lax.ppermute(grads[c], "member", swap_across), computed)
        far = lax.ppermute(across, "member", swap_mates)
        *updated, computed = adam_update(
            start, size, rows, choices, states[c], (grads[c], mate, across, far), computed, updated
        )
    return (context_grad[None],) + tuple(array[None] for array in updated)


def solution(mesh):
    whole = P(("groups", "member"), "shard", None)
    n, members = mesh.shape["shard"], mesh.shape["member"]
    return jax.shard_map(
        functools.partial(on_device, n, members),
        mesh=mesh,
        in_specs=(whole,) * 5 + (P("groups"),) * 4,
        out_specs=(whole,) * 4,
        check_vma=False,
    )
```

```python
import functools
import math

import jax
import jax.numpy as jnp
from jax import lax
from jax.experimental import pallas as pl
from jax.experimental.pallas import tpu as pltpu
from jax.sharding import PartitionSpec as P

beta_one = 0.9
beta_two = 0.999
epsilon = 1e-08

MIB = 1 << 20
SUM_FLOPS = 5 * 2 ** 28
SMEM = pl.BlockSpec(memory_space=pltpu.SMEM)
VMEM = pl.BlockSpec(memory_space=pltpu.VMEM)
HBM = pl.BlockSpec(memory_space=pltpu.HBM)
ANY = pl.BlockSpec(memory_space=pl.ANY)


def call(kernel, name, out_shape, in_specs, out_specs, limit=8, scratch=(), aliases=None, flops=0):
    return pl.pallas_call(
        kernel,
        out_shape=out_shape,
        in_specs=in_specs,
        out_specs=out_specs,
        scratch_shapes=scratch,
        input_output_aliases=aliases or {},
        compiler_params=pltpu.CompilerParams(vmem_limit_bytes=limit * MIB),
        cost_estimate=pl.CostEstimate(flops=flops, bytes_accessed=1024, transcendentals=0),
        name=name,
    )


def half_array(rows, depth):
    return jax.ShapeDtypeStruct((rows, depth), jnp.bfloat16)


def gate_kernel(value_ref, after_ref, out_ref):
    pass


def gate(value, after):
    return call(gate_kernel, "gate", half_array(*value.shape), [ANY, ANY], ANY, aliases={0: 0})(value, after)


def by_rows(ref, body, step=16):
    @pl.loop(0, ref.shape[0] // step)
    def _(i):
        body(pl.ds(pl.multiple_of(i * step, step), step))


def source_of(member, donor_ref):
    donor = donor_ref[member]
    return jnp.where(donor >= 0, donor, member)


def make_choices(where_ref, rates_ref, decays_ref, steps_ref, donor_ref, out_ref):
    member = where_ref[1]
    source = source_of(member, donor_ref)
    way = jnp.bitwise_xor(source, member)
    partner_source = source_of(jnp.bitwise_xor(member, 2), donor_ref)
    flags = [partner_source == jnp.bitwise_xor(member, 1), way == 0, way == 1, way == 2]
    depth = out_ref.shape[1]
    for k, flag in enumerate(flags):
        out_ref[k:k + 1, :] = jnp.full((1, depth), jnp.where(flag, 1.0, 0.0))
    out_ref[4:5, :] = jnp.full((1, depth), rates_ref[source])
    out_ref[5:6, :] = jnp.full((1, depth), decays_ref[source])
    count = jnp.full((1, depth), (steps_ref[source] + 1).astype(jnp.float32))
    out_ref[6:7, :] = 1.0 / (1.0 - jnp.exp(count * math.log(beta_one)))
    out_ref[7:8, :] = 1.0 / (1.0 - jnp.exp(count * math.log(beta_two)))


def halves_kernel(parts, weight_ref, first_ref, second_ref, *refs):
    state_ref, own_refs, (full, sems) = refs[0], refs[1:-2], refs[-2:]
    rows = weight_ref.shape[0]
    copies = []
    for k, ref in enumerate((weight_ref, first_ref, second_ref)):
        for c, (start, size) in enumerate(parts):
            copies.append(pltpu.make_async_copy(
                ref.at[pl.ds(start, size), :], full.at[k, pl.ds(start, size), :], sems.at[k * len(parts) + c]
            ))
            copies[-1].start()
    for k in range(3):
        for c, (start, size) in enumerate(parts):
            copies[k * len(parts) + c].wait()
            rounded = full[k, start:start + size, :].astype(jnp.bfloat16)
            if k == 0:
                own_refs[c][...] = rounded
            state_ref[k * rows + start:k * rows + start + size, :] = rounded


def halves(parts, arrays):
    rows, depth = arrays[0].shape
    shapes = [half_array(3 * rows, depth)] + [half_array(size, depth) for _, size in parts]
    return call(
        functools.partial(halves_kernel, parts), "halves",
        shapes, [HBM] * 3, [VMEM] * len(shapes), limit=56,
        scratch=[pltpu.VMEM((3, rows, depth), jnp.float32), pltpu.SemaphoreType.DMA((3 * len(parts),))],
    )(*arrays)


def pick_kernel(choices_ref, own_ref, mate_ref, after_ref, out_ref):
    def body(at):
        wants_mate = jnp.broadcast_to(choices_ref[0:1, :], (16, out_ref.shape[1])) > 0
        own, mate = own_ref[at, :].astype(jnp.float32), mate_ref[at, :].astype(jnp.float32)
        out_ref[at, :] = jnp.where(wants_mate, mate, own).astype(out_ref.dtype)

    by_rows(out_ref, body)


def pick(choices, own, mate, after):
    return call(pick_kernel, "pick", half_array(*own.shape), [VMEM, VMEM, VMEM, ANY], VMEM)(
        choices, own, mate, after
    )


def partial_kernel(n, scale, parts, order, context_ref, cotangent_ref, where_ref, *refs):
    tables, choices_ref, outs, (product, rounded, out_sems) = refs[:4], refs[4], refs[5:-3], refs[-3:]
    width = product.shape[0]
    rows = width // n
    me = where_ref[0]
    even = lax.rem(me, 2) == 0
    tile = min(256, width)
    rounded[width:, :] = jnp.zeros((rows, rounded.shape[1]), rounded.dtype)
    for start in range(0, width, tile):
        block = scale * lax.dot_general(
            context_ref[:, start:start + tile], cotangent_ref[...],
            (((0,), (0,)), ((), ())), preferred_element_type=jnp.float32,
        )
        product[start:start + tile, :] = block
        rounded[start:start + tile, :] = block.astype(rounded.dtype)
    writes = []

    def write(source, first_row, size):
        at = len(writes)
        writes.append(pltpu.make_async_copy(
            source.at[pl.ds(pl.multiple_of(first_row, 16), size), :], outs[at], out_sems.at[at]
        ))
        writes[-1].start()

    for slot, swap in order:
        rightward = even if swap == 0 else jnp.logical_not(even)
        block = lax.rem(me + jnp.where(rightward, n + 1 - slot, slot - 1), n)
        place = jnp.where(rightward, me, n - 1 - me)
        first_row = jnp.where(place >= slot - 1, width, block * rows)
        for start, size in parts:
            write(rounded, first_row + start, size)
    for start, size in parts:
        write(product, me * rows + start, size)
    make_choices(where_ref, *tables, choices_ref)
    for copy in writes:
        copy.wait()


def partial_blocks(n, scale, parts, order, context_rows, cotangent, tables):
    tokens, width = context_rows.shape
    depth = cotangent.shape[1]
    outs = (len(order) + 1) * len(parts)
    choices, *flat = call(
        functools.partial(partial_kernel, n, scale, parts, order), "partial_blocks",
        [jax.ShapeDtypeStruct((8, depth), jnp.float32)]
        + [half_array(size, depth) for _, size in parts] * len(order)
        + [jax.ShapeDtypeStruct((size, depth), jnp.float32) for _, size in parts],
        [VMEM] * 2 + [SMEM] * 5, [VMEM] + [HBM] * outs, limit=14,
        scratch=[
            pltpu.VMEM((width, depth), jnp.float32),
            pltpu.VMEM((width + width // n, depth), jnp.bfloat16),
            pltpu.SemaphoreType.DMA((outs,)),
        ],
    )(context_rows, cotangent, *tables)
    return choices, [flat[k * len(parts):(k + 1) * len(parts)] for k in range(len(order) + 1)]


def send_kernel(arrived_ref, term_ref, arrived_too_ref, term_too_ref, after_ref, out_ref, out_too_ref):
    def body(at):
        total = arrived_ref[at, :].astype(jnp.float32) + term_ref[at, :].astype(jnp.float32)
        out_ref[at, :] = total.astype(out_ref.dtype)
        total = arrived_too_ref[at, :].astype(jnp.float32) + term_too_ref[at, :].astype(jnp.float32)
        out_too_ref[at, :] = total.astype(out_too_ref.dtype)

    by_rows(out_ref, body)


def to_send(pairs, after):
    like = half_array(*pairs[0][0].shape)
    return call(send_kernel, "to_send", [like] * 2, [VMEM] * 4 + [ANY], [VMEM] * 2, flops=SUM_FLOPS)(
        *pairs[0], *pairs[1], after
    )


def grad_kernel(cuts, own_ref, one_ref, other_ref, after_ref, *refs):
    def body(at):
        arrived = one_ref[at, :].astype(jnp.float32) + other_ref[at, :].astype(jnp.float32)
        return (own_ref[at, :] + arrived).astype(jnp.bfloat16)

    first = 0
    carried = refs[0] if len(refs) > len(cuts) else None
    for out_ref, size in zip(refs[len(refs) - len(cuts):], cuts):
        top = 0
        if carried is not None:
            top = carried.shape[0]
            out_ref[0:top, :] = carried[...]

        @pl.loop(0, (size - top) // 16)
        def _(i):
            out_ref[pl.ds(pl.multiple_of(top + i * 16, 16), 16), :] = body(
                pl.ds(pl.multiple_of(first + i * 16, 16), 16)
            )

        first, carried = first + size - top, None


def summed_grad(own, one, other, after, cuts, carried=()):
    depth = one.shape[1]
    return call(
        functools.partial(grad_kernel, cuts), "summed_grad", [half_array(size, depth) for size in cuts],
        [VMEM] * 3 + [ANY] + [VMEM] * len(carried), [VMEM] * len(cuts),
    )(own, one, other, after, *carried)


def columns_kernel(n, scale, parts, where_ref, cotangent_ref, after_ref, *refs):
    blocks, (out_ref, token_ref, full, result, out_sems) = refs[:-5], refs[-5:]
    token_ref[...] = jnp.zeros_like(token_ref)
    width = full.shape[0]
    rows = width // n
    me = where_ref[0]
    even = lax.rem(me, 2) == 0
    for k in range(2 * n - 1):
        slot, swap = (k + 1) // 2, (k + 1) % 2
        shard = me + (jnp.where(even, slot, -slot) if swap == 0 else jnp.where(even, -slot, slot))

        @pl.when(jnp.logical_and(shard >= 0, shard < n))
        def _():
            for c, (start, size) in enumerate(parts):
                first_row = pl.multiple_of(shard * rows + start, 16)
                full[pl.ds(first_row, size), :] = blocks[k * len(parts) + c][...]
    tile = min(256, width)
    writes = []
    for i, start in enumerate(range(0, width, tile)):
        result[:, start:start + tile] = (scale * lax.dot_general(
            cotangent_ref[...], full[start:start + tile, :],
            (((1,), (1,)), ((), ())), preferred_element_type=jnp.float32,
        )).astype(out_ref.dtype)
        at = pl.ds(start, tile)
        writes.append(pltpu.make_async_copy(result.at[:, at], out_ref.at[:, at], out_sems.at[i]))
        writes[-1].start()
    for write in writes:
        write.wait()


def columns(n, scale, parts, where, cotangent, after, blocks):
    tokens, depth = cotangent.shape
    width = n * sum(size for _, size in parts)
    return call(
        functools.partial(columns_kernel, n, scale, parts), "context_grad",
        [half_array(tokens, width), jax.ShapeDtypeStruct((8, 128), jnp.float32)],
        [SMEM, VMEM, ANY] + [VMEM] * len(blocks), [HBM, VMEM], limit=14,
        scratch=[
            pltpu.VMEM((width, depth), cotangent.dtype),
            pltpu.VMEM((tokens, width), cotangent.dtype),
            pltpu.SemaphoreType.DMA((width // min(256, width),)),
        ],
    )(where, cotangent, after, *blocks)


def state_kernel(parts, where_ref, donor_ref, after_ref, *refs):
    own, (mate_ref, across_ref), refs = refs[:3], refs[3:5], refs[5:]
    outs, (taken, sems) = refs[:-2], refs[-2:]
    rows = own[0].shape[0]
    member = where_ref[1]
    way = jnp.bitwise_xor(source_of(member, donor_ref), member)

    @pl.when(way == 0)
    def _():
        copies = []
        for c, (start, size) in enumerate(parts):
            for k in range(3):
                copies.append(pltpu.make_async_copy(
                    own[k].at[pl.ds(start, size), :], outs[c].at[pl.ds(k * size, size), :], sems.at[c * 3 + k]
                ))
                copies[-1].start()
        for copy in copies:
            copy.wait()

    def widen(ref):
        copies = []
        for k in range(3):
            at = pl.ds(k * rows, rows)
            copies.append(pltpu.make_async_copy(ref.at[at, :], taken.at[at, :], sems.at[k]))
            copies[-1].start()
        for k in range(3):
            copies[k].wait()
            for c, (start, size) in enumerate(parts):
                first_row = k * rows + start
                outs[c][k * size:(k + 1) * size, :] = taken[first_row:first_row + size, :].astype(jnp.float32)

    pl.when(way == 1)(lambda: widen(mate_ref))
    pl.when(way > 1)(lambda: widen(across_ref))


def taken_state(parts, where, donor, own, donated, after):
    rows, depth = own[0].shape
    return call(
        functools.partial(state_kernel, parts), "taken_state",
        [jax.ShapeDtypeStruct((3 * size, depth), jnp.float32) for _, size in parts],
        [SMEM, SMEM, ANY] + [HBM] * 3 + [ANY] * 2, [VMEM] * len(parts),
        scratch=[pltpu.VMEM((3 * rows, depth), jnp.bfloat16), pltpu.SemaphoreType.DMA((3 * len(parts),))],
    )(where, donor, after, *own, *donated)


def adam_kernel(start, size, filled, choices_ref, state_ref, own_ref, mate_ref, across_ref, far_ref, after_ref, *refs):
    refs = refs[3 if filled else 0:]
    outs, (token_ref, stepped, sems) = refs[:3], refs[3:]
    token_ref[...] = jnp.zeros_like(token_ref)
    depth = own_ref.shape[1]
    writes = []
    piece = 32
    for top in range(0, size, piece):
        height = min(piece, size - top)

        def body(i):
            at = pl.ds(pl.multiple_of(top + i * 16, 16), 16)
            row = lambda k: jnp.broadcast_to(choices_ref[k:k + 1, :], (16, depth))
            load = lambda k: state_ref[pl.ds(pl.multiple_of(k * size + top + i * 16, 16), 16), :]
            g = far_ref[at, :].astype(jnp.float32)
            for k, ref in ((1, own_ref), (2, mate_ref), (3, across_ref)):
                g = jnp.where(row(k) > 0, ref[at, :].astype(jnp.float32), g)
            w = load(0)
            first_step = beta_one * load(1) + (1.0 - beta_one) * g
            second_step = beta_two * load(2) + (1.0 - beta_two) * g * g
            ratio = (first_step * row(6)) / (jnp.sqrt(second_step * row(7)) + epsilon)
            stepped[0, at, :] = w - row(4) * (ratio + row(5) * w)
            stepped[1, at, :] = first_step
            stepped[2, at, :] = second_step

        pl.loop(0, height // 16)(body)
        for k in range(3):
            writes.append(pltpu.make_async_copy(
                stepped.at[k, pl.ds(top, height), :],
                outs[k].at[pl.ds(start + top, height), :], sems.at[len(writes)],
            ))
            writes[-1].start()
    for write in writes:
        write.wait()


def adam_update(start, size, rows, choices, state, grads, after, filled):
    depth = state.shape[1]
    return call(
        functools.partial(adam_kernel, start, size, bool(filled)), "adam",
        [jax.ShapeDtypeStruct((rows, depth), jnp.float32)] * 3 + [jax.ShapeDtypeStruct((8, 128), jnp.float32)],
        [VMEM] * 6 + [ANY] + [HBM] * len(filled), [HBM] * 3 + [VMEM],
        scratch=[pltpu.VMEM((3, size, depth), jnp.float32), pltpu.SemaphoreType.DMA((3 * (-(-size // 32)),))],
        aliases={7 + k: k for k in range(len(filled))},
    )(choices, state, *grads, after, *filled)


def on_device(n, members, context, out_grad, weight, first, second, rates, decays, steps, donor):
    context_rows = context[0]
    cotangent = out_grad[0]
    scale = context_rows.shape[1] ** (-0.5)
    rows, depth = weight.shape[1:]
    chains = 2 if rows % 32 == 0 else 1
    parts = [(c * rows // chains, rows // chains) for c in range(chains)]
    lower = rows * 112 // 256 // 16 * 16
    steps_of = [(0, lower), (lower, rows - lower)] if chains == 2 and lower else [(0, rows)]
    where = jnp.stack([lax.axis_index("shard"), lax.axis_index("member")]).astype(jnp.int32)

    swap_across = [(m, m ^ 2) for m in range(members)]
    swap_mates = [(m, m ^ 1) for m in range(members)]
    swaps = []
    for swap in range(2):
        pairs = [(s, s + 1) for s in range(swap, n - 1, 2)]
        swaps.append(pairs + [(b, a) for a, b in pairs])

    arrays = (weight[0], first[0], second[0])
    state, *own = halves(parts, arrays)
    order = [(slot, swap) for slot in range(2, n + 1) for swap in range(2)]
    tables = (where, rates, decays, steps, donor)
    choices, terms = partial_blocks(n, scale, parts, order, context_rows, cotangent, tables)

    arrived = [[own, own]]
    sent = own[0]
    for slot in range(1, n + 1):
        now = [[], []]
        for c in range(len(parts)):
            blocks = [arrived[-1][1][c], arrived[-1][0][c]]
            if slot > 1:
                blocks = to_send([(blocks[swap], terms[2 * (slot - 2) + swap][c]) for swap in range(2)], sent)
                sent = blocks[0]
            for swap in range(2):
                now[swap].append(lax.ppermute(blocks[swap], "shard", swaps[swap]))
        arrived.append(now)

    mate = lax.ppermute(state, "member", swap_mates)
    across = lax.ppermute(pick(choices, state, mate, terms[0][0]), "member", swap_across)
    states = taken_state(steps_of, where, donor, arrays, (mate, across), sent)

    grads, carried = [], ()
    for c, (_, size) in enumerate(parts):
        last = c == len(parts) - 1
        cuts = [steps_of[c][1]] if last else [steps_of[c][1], size - steps_of[c][1]]
        cuts = [cut for cut in cuts if cut]
        sums = summed_grad(terms[-1][c], arrived[n][0][c], arrived[n][1][c], sent, cuts, carried)
        grads.append(sums[0])
        sent, carried = sums[0], tuple(sums[1:])
    blocks = list(own)
    for slot in range(1, n):
        blocks += arrived[slot][0] + arrived[slot][1]
    context_grad, computed = columns(n, scale, parts, where, cotangent, sent, blocks)

    updated = ()
    for c, (start, size) in enumerate(steps_of):
        mate = lax.ppermute(grads[c], "member", swap_mates)
        across = gate(lax.ppermute(grads[c], "member", swap_across), computed)
        far = lax.ppermute(across, "member", swap_mates)
        *updated, computed = adam_update(
            start, size, rows, choices, states[c], (grads[c], mate, across, far), computed, updated
        )
    return (context_grad[None],) + tuple(array[None] for array in updated)


def solution(mesh):
    whole = P(("groups", "member"), "shard", None)
    n, members = mesh.shape["shard"], mesh.shape["member"]
    return jax.shard_map(
        functools.partial(on_device, n, members),
        mesh=mesh,
        in_specs=(whole,) * 5 + (P("groups"),) * 4,
        out_specs=(whole,) * 4,
        check_vma=False,
    )
```

```python
import functools
import math

import jax
import jax.numpy as jnp
from jax import lax
from jax.experimental import pallas as pl
from jax.experimental.pallas import tpu as pltpu
from jax.sharding import PartitionSpec as P

beta_one = 0.9
beta_two = 0.999
epsilon = 1e-08

MIB = 1 << 20
SUM_FLOPS = 5 * 2 ** 28
SMEM = pl.BlockSpec(memory_space=pltpu.SMEM)
VMEM = pl.BlockSpec(memory_space=pltpu.VMEM)
HBM = pl.BlockSpec(memory_space=pltpu.HBM)
ANY = pl.BlockSpec(memory_space=pl.ANY)


def call(kernel, name, out_shape, in_specs, out_specs, limit=8, scratch=(), aliases=None, flops=0):
    return pl.pallas_call(
        kernel,
        out_shape=out_shape,
        in_specs=in_specs,
        out_specs=out_specs,
        scratch_shapes=scratch,
        input_output_aliases=aliases or {},
        compiler_params=pltpu.CompilerParams(vmem_limit_bytes=limit * MIB),
        cost_estimate=pl.CostEstimate(flops=flops, bytes_accessed=1024, transcendentals=0),
        name=name,
    )


def half_array(rows, depth):
    return jax.ShapeDtypeStruct((rows, depth), jnp.bfloat16)


def gate_kernel(value_ref, after_ref, *out_refs):
    size = out_refs[0].shape[0]
    for k, out_ref in enumerate(out_refs):
        out_ref[...] = value_ref[k * size:(k + 1) * size, :]


def gate(value, after, count):
    rows, depth = value.shape
    return call(gate_kernel, "gate", [half_array(rows // count, depth)] * count, [VMEM, ANY], [VMEM] * count)(
        value, after
    )


def by_rows(ref, body, step=16):
    @pl.loop(0, ref.shape[0] // step)
    def _(i):
        body(pl.ds(pl.multiple_of(i * step, step), step))


def source_of(member, donor_ref):
    donor = donor_ref[member]
    return jnp.where(donor >= 0, donor, member)


def make_choices(where_ref, rates_ref, decays_ref, steps_ref, donor_ref, out_ref):
    member = where_ref[1]
    source = source_of(member, donor_ref)
    way = jnp.bitwise_xor(source, member)
    partner_source = source_of(jnp.bitwise_xor(member, 2), donor_ref)
    flags = [partner_source == jnp.bitwise_xor(member, 1), way == 0, way == 1, way == 2]
    depth = out_ref.shape[1]
    for k, flag in enumerate(flags):
        out_ref[k:k + 1, :] = jnp.full((1, depth), jnp.where(flag, 1.0, 0.0))
    out_ref[4:5, :] = jnp.full((1, depth), rates_ref[source])
    out_ref[5:6, :] = jnp.full((1, depth), decays_ref[source])
    count = jnp.full((1, depth), (steps_ref[source] + 1).astype(jnp.float32))
    out_ref[6:7, :] = 1.0 / (1.0 - jnp.exp(count * math.log(beta_one)))
    out_ref[7:8, :] = 1.0 / (1.0 - jnp.exp(count * math.log(beta_two)))


def halves_kernel(parts, weight_ref, first_ref, second_ref, *refs):
    state_ref, own_refs, (full, sems) = refs[0], refs[1:-2], refs[-2:]
    rows = weight_ref.shape[0]
    copies = []
    for k, ref in enumerate((weight_ref, first_ref, second_ref)):
        for c, (start, size) in enumerate(parts):
            copies.append(pltpu.make_async_copy(
                ref.at[pl.ds(start, size), :], full.at[k, pl.ds(start, size), :], sems.at[k * len(parts) + c]
            ))
            copies[-1].start()
    for k in range(3):
        for c, (start, size) in enumerate(parts):
            copies[k * len(parts) + c].wait()
            rounded = full[k, start:start + size, :].astype(jnp.bfloat16)
            if k == 0:
                own_refs[c][...] = rounded
            state_ref[k * rows + start:k * rows + start + size, :] = rounded


def halves(parts, arrays):
    rows, depth = arrays[0].shape
    shapes = [half_array(3 * rows, depth)] + [half_array(size, depth) for _, size in parts]
    return call(
        functools.partial(halves_kernel, parts), "halves",
        shapes, [HBM] * 3, [VMEM] * len(shapes), limit=56,
        scratch=[pltpu.VMEM((3, rows, depth), jnp.float32), pltpu.SemaphoreType.DMA((3 * len(parts),))],
    )(*arrays)


def pick_kernel(choices_ref, own_ref, mate_ref, after_ref, out_ref):
    def body(at):
        wants_mate = jnp.broadcast_to(choices_ref[0:1, :], (16, out_ref.shape[1])) > 0
        own, mate = own_ref[at, :].astype(jnp.float32), mate_ref[at, :].astype(jnp.float32)
        out_ref[at, :] = jnp.where(wants_mate, mate, own).astype(out_ref.dtype)

    by_rows(out_ref, body)


def pick(choices, own, mate, after):
    return call(pick_kernel, "pick", half_array(*own.shape), [VMEM, VMEM, VMEM, ANY], VMEM)(
        choices, own, mate, after
    )


def partial_kernel(n, scale, parts, order, context_ref, cotangent_ref, where_ref, *refs):
    tables, choices_ref, outs, (product, rounded, out_sems) = refs[:4], refs[4], refs[5:-3], refs[-3:]
    width = product.shape[0]
    rows = width // n
    me = where_ref[0]
    even = lax.rem(me, 2) == 0
    tile = min(256, width)
    rounded[width:, :] = jnp.zeros((rows, rounded.shape[1]), rounded.dtype)
    for start in range(0, width, tile):
        block = scale * lax.dot_general(
            context_ref[:, start:start + tile], cotangent_ref[...],
            (((0,), (0,)), ((), ())), preferred_element_type=jnp.float32,
        )
        product[start:start + tile, :] = block
        rounded[start:start + tile, :] = block.astype(rounded.dtype)
    writes = []

    def write(source, first_row, size):
        at = len(writes)
        writes.append(pltpu.make_async_copy(
            source.at[pl.ds(pl.multiple_of(first_row, 16), size), :], outs[at], out_sems.at[at]
        ))
        writes[-1].start()

    for slot, swap in order:
        rightward = even if swap == 0 else jnp.logical_not(even)
        block = lax.rem(me + jnp.where(rightward, n + 1 - slot, slot - 1), n)
        place = jnp.where(rightward, me, n - 1 - me)
        first_row = jnp.where(place >= slot - 1, width, block * rows)
        for start, size in parts:
            write(rounded, first_row + start, size)
    for start, size in parts:
        write(product, me * rows + start, size)
    make_choices(where_ref, *tables, choices_ref)
    for copy in writes:
        copy.wait()


def partial_blocks(n, scale, parts, order, context_rows, cotangent, tables):
    tokens, width = context_rows.shape
    depth = cotangent.shape[1]
    outs = (len(order) + 1) * len(parts)
    choices, *flat = call(
        functools.partial(partial_kernel, n, scale, parts, order), "partial_blocks",
        [jax.ShapeDtypeStruct((8, depth), jnp.float32)]
        + [half_array(size, depth) for _, size in parts] * len(order)
        + [jax.ShapeDtypeStruct((size, depth), jnp.float32) for _, size in parts],
        [VMEM] * 2 + [SMEM] * 5, [VMEM] + [HBM] * outs, limit=14,
        scratch=[
            pltpu.VMEM((width, depth), jnp.float32),
            pltpu.VMEM((width + width // n, depth), jnp.bfloat16),
            pltpu.SemaphoreType.DMA((outs,)),
        ],
    )(context_rows, cotangent, *tables)
    return choices, [flat[k * len(parts):(k + 1) * len(parts)] for k in range(len(order) + 1)]


def send_kernel(arrived_ref, term_ref, arrived_too_ref, term_too_ref, after_ref, out_ref, out_too_ref):
    def body(at):
        total = arrived_ref[at, :].astype(jnp.float32) + term_ref[at, :].astype(jnp.float32)
        out_ref[at, :] = total.astype(out_ref.dtype)
        total = arrived_too_ref[at, :].astype(jnp.float32) + term_too_ref[at, :].astype(jnp.float32)
        out_too_ref[at, :] = total.astype(out_too_ref.dtype)

    by_rows(out_ref, body)


def to_send(pairs, after):
    like = half_array(*pairs[0][0].shape)
    return call(send_kernel, "to_send", [like] * 2, [VMEM] * 4 + [ANY], [VMEM] * 2, flops=SUM_FLOPS)(
        *pairs[0], *pairs[1], after
    )


def grad_kernel(cuts, own_ref, one_ref, other_ref, after_ref, *refs):
    def body(at):
        arrived = one_ref[at, :].astype(jnp.float32) + other_ref[at, :].astype(jnp.float32)
        return (own_ref[at, :] + arrived).astype(jnp.bfloat16)

    first = 0
    carried = refs[0] if len(refs) > len(cuts) else None
    for out_ref, size in zip(refs[len(refs) - len(cuts):], cuts):
        top = 0
        if carried is not None:
            top = carried.shape[0]
            out_ref[0:top, :] = carried[...]

        @pl.loop(0, (size - top) // 16)
        def _(i):
            out_ref[pl.ds(pl.multiple_of(top + i * 16, 16), 16), :] = body(
                pl.ds(pl.multiple_of(first + i * 16, 16), 16)
            )

        first, carried = first + size - top, None


def summed_grad(own, one, other, after, cuts, carried=()):
    depth = one.shape[1]
    return call(
        functools.partial(grad_kernel, cuts), "summed_grad", [half_array(size, depth) for size in cuts],
        [VMEM] * 3 + [ANY] + [VMEM] * len(carried), [VMEM] * len(cuts),
    )(own, one, other, after, *carried)


def columns_kernel(n, scale, parts, where_ref, cotangent_ref, after_ref, *refs):
    blocks, (out_ref, token_ref, full, result, out_sems) = refs[:-5], refs[-5:]
    token_ref[...] = jnp.zeros_like(token_ref)
    width = full.shape[0]
    rows = width // n
    me = where_ref[0]
    even = lax.rem(me, 2) == 0
    for k in range(2 * n - 1):
        slot, swap = (k + 1) // 2, (k + 1) % 2
        shard = me + (jnp.where(even, slot, -slot) if swap == 0 else jnp.where(even, -slot, slot))

        @pl.when(jnp.logical_and(shard >= 0, shard < n))
        def _():
            for c, (start, size) in enumerate(parts):
                first_row = pl.multiple_of(shard * rows + start, 16)
                full[pl.ds(first_row, size), :] = blocks[k * len(parts) + c][...]
    tile = min(256, width)
    writes = []
    for i, start in enumerate(range(0, width, tile)):
        result[:, start:start + tile] = (scale * lax.dot_general(
            cotangent_ref[...], full[start:start + tile, :],
            (((1,), (1,)), ((), ())), preferred_element_type=jnp.float32,
        )).astype(out_ref.dtype)
        at = pl.ds(start, tile)
        writes.append(pltpu.make_async_copy(result.at[:, at], out_ref.at[:, at], out_sems.at[i]))
        writes[-1].start()
    for write in writes:
        write.wait()


def columns(n, scale, parts, where, cotangent, after, blocks):
    tokens, depth = cotangent.shape
    width = n * sum(size for _, size in parts)
    return call(
        functools.partial(columns_kernel, n, scale, parts), "context_grad",
        [half_array(tokens, width), jax.ShapeDtypeStruct((8, 128), jnp.float32)],
        [SMEM, VMEM, ANY] + [VMEM] * len(blocks), [HBM, VMEM], limit=14,
        scratch=[
            pltpu.VMEM((width, depth), cotangent.dtype),
            pltpu.VMEM((tokens, width), cotangent.dtype),
            pltpu.SemaphoreType.DMA((width // min(256, width),)),
        ],
    )(where, cotangent, after, *blocks)


def state_kernel(parts, where_ref, donor_ref, after_ref, *refs):
    own, (mate_ref, across_ref), refs = refs[:3], refs[3:5], refs[5:]
    outs, (taken, sems) = refs[:-2], refs[-2:]
    rows = own[0].shape[0]
    member = where_ref[1]
    way = jnp.bitwise_xor(source_of(member, donor_ref), member)

    @pl.when(way == 0)
    def _():
        copies = []
        for c, (start, size) in enumerate(parts):
            for k in range(3):
                copies.append(pltpu.make_async_copy(
                    own[k].at[pl.ds(start, size), :], outs[c].at[pl.ds(k * size, size), :], sems.at[c * 3 + k]
                ))
                copies[-1].start()
        for copy in copies:
            copy.wait()

    def widen(ref):
        copies = []
        for k in range(3):
            at = pl.ds(k * rows, rows)
            copies.append(pltpu.make_async_copy(ref.at[at, :], taken.at[at, :], sems.at[k]))
            copies[-1].start()
        for k in range(3):
            copies[k].wait()
            for c, (start, size) in enumerate(parts):
                first_row = k * rows + start
                outs[c][k * size:(k + 1) * size, :] = taken[first_row:first_row + size, :].astype(jnp.float32)

    pl.when(way == 1)(lambda: widen(mate_ref))
    pl.when(way > 1)(lambda: widen(across_ref))


def taken_state(parts, where, donor, own, donated, after):
    rows, depth = own[0].shape
    return call(
        functools.partial(state_kernel, parts), "taken_state",
        [jax.ShapeDtypeStruct((3 * size, depth), jnp.float32) for _, size in parts],
        [SMEM, SMEM, ANY] + [HBM] * 3 + [ANY] * 2, [VMEM] * len(parts),
        scratch=[pltpu.VMEM((3 * rows, depth), jnp.bfloat16), pltpu.SemaphoreType.DMA((3 * len(parts),))],
    )(where, donor, after, *own, *donated)


def adam_kernel(start, size, hops, filled, choices_ref, state_ref, own_ref, mate_ref, across_ref, after_ref, *refs):
    far_refs, refs = refs[:hops], refs[hops + (3 if filled else 0):]
    outs, (token_ref, stepped, sems) = refs[:3], refs[3:]
    token_ref[...] = jnp.zeros_like(token_ref)
    depth = own_ref.shape[1]
    writes = []
    piece, hop = 32, size // hops
    for top in range(0, size, piece):
        height = min(piece, size - top)

        def body(i):
            at = pl.ds(pl.multiple_of(top + i * 16, 16), 16)
            row = lambda k: jnp.broadcast_to(choices_ref[k:k + 1, :], (16, depth))
            load = lambda k: state_ref[pl.ds(pl.multiple_of(k * size + top + i * 16, 16), 16), :]
            near = pl.ds(pl.multiple_of(top % hop + i * 16, 16), 16)
            g = far_refs[top // hop][near, :].astype(jnp.float32)
            for k, ref in ((1, own_ref), (2, mate_ref), (3, across_ref)):
                g = jnp.where(row(k) > 0, ref[at, :].astype(jnp.float32), g)
            w = load(0)
            first_step = beta_one * load(1) + (1.0 - beta_one) * g
            second_step = beta_two * load(2) + (1.0 - beta_two) * g * g
            ratio = (first_step * row(6)) / (jnp.sqrt(second_step * row(7)) + epsilon)
            stepped[0, at, :] = w - row(4) * (ratio + row(5) * w)
            stepped[1, at, :] = first_step
            stepped[2, at, :] = second_step

        pl.loop(0, height // 16)(body)
        for k in range(3):
            writes.append(pltpu.make_async_copy(
                stepped.at[k, pl.ds(top, height), :],
                outs[k].at[pl.ds(start + top, height), :], sems.at[len(writes)],
            ))
            writes[-1].start()
    for write in writes:
        write.wait()


def adam_update(start, size, rows, choices, state, grads, far, after, filled):
    depth = state.shape[1]
    return call(
        functools.partial(adam_kernel, start, size, len(far), bool(filled)), "adam",
        [jax.ShapeDtypeStruct((rows, depth), jnp.float32)] * 3 + [jax.ShapeDtypeStruct((8, 128), jnp.float32)],
        [VMEM] * 5 + [ANY] + [VMEM] * len(far) + [HBM] * len(filled), [HBM] * 3 + [VMEM],
        scratch=[pltpu.VMEM((3, size, depth), jnp.float32), pltpu.SemaphoreType.DMA((3 * (-(-size // 32)),))],
        aliases={6 + len(far) + k: k for k in range(len(filled))},
    )(choices, state, *grads, after, *far, *filled)


def on_device(n, members, context, out_grad, weight, first, second, rates, decays, steps, donor):
    context_rows = context[0]
    cotangent = out_grad[0]
    scale = context_rows.shape[1] ** (-0.5)
    rows, depth = weight.shape[1:]
    chains = 2 if rows % 32 == 0 else 1
    parts = [(c * rows // chains, rows // chains) for c in range(chains)]
    lower = rows // 2 // 16 * 16
    steps_of = [(0, lower), (lower, rows - lower)] if chains == 2 and lower else [(0, rows)]
    where = jnp.stack([lax.axis_index("shard"), lax.axis_index("member")]).astype(jnp.int32)

    swap_across = [(m, m ^ 2) for m in range(members)]
    swap_mates = [(m, m ^ 1) for m in range(members)]
    swaps = []
    for swap in range(2):
        pairs = [(s, s + 1) for s in range(swap, n - 1, 2)]
        swaps.append(pairs + [(b, a) for a, b in pairs])

    arrays = (weight[0], first[0], second[0])
    state, *own = halves(parts, arrays)
    order = [(slot, swap) for slot in range(2, n + 1) for swap in range(2)]
    tables = (where, rates, decays, steps, donor)
    choices, terms = partial_blocks(n, scale, parts, order, context_rows, cotangent, tables)

    arrived = [[own, own]]
    sent = own[0]
    for slot in range(1, n + 1):
        now = [[], []]
        for c in range(len(parts)):
            blocks = [arrived[-1][1][c], arrived[-1][0][c]]
            if slot > 1:
                blocks = to_send([(blocks[swap], terms[2 * (slot - 2) + swap][c]) for swap in range(2)], sent)
                sent = blocks[0]
            for swap in range(2):
                now[swap].append(lax.ppermute(blocks[swap], "shard", swaps[swap]))
        arrived.append(now)

    mate = lax.ppermute(state, "member", swap_mates)
    across = lax.ppermute(pick(choices, state, mate, terms[0][0]), "member", swap_across)
    states = taken_state(steps_of, where, donor, arrays, (mate, across), sent)

    grads, carried = [], ()
    for c, (_, size) in enumerate(parts):
        last = c == len(parts) - 1
        cuts = [steps_of[c][1]] if last else [steps_of[c][1], size - steps_of[c][1]]
        cuts = [cut for cut in cuts if cut]
        sums = summed_grad(terms[-1][c], arrived[n][0][c], arrived[n][1][c], sent, cuts, carried)
        grads.append(sums[0])
        sent, carried = sums[0], tuple(sums[1:])
    blocks = list(own)
    for slot in range(1, n):
        blocks += arrived[slot][0] + arrived[slot][1]
    context_grad, computed = columns(n, scale, parts, where, cotangent, sent, blocks)

    updated = ()
    for c, (start, size) in enumerate(steps_of):
        mate = lax.ppermute(grads[c], "member", swap_mates)
        across = lax.ppermute(grads[c], "member", swap_across)
        pieces = gate(across, computed, 2 if c == 0 and size % 64 == 0 else 1)
        far = [lax.ppermute(piece, "member", swap_mates) for piece in pieces]
        *updated, computed = adam_update(
            start, size, rows, choices, states[c], (grads[c], mate, across), far, computed, updated
        )
    return (context_grad[None],) + tuple(array[None] for array in updated)


def solution(mesh):
    whole = P(("groups", "member"), "shard", None)
    n, members = mesh.shape["shard"], mesh.shape["member"]
    return jax.shard_map(
        functools.partial(on_device, n, members),
        mesh=mesh,
        in_specs=(whole,) * 5 + (P("groups"),) * 4,
        out_specs=(whole,) * 4,
        check_vma=False,
    )
```

```python
import functools
import math

import jax
import jax.numpy as jnp
from jax import lax
from jax.experimental import pallas as pl
from jax.experimental.pallas import tpu as pltpu
from jax.sharding import PartitionSpec as P

beta_one = 0.9
beta_two = 0.999
epsilon = 1e-08

MIB = 1 << 20
SUM_FLOPS = 5 * 2 ** 28
SMEM = pl.BlockSpec(memory_space=pltpu.SMEM)
VMEM = pl.BlockSpec(memory_space=pltpu.VMEM)
HBM = pl.BlockSpec(memory_space=pltpu.HBM)
ANY = pl.BlockSpec(memory_space=pl.ANY)


def call(kernel, name, out_shape, in_specs, out_specs, limit=8, scratch=(), aliases=None, flops=0):
    return pl.pallas_call(
        kernel,
        out_shape=out_shape,
        in_specs=in_specs,
        out_specs=out_specs,
        scratch_shapes=scratch,
        input_output_aliases=aliases or {},
        compiler_params=pltpu.CompilerParams(vmem_limit_bytes=limit * MIB),
        cost_estimate=pl.CostEstimate(flops=flops, bytes_accessed=1024, transcendentals=0),
        name=name,
    )


def half_array(rows, depth):
    return jax.ShapeDtypeStruct((rows, depth), jnp.bfloat16)


def gate_kernel(value_ref, after_ref, *out_refs):
    size = out_refs[0].shape[0]
    for k, out_ref in enumerate(out_refs):
        out_ref[...] = value_ref[k * size:(k + 1) * size, :]


def gate(value, after, count):
    rows, depth = value.shape
    return call(gate_kernel, "gate", [half_array(rows // count, depth)] * count, [VMEM, ANY], [VMEM] * count)(
        value, after
    )


def by_rows(ref, body, step=16):
    @pl.loop(0, ref.shape[0] // step)
    def _(i):
        body(pl.ds(pl.multiple_of(i * step, step), step))


def source_of(member, donor_ref):
    donor = donor_ref[member]
    return jnp.where(donor >= 0, donor, member)


def make_choices(where_ref, rates_ref, decays_ref, steps_ref, donor_ref, out_ref):
    member = where_ref[1]
    source = source_of(member, donor_ref)
    way = jnp.bitwise_xor(source, member)
    partner_source = source_of(jnp.bitwise_xor(member, 2), donor_ref)
    flags = [partner_source == jnp.bitwise_xor(member, 1), way == 0, way == 1, way == 2]
    depth = out_ref.shape[1]
    for k, flag in enumerate(flags):
        out_ref[k:k + 1, :] = jnp.full((1, depth), jnp.where(flag, 1.0, 0.0))
    out_ref[4:5, :] = jnp.full((1, depth), rates_ref[source])
    out_ref[5:6, :] = jnp.full((1, depth), decays_ref[source])
    count = jnp.full((1, depth), (steps_ref[source] + 1).astype(jnp.float32))
    out_ref[6:7, :] = 1.0 / (1.0 - jnp.exp(count * math.log(beta_one)))
    out_ref[7:8, :] = 1.0 / (1.0 - jnp.exp(count * math.log(beta_two)))


def halves_kernel(parts, weight_ref, first_ref, second_ref, *refs):
    state_ref, own_refs, (full, sems) = refs[0], refs[1:-2], refs[-2:]
    rows = weight_ref.shape[0]
    copies = []
    for k, ref in enumerate((weight_ref, first_ref, second_ref)):
        for c, (start, size) in enumerate(parts):
            copies.append(pltpu.make_async_copy(
                ref.at[pl.ds(start, size), :], full.at[k, pl.ds(start, size), :], sems.at[k * len(parts) + c]
            ))
            copies[-1].start()
    for k in range(3):
        for c, (start, size) in enumerate(parts):
            copies[k * len(parts) + c].wait()
            rounded = full[k, start:start + size, :].astype(jnp.bfloat16)
            if k == 0:
                own_refs[c][...] = rounded
            state_ref[k * rows + start:k * rows + start + size, :] = rounded


def halves(parts, arrays):
    rows, depth = arrays[0].shape
    shapes = [half_array(3 * rows, depth)] + [half_array(size, depth) for _, size in parts]
    return call(
        functools.partial(halves_kernel, parts), "halves",
        shapes, [HBM] * 3, [VMEM] * len(shapes), limit=56,
        scratch=[pltpu.VMEM((3, rows, depth), jnp.float32), pltpu.SemaphoreType.DMA((3 * len(parts),))],
    )(*arrays)


def pick_kernel(choices_ref, own_ref, mate_ref, after_ref, out_ref):
    def body(at):
        wants_mate = jnp.broadcast_to(choices_ref[0:1, :], (16, out_ref.shape[1])) > 0
        own, mate = own_ref[at, :].astype(jnp.float32), mate_ref[at, :].astype(jnp.float32)
        out_ref[at, :] = jnp.where(wants_mate, mate, own).astype(out_ref.dtype)

    by_rows(out_ref, body)


def pick(choices, own, mate, after):
    return call(pick_kernel, "pick", half_array(*own.shape), [VMEM, VMEM, VMEM, ANY], VMEM)(
        choices, own, mate, after
    )


def partial_kernel(n, scale, parts, order, context_ref, cotangent_ref, where_ref, *refs):
    tables, choices_ref, outs, (product, rounded, out_sems) = refs[:4], refs[4], refs[5:-3], refs[-3:]
    width = product.shape[0]
    rows = width // n
    me = where_ref[0]
    even = lax.rem(me, 2) == 0
    tile = min(256, width)
    rounded[width:, :] = jnp.zeros((rows, rounded.shape[1]), rounded.dtype)
    for start in range(0, width, tile):
        block = scale * lax.dot_general(
            context_ref[:, start:start + tile], cotangent_ref[...],
            (((0,), (0,)), ((), ())), preferred_element_type=jnp.float32,
        )
        product[start:start + tile, :] = block
        rounded[start:start + tile, :] = block.astype(rounded.dtype)
    writes = []

    def write(source, first_row, size):
        at = len(writes)
        writes.append(pltpu.make_async_copy(
            source.at[pl.ds(pl.multiple_of(first_row, 16), size), :], outs[at], out_sems.at[at]
        ))
        writes[-1].start()

    for slot, swap in order:
        rightward = even if swap == 0 else jnp.logical_not(even)
        block = lax.rem(me + jnp.where(rightward, n + 1 - slot, slot - 1), n)
        place = jnp.where(rightward, me, n - 1 - me)
        first_row = jnp.where(place >= slot - 1, width, block * rows)
        for start, size in parts:
            write(rounded, first_row + start, size)
    for start, size in parts:
        write(product, me * rows + start, size)
    make_choices(where_ref, *tables, choices_ref)
    for copy in writes:
        copy.wait()


def partial_blocks(n, scale, parts, order, context_rows, cotangent, tables):
    tokens, width = context_rows.shape
    depth = cotangent.shape[1]
    outs = (len(order) + 1) * len(parts)
    choices, *flat = call(
        functools.partial(partial_kernel, n, scale, parts, order), "partial_blocks",
        [jax.ShapeDtypeStruct((8, depth), jnp.float32)]
        + [half_array(size, depth) for _, size in parts] * len(order)
        + [jax.ShapeDtypeStruct((size, depth), jnp.float32) for _, size in parts],
        [VMEM] * 2 + [SMEM] * 5, [VMEM] + [HBM] * outs, limit=14,
        scratch=[
            pltpu.VMEM((width, depth), jnp.float32),
            pltpu.VMEM((width + width // n, depth), jnp.bfloat16),
            pltpu.SemaphoreType.DMA((outs,)),
        ],
    )(context_rows, cotangent, *tables)
    return choices, [flat[k * len(parts):(k + 1) * len(parts)] for k in range(len(order) + 1)]


def send_kernel(arrived_ref, term_ref, arrived_too_ref, term_too_ref, after_ref, out_ref, out_too_ref):
    def body(at):
        total = arrived_ref[at, :].astype(jnp.float32) + term_ref[at, :].astype(jnp.float32)
        out_ref[at, :] = total.astype(out_ref.dtype)
        total = arrived_too_ref[at, :].astype(jnp.float32) + term_too_ref[at, :].astype(jnp.float32)
        out_too_ref[at, :] = total.astype(out_too_ref.dtype)

    by_rows(out_ref, body)


def to_send(pairs, after):
    like = half_array(*pairs[0][0].shape)
    return call(send_kernel, "to_send", [like] * 2, [VMEM] * 4 + [ANY], [VMEM] * 2, flops=SUM_FLOPS)(
        *pairs[0], *pairs[1], after
    )


def grad_kernel(cuts, own_ref, one_ref, other_ref, after_ref, *refs):
    def body(at):
        arrived = one_ref[at, :].astype(jnp.float32) + other_ref[at, :].astype(jnp.float32)
        return (own_ref[at, :] + arrived).astype(jnp.bfloat16)

    first = 0
    carried = refs[0] if len(refs) > len(cuts) else None
    for out_ref, size in zip(refs[len(refs) - len(cuts):], cuts):
        top = 0
        if carried is not None:
            top = carried.shape[0]
            out_ref[0:top, :] = carried[...]

        @pl.loop(0, (size - top) // 16)
        def _(i):
            out_ref[pl.ds(pl.multiple_of(top + i * 16, 16), 16), :] = body(
                pl.ds(pl.multiple_of(first + i * 16, 16), 16)
            )

        first, carried = first + size - top, None


def summed_grad(own, one, other, after, cuts, carried=()):
    depth = one.shape[1]
    return call(
        functools.partial(grad_kernel, cuts), "summed_grad", [half_array(size, depth) for size in cuts],
        [VMEM] * 3 + [ANY] + [VMEM] * len(carried), [VMEM] * len(cuts),
    )(own, one, other, after, *carried)


def columns_kernel(n, scale, parts, where_ref, cotangent_ref, after_ref, *refs):
    blocks, (out_ref, token_ref, full, result, out_sems) = refs[:-5], refs[-5:]
    token_ref[...] = jnp.zeros_like(token_ref)
    width = full.shape[0]
    rows = width // n
    me = where_ref[0]
    even = lax.rem(me, 2) == 0
    for k in range(2 * n - 1):
        slot, swap = (k + 1) // 2, (k + 1) % 2
        shard = me + (jnp.where(even, slot, -slot) if swap == 0 else jnp.where(even, -slot, slot))

        @pl.when(jnp.logical_and(shard >= 0, shard < n))
        def _():
            for c, (start, size) in enumerate(parts):
                first_row = pl.multiple_of(shard * rows + start, 16)
                full[pl.ds(first_row, size), :] = blocks[k * len(parts) + c][...]
    tile = min(256, width)
    writes = []
    for i, start in enumerate(range(0, width, tile)):
        result[:, start:start + tile] = (scale * lax.dot_general(
            cotangent_ref[...], full[start:start + tile, :],
            (((1,), (1,)), ((), ())), preferred_element_type=jnp.float32,
        )).astype(out_ref.dtype)
        at = pl.ds(start, tile)
        writes.append(pltpu.make_async_copy(result.at[:, at], out_ref.at[:, at], out_sems.at[i]))
        writes[-1].start()
    for write in writes:
        write.wait()


def columns(n, scale, parts, where, cotangent, after, blocks):
    tokens, depth = cotangent.shape
    width = n * sum(size for _, size in parts)
    return call(
        functools.partial(columns_kernel, n, scale, parts), "context_grad",
        [half_array(tokens, width), jax.ShapeDtypeStruct((8, 128), jnp.float32)],
        [SMEM, VMEM, ANY] + [VMEM] * len(blocks), [HBM, VMEM], limit=14,
        scratch=[
            pltpu.VMEM((width, depth), cotangent.dtype),
            pltpu.VMEM((tokens, width), cotangent.dtype),
            pltpu.SemaphoreType.DMA((width // min(256, width),)),
        ],
    )(where, cotangent, after, *blocks)


def state_kernel(parts, where_ref, donor_ref, after_ref, *refs):
    own, (mate_ref, across_ref), refs = refs[:3], refs[3:5], refs[5:]
    outs, (taken, sems) = refs[:-2], refs[-2:]
    rows = own[0].shape[0]
    member = where_ref[1]
    way = jnp.bitwise_xor(source_of(member, donor_ref), member)

    @pl.when(way == 0)
    def _():
        copies = []
        for c, (start, size) in enumerate(parts):
            for k in range(3):
                copies.append(pltpu.make_async_copy(
                    own[k].at[pl.ds(start, size), :], outs[c].at[pl.ds(k * size, size), :], sems.at[c * 3 + k]
                ))
                copies[-1].start()
        for copy in copies:
            copy.wait()

    def widen(ref):
        copies = []
        for k in range(3):
            at = pl.ds(k * rows, rows)
            copies.append(pltpu.make_async_copy(ref.at[at, :], taken.at[at, :], sems.at[k]))
            copies[-1].start()
        for k in range(3):
            copies[k].wait()
            for c, (start, size) in enumerate(parts):
                first_row = k * rows + start
                outs[c][k * size:(k + 1) * size, :] = taken[first_row:first_row + size, :].astype(jnp.float32)

    pl.when(way == 1)(lambda: widen(mate_ref))
    pl.when(way > 1)(lambda: widen(across_ref))


def taken_state(parts, where, donor, own, donated, after):
    rows, depth = own[0].shape
    return call(
        functools.partial(state_kernel, parts), "taken_state",
        [jax.ShapeDtypeStruct((3 * size, depth), jnp.float32) for _, size in parts],
        [SMEM, SMEM, ANY] + [HBM] * 3 + [ANY] * 2, [VMEM] * len(parts),
        scratch=[pltpu.VMEM((3 * rows, depth), jnp.bfloat16), pltpu.SemaphoreType.DMA((3 * len(parts),))],
    )(where, donor, after, *own, *donated)


def adam_kernel(start, size, hops, filled, choices_ref, state_ref, own_ref, mate_ref, across_ref, after_ref, *refs):
    far_refs, refs = refs[:hops], refs[hops + (3 if filled else 0):]
    outs, tokens, (stepped, sems) = refs[:3], refs[3:-2], refs[-2:]
    for token_ref in tokens:
        token_ref[...] = jnp.zeros_like(token_ref)
    depth = own_ref.shape[1]
    writes = []
    piece, hop = 32, size // hops
    for top in range(0, size, piece):
        height = min(piece, size - top)

        def body(i):
            at = pl.ds(pl.multiple_of(top + i * 16, 16), 16)
            row = lambda k: jnp.broadcast_to(choices_ref[k:k + 1, :], (16, depth))
            load = lambda k: state_ref[pl.ds(pl.multiple_of(k * size + top + i * 16, 16), 16), :]
            near = pl.ds(pl.multiple_of(top % hop + i * 16, 16), 16)
            g = far_refs[top // hop][near, :].astype(jnp.float32)
            for k, ref in ((1, own_ref), (2, mate_ref), (3, across_ref)):
                g = jnp.where(row(k) > 0, ref[at, :].astype(jnp.float32), g)
            w = load(0)
            first_step = beta_one * load(1) + (1.0 - beta_one) * g
            second_step = beta_two * load(2) + (1.0 - beta_two) * g * g
            ratio = (first_step * row(6)) / (jnp.sqrt(second_step * row(7)) + epsilon)
            stepped[0, at, :] = w - row(4) * (ratio + row(5) * w)
            stepped[1, at, :] = first_step
            stepped[2, at, :] = second_step

        pl.loop(0, height // 16)(body)
        for k in range(3):
            writes.append(pltpu.make_async_copy(
                stepped.at[k, pl.ds(top, height), :],
                outs[k].at[pl.ds(start + top, height), :], sems.at[len(writes)],
            ))
            writes[-1].start()
    for write in writes:
        write.wait()


def adam_update(start, size, rows, choices, state, grads, far, after, filled, tokens):
    depth = state.shape[1]
    return call(
        functools.partial(adam_kernel, start, size, len(far), bool(filled)), "adam",
        [jax.ShapeDtypeStruct((rows, depth), jnp.float32)] * 3
        + [jax.ShapeDtypeStruct((8, 128), jnp.float32)] * tokens,
        [VMEM] * 5 + [ANY] + [VMEM] * len(far) + [HBM] * len(filled), [HBM] * 3 + [VMEM] * tokens,
        scratch=[pltpu.VMEM((3, size, depth), jnp.float32), pltpu.SemaphoreType.DMA((3 * (-(-size // 32)),))],
        aliases={6 + len(far) + k: k for k in range(len(filled))},
    )(choices, state, *grads, after, *far, *filled)


def on_device(n, members, context, out_grad, weight, first, second, rates, decays, steps, donor):
    context_rows = context[0]
    cotangent = out_grad[0]
    scale = context_rows.shape[1] ** (-0.5)
    rows, depth = weight.shape[1:]
    chains = 2 if rows % 32 == 0 else 1
    parts = [(c * rows // chains, rows // chains) for c in range(chains)]
    lower = rows // 2 // 16 * 16
    steps_of = [(0, lower), (lower, rows - lower)] if chains == 2 and lower else [(0, rows)]
    where = jnp.stack([lax.axis_index("shard"), lax.axis_index("member")]).astype(jnp.int32)

    swap_across = [(m, m ^ 2) for m in range(members)]
    swap_mates = [(m, m ^ 1) for m in range(members)]
    swaps = []
    for swap in range(2):
        pairs = [(s, s + 1) for s in range(swap, n - 1, 2)]
        swaps.append(pairs + [(b, a) for a, b in pairs])

    arrays = (weight[0], first[0], second[0])
    state, *own = halves(parts, arrays)
    order = [(slot, swap) for slot in range(2, n + 1) for swap in range(2)]
    tables = (where, rates, decays, steps, donor)
    choices, terms = partial_blocks(n, scale, parts, order, context_rows, cotangent, tables)

    arrived = [[own, own]]
    sent = own[0]
    for slot in range(1, n + 1):
        now = [[], []]
        for c in range(len(parts)):
            blocks = [arrived[-1][1][c], arrived[-1][0][c]]
            if slot > 1:
                blocks = to_send([(blocks[swap], terms[2 * (slot - 2) + swap][c]) for swap in range(2)], sent)
                sent = blocks[0]
            for swap in range(2):
                now[swap].append(lax.ppermute(blocks[swap], "shard", swaps[swap]))
        arrived.append(now)

    mate = lax.ppermute(state, "member", swap_mates)
    across = lax.ppermute(pick(choices, state, mate, terms[0][0]), "member", swap_across)
    states = taken_state(steps_of, where, donor, arrays, (mate, across), sent)

    grads, carried = [], ()
    for c, (_, size) in enumerate(parts):
        last = c == len(parts) - 1
        cuts = [steps_of[c][1]] if last else [steps_of[c][1], size - steps_of[c][1]]
        cuts = [cut for cut in cuts if cut]
        sums = summed_grad(terms[-1][c], arrived[n][0][c], arrived[n][1][c], sent, cuts, carried)
        grads.append(sums[0])
        sent, carried = sums[0], tuple(sums[1:])
    blocks = list(own)
    for slot in range(1, n):
        blocks += arrived[slot][0] + arrived[slot][1]
    context_grad, computed = columns(n, scale, parts, where, cotangent, sent, blocks)

    updated = ()
    for c, (start, size) in enumerate(steps_of):
        mate = lax.ppermute(grads[c], "member", swap_mates)
        across = lax.ppermute(grads[c], "member", swap_across)
        pieces = gate(across, computed, 2 if c == 0 and size % 64 == 0 else 1)
        far = [lax.ppermute(piece, "member", swap_mates) for piece in pieces]
        last = c == len(steps_of) - 1
        stepped = adam_update(
            start, size, rows, choices, states[c], (grads[c], mate, across), far, computed, updated, int(not last)
        )
        updated, computed = stepped[:3], stepped[-1]
    return (context_grad[None],) + tuple(array[None] for array in updated)


def solution(mesh):
    whole = P(("groups", "member"), "shard", None)
    n, members = mesh.shape["shard"], mesh.shape["member"]
    return jax.shard_map(
        functools.partial(on_device, n, members),
        mesh=mesh,
        in_specs=(whole,) * 5 + (P("groups"),) * 4,
        out_specs=(whole,) * 4,
        check_vma=False,
    )
```
